32 devices in a mesh: seq: 4 (over y, core), wa: 2 (over x), wb: 4 (over z).
Axes of the slice: x: 2, y: 2, z: 4, core: 2. Of those that a mesh axis runs over, the one named last changes fastest.
Arguments:
- residual: bfloat16 [8, 2048, 768], P(('wa', 'wb'), 'seq'), may hold values from -6 to 6
- cotangent: bfloat16 [8, 2048, 768], P(('wa', 'wb'), 'seq'), may hold values from -6 to 6
- norm_gain: bfloat16 [768], replicated, may hold values from 0.5 to 1.5
- w_zx: bfloat16 [768, 2, 1536], P('wa', None, 'wb'), may hold values from -0.21875 to 0.21875
- w_bc: bfloat16 [768, 2, 128], P('wa'), may hold values from -0.21875 to 0.21875
- w_dt: bfloat16 [768, 24], P('wa', 'wb'), may hold values from -0.21875 to 0.21875
- x_kernel: bfloat16 [4, 1536], P(None, 'wb'), may hold values from -3 to 3
- x_offset: bfloat16 [1536], P('wb'), may hold values from -0.5 to 0.5
- bc_kernel: bfloat16 [4, 2, 128], replicated, may hold values from -3 to 3
- bc_offset: bfloat16 [2, 128], replicated, may hold values from -0.5 to 0.5
- dt_bias: float32 [24], P('wb'), may hold values from -6 to -2
- a_log: float32 [24], P('wb'), may hold values from -2.5 to 2.5
- d_skip: float32 [24], P('wb'), may hold values from 0.5 to 1.5
- gate_gain: bfloat16 [1536], P('wb'), may hold values from 0.5 to 1.5
- w_out: bfloat16 [768, 1536], P('wa', 'wb'), may hold values from -0.15625 to 0.15625
Outputs:
- layer_out: bfloat16 [8, 2048, 768], P(('wa', 'wb'), 'seq')
- input_grad: float32 [8, 2048, 768], P(('wa', 'wb'), 'seq')
- norm_gain_grad: float32 [768], replicated
- w_zx_grad: float32 [768, 2, 1536], P('wa', None, 'wb')
- w_bc_grad: float32 [768, 2, 128], P('wa')
- w_dt_grad: float32 [768, 24], P('wa', 'wb')
- x_kernel_grad: float32 [4, 1536], P(None, 'wb')
- x_offset_grad: float32 [1536], P('wb')
- bc_kernel_grad: float32 [4, 2, 128], replicated
- bc_offset_grad: float32 [2, 128], replicated
- dt_bias_grad: float32 [24], P('wb')
- a_log_grad: float32 [24], P('wb')
- d_skip_grad: float32 [24], P('wb')
- gate_gain_grad: float32 [1536], P('wb')
- w_out_grad: float32 [768, 1536], P('wa', 'wb')
The draws below stay inside these ranges and needn't reach their ends.
All inputs are finite; a program needn't handle non-finite values.
Results may differ from the reference program's by a relative error of at most 0.03.
Values may be sent and summed in bfloat16 or wider, within the bound.
A program may use at most 192 MiB of HBM per device.

```python
import jax
import jax.numpy as jnp
from jax import lax

D = 768
H = 24
P_SIZE = 64
N = 128
E = 1536
CONV = 4
SPAN = 256
SEQS = 8
LENGTH = 2048


def levels(stream_key, shape, cuts, smallest, top_value):
    loudness, own = 1.0, jax.random.fold_in(stream_key, 6)
    for axis_at, parts in cuts:
        heights = jnp.exp(jax.random.uniform(jax.random.fold_in(own, axis_at), (parts,), jnp.float32, smallest / len(cuts), top_value / len(cuts)))
        loudness = loudness * jnp.repeat(heights, shape[axis_at] // parts).reshape([-1 if axis == axis_at else 1 for axis in range(len(shape))])
    return loudness


def centred(stream_key, extent, scale, reach, shards=(), held_as=jnp.bfloat16):
    level = levels(stream_key, extent, shards, -0.22, 0.18) if shards else 1.0
    values = jax.random.normal(stream_key, extent, jnp.float32) * scale * level
    return jnp.minimum(jnp.maximum(values, -reach), reach).astype(held_as)


def setup_inputs(seed: int = 0) -> dict:
    streams_of = jax.random.split(jax.random.key(seed), 16)
    residual = centred(streams_of[0], (SEQS, LENGTH, D), 1.0, 6.0, ((0, 8), (1, 4)))
    cotangent = centred(streams_of[1], (SEQS, LENGTH, D), 1.0, 6.0, ((0, 8), (1, 4)))
    norm_gain = jnp.clip(1.0 + 0.1 * jax.random.normal(streams_of[2], (D,), jnp.float32), 0.5, 1.5).astype(jnp.bfloat16)
    w_zx = centred(streams_of[3], (D, 2, E), D ** -0.5, 0.21875, ((0, 2), (2, 4)))
    w_bc = centred(streams_of[4], (D, 2, N), D ** -0.5, 0.21875, ((0, 2),))
    w_dt = centred(streams_of[5], (D, H), D ** -0.5, 0.21875, ((0, 2), (1, 4)))
    x_kernel = centred(streams_of[6], (CONV, E), CONV ** -0.5, 3.0, ((1, 4),))
    x_offset = jnp.clip(jax.random.uniform(streams_of[7], (E,), jnp.float32, -0.5, 0.5) * levels(streams_of[7], (E,), ((0, 4),), -0.4, 0.0), -0.5, 0.5).astype(jnp.bfloat16)
    bc_kernel = centred(streams_of[8], (CONV, 2, N), CONV ** -0.5, 3.0)
    bc_offset = jnp.clip(jax.random.uniform(streams_of[9], (2, N), jnp.float32, -0.5, 0.5), -0.5, 0.5).astype(jnp.bfloat16)
    dt_bias = jnp.clip(-6.0 + 4.0 * jax.random.uniform(streams_of[10], (H,), jnp.float32) ** levels(streams_of[10], (H,), ((0, 4),), -0.2, 0.2), -6.0, -2.0)
    a_log = jnp.clip(jax.random.uniform(streams_of[11], (H,), jnp.float32, -2.5, 2.5) * levels(streams_of[11], (H,), ((0, 4),), -0.4, 0.0), -2.5, 2.5)
    d_skip = jnp.clip(0.5 + 1.0 * jax.random.uniform(streams_of[12], (H,), jnp.float32) ** levels(streams_of[12], (H,), ((0, 4),), -0.2, 0.2), 0.5, 1.5)
    gate_gain = jnp.clip(1.0 + 0.1 * jax.random.normal(streams_of[13], (E,), jnp.float32), 0.5, 1.5).astype(jnp.bfloat16)
    w_out = centred(streams_of[14], (D, E), E ** -0.5, 0.15625, ((0, 2), (1, 4)))
    return dict(residual=residual, cotangent=cotangent, norm_gain=norm_gain, w_zx=w_zx, w_bc=w_bc, w_dt=w_dt, x_kernel=x_kernel, x_offset=x_offset, bc_kernel=bc_kernel, bc_offset=bc_offset, dt_bias=dt_bias, a_log=a_log, d_skip=d_skip, gate_gain=gate_gain, w_out=w_out)


EPSILON = 1e-05
PRECISION_HIGH = lax.Precision.HIGHEST

@jax.custom_vjp
def low(v):
    return lax.optimization_barrier(v.astype(jnp.bfloat16)).astype(jnp.float32)

@jax.custom_vjp
def lowered_backward(v):
    return v

def low_keep(v):
    return (low(v), None)

def low_pass(kept, grad):
    return (grad,)

def back_keep(v):
    return (v, None)

def back_low(kept, grad):
    return (low(grad),)
low.defvjp(low_keep, low_pass)
lowered_backward.defvjp(back_keep, back_low)

def sigmoid_linear(values):
    return values * jax.nn.sigmoid(values)

def causal_conv(padded, kernel, offset):
    steps_out = padded.shape[1] - kernel.shape[0] + 1
    summation = offset + kernel[0] * padded[:, 0:steps_out]
    for tap_index in range(1, kernel.shape[0]):
        summation = summation + kernel[tap_index] * padded[:, tap_index:tap_index + steps_out]
    return sigmoid_linear(summation)

def span_scan(x_all, b_all, c_all, dt_all, decay_rate, start_state):
    groups = x_all.shape[0]
    blocks = x_all.shape[1] // SPAN

    def to_blocks(values):
        shaped = values.reshape((groups, blocks, SPAN) + values.shape[2:])
        return jnp.moveaxis(shaped, 1, 0)
    position = jnp.arange(SPAN)
    causal = (position[:, None] >= position[None, :])[None, :, :, None]

    def span_step(carry_state, pieces):
        x_blk, b_blk, c_blk, dt_blk = pieces
        log_decay = jnp.cumsum(dt_blk * decay_rate, axis=1)
        decay_gap = log_decay[:, :, None, :] - log_decay[:, None, :, :]
        decay_mat = jnp.where(causal, jnp.exp(jnp.where(causal, decay_gap, 0.0)), 0.0)
        inner_prod = jnp.einsum('gtn,gsn->gts', c_blk, b_blk, precision=PRECISION_HIGH)
        mix_weight = inner_prod[..., None] * decay_mat * dt_blk[:, None, :, :]
        y_blk = jnp.einsum('gtsh,gshp->gthp', mix_weight, x_blk, precision=PRECISION_HIGH)
        carried = jnp.einsum('gtn,ghpn->gthp', c_blk, carry_state, precision=PRECISION_HIGH)
        y_blk = y_blk + carried * jnp.exp(log_decay)[..., None]
        last_decay = log_decay[:, -1, :]
        tail_weight = jnp.exp(last_decay[:, None, :] - log_decay) * dt_blk
        fresh_state = jnp.einsum('gsh,gshp,gsn->ghpn', tail_weight, x_blk, b_blk, precision=PRECISION_HIGH)
        carry_state = carry_state * jnp.exp(last_decay)[:, :, None, None] + fresh_state
        return (carry_state, y_blk)
    final_state, y_blocks = lax.scan(jax.checkpoint(span_step), start_state, (to_blocks(x_all), to_blocks(b_all), to_blocks(c_all), to_blocks(dt_all)))
    y_all = jnp.moveaxis(y_blocks, 0, 1).reshape(x_all.shape)
    return (y_all, final_state)

def layer(x_grp, norm_gain, w_zx, w_bc, w_dt, x_kernel, x_offset, bc_kernel, bc_offset, dt_bias, a_log, d_skip, gate_gain, w_out):
    groups = x_grp.shape[0]
    inv_rms = lax.rsqrt(lax.optimization_barrier(jnp.mean(x_grp * x_grp, axis=-1, keepdims=True)) + EPSILON)
    normalized_rows = low(x_grp * inv_rms * norm_gain)
    input_weights = jnp.concatenate([w_zx.reshape(D, 2 * E), w_bc.reshape(D, 2 * N), w_dt], axis=1)
    projected_rows = lowered_backward(jnp.einsum('xje,eb->xjb', normalized_rows, input_weights, precision=PRECISION_HIGH))
    z_part = projected_rows[..., :E]
    conv_in = projected_rows[..., E:2 * E + 2 * N]
    dt_raw = projected_rows[..., 2 * E + 2 * N:]
    padded = jnp.pad(conv_in, ((0, 0), (CONV - 1, 0), (0, 0)))
    kernel = jnp.concatenate([x_kernel, bc_kernel.reshape(CONV, 2 * N)], axis=1)
    offset = jnp.concatenate([x_offset, bc_offset.reshape(2 * N)])
    activated = causal_conv(padded, kernel, offset)
    input_heads = activated[..., :E].reshape(groups, LENGTH, H, P_SIZE)
    b_mat = activated[..., E:E + N]
    c_mat = activated[..., E + N:]
    dt_val = jax.nn.softplus(dt_raw + dt_bias)
    decay_rate = -jnp.exp(a_log)
    start_state = jnp.zeros((groups, H, P_SIZE, N), jnp.float32)
    y_ssm, final_state = span_scan(input_heads, b_mat, c_mat, dt_val, decay_rate, start_state)
    y_all = y_ssm + d_skip[:, None] * input_heads
    gated = lowered_backward(low(y_all.reshape(groups, LENGTH, E) * sigmoid_linear(z_part)))
    inv_gate = lax.rsqrt(lax.optimization_barrier(jnp.mean(gated * gated, axis=-1, keepdims=True)) + EPSILON)
    hidden = low(gated * inv_gate * gate_gain)
    branch = jnp.einsum('gle,de->gld', hidden, w_out, precision=PRECISION_HIGH)
    return x_grp + branch

def reference(residual, cotangent, norm_gain, w_zx, w_bc, w_dt, x_kernel, x_offset, bc_kernel, bc_offset, dt_bias, a_log, d_skip, gate_gain, w_out):
    weights = tuple((entry.astype(jnp.float32) for entry in (norm_gain, w_zx, w_bc, w_dt, x_kernel, x_offset, bc_kernel, bc_offset, dt_bias, a_log, d_skip, gate_gain, w_out)))
    group_size = 4 if SEQS % 4 == 0 else 2 if SEQS % 2 == 0 else 1
    batches = SEQS // group_size
    inputs = residual.astype(jnp.float32).reshape(batches, group_size, LENGTH, D)
    incoming = cotangent.astype(jnp.float32).reshape(batches, group_size, LENGTH, D)

    def whole(values, *params):
        return lax.map(lambda seq_block: jax.checkpoint(layer)(seq_block, *params), values)
    result, pullback = jax.vjp(whole, inputs, *weights)
    gradients = pullback(incoming)
    layer_out = result.reshape(SEQS, LENGTH, D).astype(jnp.bfloat16)
    input_grad = gradients[0].reshape(SEQS, LENGTH, D)
    return (layer_out, input_grad, gradients[1], gradients[2], gradients[3], gradients[4], gradients[5], gradients[6], gradients[7], gradients[8], gradients[9], gradients[10], gradients[11], gradients[12], gradients[13])
```

```python
import functools
import types

import jax
import jax.numpy as jnp
from jax import lax
from jax.experimental import pallas as pl
from jax.experimental.pallas import tpu as pltpu
from jax.sharding import PartitionSpec as P

F32, BF16 = jnp.float32, jnp.bfloat16
EPSILON = 1e-05
Q = 128
LANES = 128
HALO = 16
SLOTS = 16
TILE = 256
NT = (((1,), (1,)), ((), ()))


def dot(a, b):
    return jnp.dot(a, b, preferred_element_type=F32)


def dot_nt(a, b):
    return lax.dot_general(a, b, NT, preferred_element_type=F32)


def dot_exact(a, b):
    return jnp.dot(a, b, precision=lax.Precision.HIGHEST, preferred_element_type=F32)


def sigmoid(v):
    return 0.5 + 0.5 * jnp.tanh(0.5 * v)


def fold8(v):
    return v.reshape(v.shape[0] // 8, 8, v.shape[1]).sum(axis=0)


def rows_at(i, size=Q, base=0):
    return pl.ds(pl.multiple_of(i * size + base, 16), size)


def cols_at(i, size=LANES):
    return pl.ds(pl.multiple_of(i * size, LANES), size)


def head_spread(R, bands, head_dim):
    inner = R.ex.shape[1]
    per_band = inner // bands
    row = lax.broadcasted_iota(jnp.int32, (LANES, LANES), 0)

    @pl.loop(0, inner // LANES)
    def _(c):
        lane = lax.broadcasted_iota(jnp.int32, (LANES, LANES), 1) + c * LANES
        hit = jnp.zeros((LANES, LANES), jnp.bool_)
        for band in range(bands):
            first = lane - band * per_band
            inside = (first >= 0) & (first < per_band)
            head = lax.shift_right_arithmetic(first, head_dim.bit_length() - 1)
            hit = hit | (inside & (row == band * SLOTS + head))
        R.ex[:, cols_at(c)] = jnp.where(hit, 1.0, 0.0).astype(BF16)


def norm_rows(R):
    gain = R.gain[...]

    def normed(rows):
        inv = lax.rsqrt(jnp.mean(rows * rows, axis=-1, keepdims=True) + EPSILON)
        return (rows * inv * gain).astype(BF16), inv

    @pl.loop(0, R.x.shape[0] // Q)
    def _(i):
        value, inv = normed(R.x[rows_at(i), :].astype(F32))
        R.xn[rows_at(i, base=HALO), :] = value
        R.inv_rms[rows_at(i), :] = inv
        R.xnT[:, cols_at(i)] = value.T
        R.gT[:, cols_at(i)] = R.g[rows_at(i), :].T


def norm_halo(R):
    rows = R.x_halo[...].astype(F32)
    inv = lax.rsqrt(jnp.mean(rows * rows, axis=-1, keepdims=True) + EPSILON)
    R.xn[0:HALO, :] = (rows * inv * R.gain[...]).astype(BF16)


def project_x(R):
    inner = R.wx.shape[1]

    @pl.loop(0, inner // TILE)
    def _(j):
        R.ci[:, cols_at(j, TILE)] = dot(R.xn[...], R.wx[:, cols_at(j, TILE)])

    R.ci[:, inner:] = dot(R.xn[...], R.wbc[...])


def project_z(R):
    @pl.loop(0, R.wz.shape[1] // TILE)
    def _(j):
        R.z[:, cols_at(j, TILE)] = dot(R.xn[HALO:, :], R.wz[:, cols_at(j, TILE)])


def convolve(R, taps):
    length = R.x.shape[0]
    inner = R.wx.shape[1]

    def tile(cols, put):
        for i in range(length // Q):
            pre = R.par[4:5, cols]
            for k in range(taps):
                first = HALO - (taps - 1) + k + i * Q
                pre = pre + R.par[k : k + 1, cols] * R.ci[pl.ds(first, Q), cols]
            sig = sigmoid(pre)
            act = pre * sig
            put(pl.ds(i * Q, Q), act)
            R.slope[pl.ds(i * Q, Q), cols] = (sig + act * (1.0 - sig)).astype(BF16)

    @pl.loop(0, inner // LANES)
    def _(c):
        def put(rows, act):
            R.xh[rows, cols_at(c)] = act.astype(BF16)

        tile(cols_at(c), put)

    def put_b(rows, act):
        R.bm[rows, :] = act.astype(BF16)

    def put_c(rows, act):
        R.cm[rows, :] = act.astype(BF16)

    tile(pl.ds(inner, LANES), put_b)
    tile(pl.ds(inner + LANES, LANES), put_c)


def lower_ones(strict=False):
    row = lax.broadcasted_iota(jnp.int32, (Q, Q), 0)
    col = lax.broadcasted_iota(jnp.int32, (Q, Q), 1)
    return jnp.where(row > col if strict else row >= col, 1.0, 0.0).astype(F32)


def step_sizes(R):
    R.rate[...] = -jnp.exp(R.par[8:9, 0:LANES])
    bias, rate = R.par[7:8, 0:LANES], R.rate[...]
    ones = lower_ones()
    chunks = R.x.shape[0] // Q
    R.ends[...] = jnp.zeros_like(R.ends)
    for i in range(chunks):
        rows = pl.ds(i * Q, Q)
        v = dot_nt(R.xn[pl.ds(HALO + i * Q, Q), :], R.wdt[...]) + bias
        dt = jnp.maximum(v, 0.0) + jnp.log1p(jnp.exp(-jnp.abs(v)))
        R.dt[rows, :] = dt
        R.dt_sig[rows, :] = jax.nn.sigmoid(v)
        logs = dot_exact(ones, dt * rate)
        R.logs[rows, :] = logs
        R.logsT[:, rows] = logs.T
        last = logs[Q - 1 : Q, :]
        R.ends[i : i + 1, :] = last
        R.dtx[rows, :] = dot(dt.astype(BF16), R.ex[...]).astype(BF16)
        R.expx[rows, :] = dot(jnp.exp(logs).astype(BF16), R.ex[...]).astype(BF16)
        R.tailx[rows, :] = dot(jnp.exp(last - logs).astype(BF16), R.ex[...]).astype(BF16)
    decay = jnp.exp(R.ends[...])
    high = decay.astype(BF16)
    low = (decay - high.astype(F32)).astype(BF16)
    R.decx[...] = dot(high, R.ex[...]) + dot(low, R.ex[...])


def local_states(R):
    chunks = R.x.shape[0] // Q

    @pl.loop(0, chunks)
    def _(i):
        rows = rows_at(i)
        weighted = R.xh[rows, :].astype(F32) * R.dtx[rows, :].astype(F32)
        R.xt[rows, :] = weighted.astype(BF16)
        R.sl[i] = dot(
            R.bm[rows, :].T, (weighted * R.tailx[rows, :].astype(F32)).astype(BF16)
        ).astype(BF16)

    total = R.sl[0].astype(F32)
    for i in range(1, chunks):
        total = total * R.decx[i : i + 1, :] + R.sl[i].astype(F32)
    R.piece[...] = total
    decay = R.decx[0:1, :]
    for i in range(1, chunks):
        decay = decay * R.decx[i : i + 1, :]
    R.piece_decay[...] = decay


def lane_half(value, half):
    lane = lax.broadcasted_iota(jnp.int32, value.shape, 1)
    keep = lane < LANES // 2 if half == 0 else lane >= LANES // 2
    return jnp.where(keep, value, jnp.zeros_like(value))


def slot_of(head, per_band):
    return head // per_band * SLOTS + head % per_band


def inside_forward(R, per_band):
    heads = R.wx.shape[1] // (LANES // 2)

    @pl.loop(0, R.x.shape[0] // Q)
    def _(i):
        rows = rows_at(i)
        row = lax.broadcasted_iota(jnp.int32, (Q, Q), 0)
        col = lax.broadcasted_iota(jnp.int32, (Q, Q), 1)
        causal = row >= col
        inner_prod = dot_nt(R.cm[rows, :], R.bm[rows, :])
        logs = R.logs[rows, :]
        for pair in range(heads // 2):
            cols = pl.ds(pair * LANES, LANES)
            xt = R.xt[rows, cols]
            total = None
            for half in range(2):
                slot = slot_of(2 * pair + half, per_band)
                gap = logs[:, slot : slot + 1] - R.logsT[slot : slot + 1, rows]
                decay = jnp.exp(jnp.where(causal, gap, -1e30))
                part = dot((inner_prod * decay).astype(BF16), lane_half(xt, half))
                total = part if total is None else total + part
            R.y[rows, cols] = total


def carried_forward(R):
    chunks = R.x.shape[0] // Q
    R.state[...] = R.from_before[...].astype(F32)

    @pl.loop(0, chunks)
    def _(i):
        rows = rows_at(i)
        state = R.state[...]
        R.s_in[i] = state.astype(BF16)
        carried = dot(R.cm[rows, :], R.s_in[i]) * R.expx[rows, :].astype(F32)
        R.yi[rows, :] = carried.astype(BF16)
        R.y[rows, :] += carried
        R.state[...] = state * R.decx[pl.ds(i, 1), :] + R.sl[i].astype(F32)


def hidden_grad(R):
    @pl.loop(0, R.x.shape[0] // Q)
    def _(i):
        R.dh[rows_at(i), :] = dot(R.g[rows_at(i), :], R.wo[...]).astype(BF16)


def gate(R):
    inner = R.wx.shape[1]
    R.gain_acc[...] = jnp.zeros_like(R.gain_acc)
    R.skip_acc[...] = jnp.zeros_like(R.skip_acc)

    @pl.loop(0, R.x.shape[0] // Q)
    def _(i):
        rows = rows_at(i)

        def first(c, sums):
            cols = cols_at(c)
            y = R.y[rows, cols] + R.par[6:7, cols] * R.xh[rows, cols].astype(F32)
            R.y[rows, cols] = y
            z = R.z[rows, cols]
            gated = (y * (z * sigmoid(z))).astype(BF16)
            R.gated[rows, cols] = gated
            gated = gated.astype(F32)
            return (
                sums[0] + gated * gated,
                sums[1] + gated * (R.dh[rows, cols].astype(F32) * R.par[5:6, cols]),
            )

        zero = jnp.zeros((Q, LANES), F32)
        squares, cross = lax.fori_loop(0, inner // LANES, first, (zero, zero))
        inv = lax.rsqrt(jnp.sum(squares, axis=-1, keepdims=True) / inner + EPSILON)
        cross = jnp.sum(cross, axis=-1, keepdims=True) * (inv * inv * inv / inner)
        inv = jnp.broadcast_to(inv, (Q, LANES))
        cross = jnp.broadcast_to(cross, (Q, LANES))

        @pl.loop(0, inner // LANES)
        def _(c):
            cols = cols_at(c)
            gated = R.gated[rows, cols].astype(F32)
            dh = R.dh[rows, cols].astype(F32)
            gain = R.par[5:6, cols]
            scaled = gated * inv
            R.hidden[rows, cols] = (scaled * gain).astype(BF16)
            R.gain_acc[:, cols] += fold8(dh * scaled)
            d_gated = dh * gain * inv - gated * cross
            z = R.z[rows, cols]
            sig = sigmoid(z)
            lin = z * sig
            dy = d_gated * lin
            R.dz[rows, cols] = (d_gated * R.y[rows, cols] * (sig + lin * (1.0 - sig))).astype(BF16)
            R.dy[rows, cols] = dy.astype(BF16)
            R.dyl[rows, cols] = (dy * R.expx[rows, cols].astype(F32)).astype(BF16)
            R.skip_acc[:, cols] += fold8(dy * R.xh[rows, cols].astype(F32))


def branch_out(R):
    @pl.loop(0, R.x.shape[0] // Q)
    def _(i):
        rows = rows_at(i)
        R.layer_out[rows, :] = (
            R.x[rows, :].astype(F32) + dot_nt(R.hidden[rows, :], R.wo[...])
        ).astype(BF16)


def grad_tiles(left, right, out):
    @pl.loop(0, right.shape[1] // TILE)
    def _(j):
        cols = cols_at(j, TILE)
        out[:, cols] = dot(left[...], right[:, cols]).astype(out.dtype)


def local_adjoints(R):
    chunks = R.x.shape[0] // Q

    @pl.loop(0, chunks)
    def _(i):
        rows = rows_at(i)
        R.dl[i] = dot(R.cm[rows, :].T, R.dyl[rows, :]).astype(BF16)

    total = R.dl[chunks - 1].astype(F32)
    for i in range(chunks - 2, -1, -1):
        total = total * R.decx[i : i + 1, :] + R.dl[i].astype(F32)
    R.piece[...] = total


def inside_backward(R, per_band):
    heads = R.wx.shape[1] // (LANES // 2)

    @pl.loop(0, R.x.shape[0] // Q)
    def _(i):
        rows = rows_at(i)
        row = lax.broadcasted_iota(jnp.int32, (Q, Q), 0)
        col = lax.broadcasted_iota(jnp.int32, (Q, Q), 1)
        causal = row <= col
        prod = dot_nt(R.bm[rows, :], R.cm[rows, :])
        logs = R.logs[rows, :]
        d_prod = jnp.zeros((Q, Q), F32)
        columns = jnp.zeros((Q, LANES), F32)
        R.pulls[...] = jnp.zeros_like(R.pulls)
        for pair in range(heads // 2):
            cols = pl.ds(pair * LANES, LANES)
            xt = R.xt[rows, cols]
            dy = R.dy[rows, cols]
            total = None
            for half in range(2):
                slot = slot_of(2 * pair + half, per_band)
                gap = R.logsT[slot : slot + 1, rows] - logs[:, slot : slot + 1]
                decay = jnp.exp(jnp.where(causal, gap, -1e30))
                dy_half = lane_half(dy, half)
                mix = prod * decay
                part = dot(mix.astype(BF16), dy_half)
                total = part if total is None else total + part
                d_mix = dot_nt(xt, dy_half)
                d_prod = d_prod + decay * d_mix
                pull = mix * d_mix
                R.pulls[slot : slot + 1, :] = jnp.sum(pull, axis=0, keepdims=True)
                columns = jnp.where(col == slot, jnp.sum(pull, axis=1, keepdims=True), columns)
            R.u[rows, cols] = total
        R.d_log[rows, :] = R.pulls[...].T - columns
        d_prod = d_prod.astype(BF16)
        R.db[rows, :] = dot(d_prod, R.cm[rows, :])
        R.dc[rows, :] = dot(d_prod.T, R.bm[rows, :])


def carried_backward(R):
    chunks = R.x.shape[0] // Q
    R.state[...] = R.from_after[...].astype(F32)
    later = lower_ones().T
    before = lower_ones(strict=True)
    R.rate_acc[...] = jnp.zeros_like(R.rate_acc)
    R.bias_acc[...] = jnp.zeros_like(R.bias_acc)

    @pl.loop(0, chunks)
    def _(k):
        i = chunks - 1 - k
        rows = rows_at(i)
        grad = R.state[...]
        grad_low = grad.astype(BF16)
        tail = R.tailx[rows, :].astype(F32)
        xt = R.xt[rows, :].astype(F32)
        pulled = dot(R.bm[rows, :], grad_low) * tail
        R.u[rows, :] += pulled
        tails = dot_nt((xt * pulled).astype(BF16), R.ex[...])
        R.db[rows, :] += dot_nt((xt * tail).astype(BF16), grad_low)
        R.dc[rows, :] += dot_nt(R.dyl[rows, :], R.s_in[i])
        inter = dot_nt(
            (R.dy[rows, :].astype(F32) * R.yi[rows, :].astype(F32)).astype(BF16), R.ex[...]
        )
        decay = R.decx[pl.ds(i, 1), :]
        kept = jnp.sum(grad * R.s_in[i].astype(F32), axis=0, keepdims=True) * decay
        kept = dot_nt(jnp.broadcast_to(kept, (8, kept.shape[1])).astype(BF16), R.ex[...])[0:1, :]
        R.state[...] = grad * decay + R.dl[i].astype(F32)
        d_decay = dot_exact(later, R.d_log[rows, :] + inter) + dot_exact(before, tails) + kept
        direct = dot_nt((R.xh[rows, :].astype(F32) * R.u[rows, :]).astype(BF16), R.ex[...])
        d_raw = (direct + R.rate[...] * d_decay) * R.dt_sig[rows, :]
        R.rate_acc[...] += fold8(R.dt[rows, :] * d_decay)
        R.bias_acc[...] += fold8(d_raw)
        R.d_raw[rows, :] = d_raw.astype(BF16)


def before_conv(R):
    inner = R.wx.shape[1]

    @pl.loop(0, inner // LANES)
    def _(c):
        cols = cols_at(c)
        skip = R.par[6:7, cols]

        @pl.loop(0, R.x.shape[0] // Q)
        def _(i):
            rows = rows_at(i)
            dx = R.dtx[rows, cols].astype(F32) * R.u[rows, cols] + skip * R.dy[rows, cols].astype(F32)
            R.dpre[rows, cols] = dx * R.slope[rows, cols].astype(F32)

    length = R.x.shape[0]
    R.dpre[0:length, inner : inner + LANES] = R.db[...] * R.slope[:, inner : inner + LANES].astype(F32)
    R.dpre[0:length, inner + LANES :] = R.dc[...] * R.slope[:, inner + LANES :].astype(F32)


def conv_backward(R, taps):
    length = R.x.shape[0]
    width = R.ci.shape[1]

    @pl.loop(0, width // LANES)
    def _(c):
        cols = cols_at(c)
        sums = [jnp.zeros((8, LANES), F32) for _ in range(taps + 1)]
        for i in range(length // Q):
            base = i * Q
            here = R.dpre[pl.ds(base, Q), cols]
            sums[taps] = sums[taps] + fold8(here)
            d_conv = None
            for k in range(taps):
                sums[k] = sums[k] + fold8(here * R.ci[pl.ds(HALO - (taps - 1) + k + base, Q), cols])
                term = R.par[k : k + 1, cols] * R.dpre[pl.ds(base + taps - 1 - k, Q), cols]
                d_conv = term if d_conv is None else d_conv + term
            R.dconv[pl.ds(base, Q), cols] = d_conv.astype(BF16)
        for k in range(taps + 1):
            R.vec[k : k + 1, cols] = jnp.sum(sums[k], axis=0, keepdims=True)


def input_side(R):
    gain = R.gain[...]
    inner = R.wx.shape[1]
    R.norm_acc[...] = jnp.zeros_like(R.norm_acc)

    @pl.loop(0, R.x.shape[0] // Q)
    def _(i):
        rows = rows_at(i)
        d_normed = (
            dot_nt(R.dz[rows, :], R.wz[...])
            + dot_nt(R.dconv[rows, 0:inner], R.wx[...])
            + dot_nt(R.dconv[rows, inner:], R.wbc[...])
            + dot(R.d_raw[rows, :], R.wdt[...])
        )
        x = R.x[rows, :].astype(F32)
        inv = R.inv_rms[rows, :]
        R.norm_acc[...] += fold8(d_normed * x * inv)
        d_scaled = d_normed * gain
        middle = jnp.mean(d_scaled * x, axis=-1, keepdims=True)
        R.input_grad[rows, :] = (
            R.g[rows, :].astype(F32) + inv * d_scaled - x * (inv * inv * inv * middle)
        )


def small_sums(R):
    inner = R.wx.shape[1]
    width = R.gain.shape[1]
    R.vec[5:16, :] = jnp.zeros((11, R.vec.shape[1]), F32)
    R.vec[5:6, 0:inner] = jnp.sum(R.gain_acc[...], axis=0, keepdims=True)
    R.vec[6:7, 0:width] = jnp.sum(R.norm_acc[...], axis=0, keepdims=True)
    R.vec[7:8, 0:LANES] = jnp.sum(R.bias_acc[...], axis=0, keepdims=True)
    R.vec[8:9, 0:LANES] = jnp.sum(R.rate_acc[...], axis=0, keepdims=True) * R.rate[...]
    skip = R.skip_acc[...]
    high = skip.astype(BF16)
    low = (skip - high.astype(F32)).astype(BF16)
    R.vec[9:10, 0:LANES] = jnp.sum(
        dot_nt(high, R.ex[...]) + dot_nt(low, R.ex[...]), axis=0, keepdims=True
    )


def neighbour(R, at):
    return {"seq": at}


def send(R, src, dst, index, at):
    return pltpu.make_async_remote_copy(
        src_ref=src,
        dst_ref=dst,
        send_sem=R.send_sem.at[index],
        recv_sem=R.recv_sem.at[index],
        device_id=neighbour(R, at),
        device_id_type=pl.DeviceIdType.MESH,
    )


PARTS = 3


def chain(R, first_sem, landing, place, count, step):
    has_from = place > 0 if step > 0 else place < count - 1
    has_to = place < count - 1 if step > 0 else place > 0
    width = R.piece.shape[1] // PARTS
    for part in range(PARTS):
        cols = pl.ds(part * width, width)
        copy = send(R, R.outgoing.at[:, cols], landing.at[:, cols], first_sem + part, place + step)

        @pl.when(has_from)
        def _():
            copy.wait_recv()

        @pl.when(has_to)
        def _():
            incoming = landing[:, cols].astype(F32)
            R.outgoing[:, cols] = (
                R.piece[:, cols] + R.piece_decay[:, cols] * incoming
            ).astype(BF16)
            copy.start()


def chain_sent(R, first_sem, landing, place, count, step):
    has_to = place < count - 1 if step > 0 else place > 0
    width = R.piece.shape[1] // PARTS

    @pl.when(has_to)
    def _():
        for part in range(PARTS):
            cols = pl.ds(part * width, width)
            send(R, R.outgoing.at[:, cols], landing.at[:, cols], first_sem + part, place + step).wait_send()


X_SEM, FWD_SEM, BWD_SEM, PRE_SEM, SEMS = 0, 1, 1 + PARTS, 1 + 2 * PARTS, 2 + 2 * PARTS


def layer(names, bands, head_dim, taps, *refs):
    R = types.SimpleNamespace(**dict(zip(names, refs)))
    R.dl, R.u, R.dyl, R.state = R.sl, R.z, R.gated, R.piece
    R.y = R.dpre.at[0 : R.x.shape[0], 0 : R.wx.shape[1]]
    count = lax.axis_size("seq")
    place = lax.axis_index("seq")
    per_band = R.wx.shape[1] // head_dim // bands
    length = R.x.shape[0]
    first, last = place == 0, place == count - 1

    barrier = pltpu.get_barrier_semaphore()

    @pl.when(jnp.logical_not(last))
    def _():
        pl.semaphore_signal(barrier, 1, device_id=neighbour(R, place + 1), device_id_type=pl.DeviceIdType.MESH)

    @pl.when(jnp.logical_not(first))
    def _():
        pl.semaphore_signal(barrier, 1, device_id=neighbour(R, place - 1), device_id_type=pl.DeviceIdType.MESH)

    pl.semaphore_wait(barrier, jnp.where(first | last, 1, 2))

    x_copy = send(R, R.x.at[pl.ds(length - HALO, HALO), :], R.x_halo, X_SEM, place + 1)

    @pl.when(jnp.logical_not(last))
    def _():
        x_copy.start()

    @pl.when(first)
    def _():
        R.x_halo[...] = jnp.zeros_like(R.x_halo)
        R.from_before[...] = jnp.zeros_like(R.from_before)

    @pl.when(last)
    def _():
        R.from_after[...] = jnp.zeros_like(R.from_after)
        R.dpre_halo[...] = jnp.zeros_like(R.dpre_halo)

    head_spread(R, bands, head_dim)
    norm_rows(R)

    @pl.when(jnp.logical_not(first))
    def _():
        x_copy.wait_recv()

    norm_halo(R)
    project_x(R)
    convolve(R, taps)
    step_sizes(R)
    local_states(R)
    early = place < count // 2

    @pl.when(early)
    def _():
        chain(R, FWD_SEM, R.from_before, place, count, 1)

    project_z(R)
    hidden_grad(R)
    inside_forward(R, per_band)

    @pl.when(jnp.logical_not(early))
    def _():
        chain(R, FWD_SEM, R.from_before, place, count, 1)

    carried_forward(R)
    chain_sent(R, FWD_SEM, R.from_before, place, count, 1)
    gate(R)
    local_adjoints(R)

    @pl.when(jnp.logical_not(early))
    def _():
        chain(R, BWD_SEM, R.from_after, place, count, -1)

    branch_out(R)
    grad_tiles(R.gT, R.hidden, R.go)
    grad_tiles(R.xnT, R.dz, R.gz)
    inside_backward(R, per_band)

    @pl.when(early)
    def _():
        chain(R, BWD_SEM, R.from_after, place, count, -1)

    carried_backward(R)
    chain_sent(R, BWD_SEM, R.from_after, place, count, -1)
    before_conv(R)
    R.dpre_out[...] = R.dpre[0:HALO, :].astype(BF16)
    pre_copy = send(R, R.dpre_out, R.dpre_halo, PRE_SEM, place - 1)

    @pl.when(jnp.logical_not(first))
    def _():
        pre_copy.start()

    @pl.when(jnp.logical_not(last))
    def _():
        pre_copy.wait_recv()

    R.dpre[pl.ds(length, HALO), :] = R.dpre_halo[...].astype(F32)
    conv_backward(R, taps)
    grad_tiles(R.xnT, R.dconv.at[:, 0 : R.wx.shape[1]], R.gx)
    R.gbc[...] = dot(R.xnT[...], R.dconv[:, R.wx.shape[1] :]).astype(R.gbc.dtype)
    R.gdt[...] = dot(R.d_raw[...].T, R.xn[HALO:, :]).astype(R.gdt.dtype)
    input_side(R)
    small_sums(R)

    @pl.when(jnp.logical_not(last))
    def _():
        x_copy.wait_send()

    @pl.when(jnp.logical_not(first))
    def _():
        pre_copy.wait_send()


def run_layer(x, g, gain, wz, wx, wbc, wdt, wo, par, bands, head_dim, taps):
    length, width = x.shape
    inner = wz.shape[1]
    conv = inner + wbc.shape[1]
    chunks = length // Q
    ins = dict(x=x, g=g, gain=gain, wz=wz, wx=wx, wbc=wbc, wdt=wdt, wo=wo, par=par)
    outs = dict(
        layer_out=((length, width), BF16),
        input_grad=((length, width), F32),
        gz=((width, inner), BF16),
        gx=((width, inner), BF16),
        go=((width, inner), BF16),
        gbc=((width, wbc.shape[1]), BF16),
        gdt=((LANES, width), F32),
        vec=((16, conv), F32),
    )
    scratch = dict(
        ex=((LANES, inner), BF16),
        xn=((HALO + length, width), BF16),
        xnT=((width, length), BF16),
        gT=((width, length), BF16),
        inv_rms=((length, 1), F32),
        x_halo=((HALO, width), BF16),
        ci=((HALO + length, conv), F32),
        z=((length, inner), F32),
        xh=((length, inner), BF16),
        xt=((length, inner), BF16),
        bm=((length, LANES), BF16),
        cm=((length, LANES), BF16),
        slope=((length, conv), BF16),
        rate=((1, LANES), F32),
        dt=((length, LANES), F32),
        dt_sig=((length, LANES), F32),
        logs=((length, LANES), F32),
        logsT=((LANES, length), F32),
        ends=((8, LANES), F32),
        decx=((8, inner), F32),
        dtx=((length, inner), BF16),
        expx=((length, inner), BF16),
        tailx=((length, inner), BF16),
        sl=((chunks, LANES, inner), BF16),
        s_in=((chunks, LANES, inner), BF16),
        piece=((LANES, inner), F32),
        piece_decay=((1, inner), F32),
        outgoing=((LANES, inner), BF16),
        from_before=((LANES, inner), BF16),
        from_after=((LANES, inner), BF16),
        yi=((length, inner), BF16),
        dh=((length, inner), BF16),
        gated=((length, inner), BF16),
        hidden=((length, inner), BF16),
        dz=((length, inner), BF16),
        dy=((length, inner), BF16),
        gain_acc=((8, inner), F32),
        skip_acc=((8, inner), F32),
        norm_acc=((8, width), F32),
        rate_acc=((8, LANES), F32),
        bias_acc=((8, LANES), F32),
        pulls=((LANES, Q), F32),
        d_log=((length, LANES), F32),
        db=((length, LANES), F32),
        dc=((length, LANES), F32),
        d_raw=((length, LANES), BF16),
        dpre=((length + HALO, conv), F32),
        dpre_out=((HALO, conv), BF16),
        dpre_halo=((HALO, conv), BF16),
        dconv=((length, conv), BF16),
    )
    names = (*ins, *outs, *scratch, "send_sem", "recv_sem")
    return pl.pallas_call(
        functools.partial(layer, names, bands, head_dim, taps),
        out_shape=[jax.ShapeDtypeStruct(*v) for v in outs.values()],
        in_specs=[pl.BlockSpec(memory_space=pltpu.VMEM)] * len(ins),
        out_specs=[pl.BlockSpec(memory_space=pltpu.VMEM)] * len(outs),
        scratch_shapes=[pltpu.VMEM(*v) for v in scratch.values()]
        + [pltpu.SemaphoreType.DMA((SEMS,)), pltpu.SemaphoreType.DMA((SEMS,))],
        compiler_params=pltpu.CompilerParams(
            collective_id=0, has_side_effects=True, vmem_limit_bytes=VMEM_BYTES
        ),
    )(*ins.values())


VMEM_BYTES = 64 * 2**20 - 2**18


def body(residual, cotangent, norm_gain, w_zx, w_bc, w_dt, x_kernel, x_offset, bc_kernel, bc_offset, dt_bias, a_log, d_skip, gate_gain, w_out):
    pieces, length, width = residual.shape
    bands = lax.axis_size("wb")
    heads_own, inner_own, state = w_dt.shape[1], w_zx.shape[2], w_bc.shape[2]
    heads, inner, conv = heads_own * bands, inner_own * bands, inner_own * bands + 2 * state
    head_dim = inner_own // heads_own
    taps = x_kernel.shape[0]
    groups = LANES // SLOTS
    groups = min(groups, 4)
    wzx = lax.all_gather(lax.all_gather(w_zx, "wa", axis=0, tiled=True), "wb", axis=2, tiled=True)
    wbc = lax.all_gather(w_bc, "wa", axis=0, tiled=True).reshape(width, 2 * state)
    wdt = lax.all_gather(lax.all_gather(w_dt, "wa", axis=0, tiled=True), "wb", axis=1, tiled=True)
    wo = lax.all_gather(lax.all_gather(w_out, "wa", axis=0, tiled=True), "wb", axis=1, tiled=True)
    per = heads // groups

    def slots(rows):
        rows = rows.reshape(groups, per, -1)
        rows = jnp.pad(rows, ((0, 0), (0, SLOTS - per), (0, 0))).reshape(groups * SLOTS, -1)
        return jnp.pad(rows, ((0, LANES - groups * SLOTS), (0, 0)))

    def unslots(rows):
        return rows[: groups * SLOTS].reshape(groups, SLOTS, -1)[:, :per].reshape(heads, -1)

    own = jnp.concatenate(
        [
            x_kernel.astype(F32),
            x_offset.astype(F32)[None],
            gate_gain.astype(F32)[None],
            jnp.repeat(d_skip, head_dim)[None],
        ],
        axis=0,
    )
    par_x = lax.all_gather(own, "wb", axis=1, tiled=True)
    small = lax.all_gather(jnp.stack([dt_bias, a_log]), "wb", axis=1, tiled=True)
    par_bc = jnp.concatenate(
        [bc_kernel.reshape(taps, 2 * state).astype(F32), bc_offset.reshape(1, 2 * state).astype(F32), jnp.zeros((2, 2 * state), F32)], axis=0
    )
    par = jnp.concatenate([par_x, par_bc], axis=1)
    rows = jnp.pad(slots(small.T).T, ((0, 0), (0, conv - LANES)))
    par = jnp.concatenate([par, rows, jnp.zeros((7, conv), F32)], axis=0)
    layer_out, input_grad, gz, gx, go, gbc, gdt, vec = run_layer(
        residual.reshape(length, width),
        cotangent.reshape(length, width),
        norm_gain.astype(F32)[None],
        wzx[:, 0],
        wzx[:, 1],
        wbc,
        slots(wdt.T),
        wo,
        par,
        groups,
        head_dim,
        taps,
    )

    def share(grad, columns=True):
        grad = grad.astype(F32)
        grad = lax.psum_scatter(grad, "wa", scatter_dimension=0, tiled=True)
        if columns:
            grad = lax.psum_scatter(grad, "wb", scatter_dimension=grad.ndim - 1, tiled=True)
        else:
            grad = lax.psum(grad, "wb")
        return lax.psum(grad, "seq")

    zx_grad = share(jnp.stack([gz, gx], axis=1))
    bc_grad = share(gbc, False).reshape(-1, 2, state)
    dt_grad = share(unslots(gdt).T)
    out_grad = share(go)
    vec = lax.psum(vec, ("seq", "wa", "wb"))
    mine = lax.axis_index("wb")
    wide = lax.dynamic_slice_in_dim(vec[:, :inner], mine * inner_own, inner_own, 1)
    heads_vec = unslots(vec[7:10, :LANES].T)
    heads_vec = lax.dynamic_slice_in_dim(heads_vec, mine * heads_own, heads_own, 0)
    return (
        layer_out.reshape(residual.shape),
        input_grad.reshape(residual.shape),
        vec[6, :width],
        zx_grad,
        bc_grad,
        dt_grad,
        wide[0:taps],
        wide[4],
        vec[0:taps, inner:].reshape(taps, 2, state),
        vec[4, inner:].reshape(2, state),
        heads_vec[:, 0],
        heads_vec[:, 1],
        heads_vec[:, 2],
        wide[5],
        out_grad,
    )


def solution(mesh):
    batch = P(("wa", "wb"), "seq", None)
    ins = (
        batch, batch, P(), P("wa", None, "wb"), P("wa", None, None), P("wa", "wb"), P(None, "wb"), P("wb"), P(), P(),
        P("wb"), P("wb"), P("wb"), P("wb"), P("wa", "wb"),
    )
    outs = (
        batch, batch, P(), P("wa", None, "wb"), P("wa", None, None), P("wa", "wb"), P(None, "wb"), P("wb"), P(), P(),
        P("wb"), P("wb"), P("wb"), P("wb"), P("wa", "wb"),
    )
    return jax.shard_map(body, mesh=mesh, in_specs=ins, out_specs=outs, check_vma=False)
```

```python
import functools
import types

import jax
import jax.numpy as jnp
from jax import lax
from jax.experimental import pallas as pl
from jax.experimental.pallas import tpu as pltpu
from jax.sharding import PartitionSpec as P

F32, BF16 = jnp.float32, jnp.bfloat16
EPSILON = 1e-05
Q = 128
LANES = 128
HALO = 16
SLOTS = 16
TILE = 256
BANDS = 4
NT = (((1,), (1,)), ((), ()))


def dot(a, b):
    return jnp.dot(a, b, preferred_element_type=F32)


def dot_nt(a, b):
    return lax.dot_general(a, b, NT, preferred_element_type=F32)


def dot_exact(a, b):
    return jnp.dot(a, b, precision=lax.Precision.HIGHEST, preferred_element_type=F32)


def sigmoid(v):
    return 0.5 + 0.5 * jnp.tanh(0.5 * v)


def fold8(v):
    return v.reshape(v.shape[0] // 8, 8, v.shape[1]).sum(axis=0)


def at(start, size):
    return pl.ds(pl.multiple_of(start, 16), size)


def lanes(start, size):
    return pl.ds(pl.multiple_of(start, LANES), size)


def rows_at(i, size=Q, base=0):
    return at(i * size + base, size)


def cols_at(i, size=LANES):
    return lanes(i * size, size)


def band_cols(R, band):
    width = R.wx.shape[1] // BANDS
    return lanes(width * band, width)


def head_spread(R, head_dim):
    inner = R.ex.shape[1]
    per_band = inner // BANDS
    row = lax.broadcasted_iota(jnp.int32, (LANES, LANES), 0)

    @pl.loop(0, inner // LANES)
    def _(c):
        lane = lax.broadcasted_iota(jnp.int32, (LANES, LANES), 1) + c * LANES
        hit = jnp.zeros((LANES, LANES), jnp.bool_)
        for band in range(BANDS):
            first = lane - band * per_band
            inside = (first >= 0) & (first < per_band)
            head = lax.shift_right_arithmetic(first, head_dim.bit_length() - 1)
            hit = hit | (inside & (row == band * SLOTS + head))
        R.ex[:, cols_at(c)] = jnp.where(hit, 1.0, 0.0).astype(BF16)

    lane = lax.broadcasted_iota(jnp.int32, (Q, LANES), 1)
    for head in range(R.pick.shape[0] // Q):
        R.pick[pl.ds(head * Q, Q), :] = jnp.where(lane == head, 1.0, 0.0).astype(BF16)


def norm_rows(R):
    gain = R.gain[...]

    @pl.loop(0, R.x.shape[0] // Q)
    def _(i):
        rows = R.x[rows_at(i), :].astype(F32)
        inv = lax.rsqrt(jnp.mean(rows * rows, axis=-1, keepdims=True) + EPSILON)
        value = (rows * inv * gain).astype(BF16)
        R.xn[rows_at(i, base=HALO), :] = value
        R.inv_rms[rows_at(i), :] = inv
        R.xnT[:, cols_at(i)] = value.T
        R.gT[:, cols_at(i)] = R.g[rows_at(i), :].T


def norm_halo(R):
    rows = R.x_halo[...].astype(F32)
    inv = lax.rsqrt(jnp.mean(rows * rows, axis=-1, keepdims=True) + EPSILON)
    R.xn[0:HALO, :] = (rows * inv * R.gain[...]).astype(BF16)


def project_x(R, band):
    cols = band_cols(R, band)
    R.ci[:, cols] = dot(R.xn[...], R.wx[:, cols])


def project_bc(R):
    R.ci[:, R.wx.shape[1] :] = dot(R.xn[...], R.wbc[...])


def project_z(R, band):
    cols = band_cols(R, band)
    R.z[:, cols] = dot(R.xn[HALO:, :], R.wz[:, cols])


def conv_tile(R, taps, cols, put):
    for i in range(R.x.shape[0] // Q):
        rows = pl.ds(i * Q, Q)
        pre = R.par[4:5, cols]
        for k in range(taps):
            conv_in = R.ci[pl.ds(HALO - (taps - 1) + k + i * Q, Q), cols]
            pre = pre + R.par[k : k + 1, cols] * conv_in
        R.cib[rows, cols] = conv_in.astype(BF16)
        sig = sigmoid(pre)
        act = pre * sig
        put(rows, act.astype(BF16))
        R.slope[rows, cols] = (sig + act * (1.0 - sig)).astype(BF16)


def convolve(R, taps, band):
    width = R.wx.shape[1] // BANDS

    @pl.loop(0, width // LANES)
    def _(c):
        cols = lanes(width * band + c * LANES, LANES)

        def put(rows, act):
            R.xh[rows, cols] = act

        conv_tile(R, taps, cols, put)


def convolve_bc(R, taps):
    inner = R.wx.shape[1]

    def put_b(rows, act):
        R.bm[rows, :] = act

    def put_c(rows, act):
        R.cm[rows, :] = act

    conv_tile(R, taps, pl.ds(inner, LANES), put_b)
    conv_tile(R, taps, pl.ds(inner + LANES, LANES), put_c)

    @pl.loop(0, R.x.shape[0] // Q)
    def _(i):
        rows = rows_at(i)
        R.prod[rows, :] = dot_nt(R.cm[rows, :], R.bm[rows, :])
        R.prodT[rows, :] = dot_nt(R.bm[rows, :], R.cm[rows, :])


def lower_ones(strict=False):
    row = lax.broadcasted_iota(jnp.int32, (Q, Q), 0)
    col = lax.broadcasted_iota(jnp.int32, (Q, Q), 1)
    return jnp.where(row > col if strict else row >= col, 1.0, 0.0).astype(F32)


def step_sizes(R, per_band):
    cols = R.wx.shape[1] // BANDS
    lane = lax.broadcasted_iota(jnp.int32, (8, LANES), 1)
    heads = jnp.zeros((8, LANES), F32)
    for band in range(BANDS):
        block = R.par[8:16, pl.ds(band * cols, LANES)]
        heads = heads + pltpu.roll(jnp.where(lane < per_band, block, 0.0), band * SLOTS, 1)
    R.heads[...] = heads
    R.rate[...] = -jnp.exp(R.heads[1:2, :])
    bias, rate = R.heads[0:1, :], R.rate[...]
    ones = lower_ones()
    chunks = R.x.shape[0] // Q
    R.ends[...] = jnp.zeros_like(R.ends)
    for i in range(chunks):
        rows = pl.ds(i * Q, Q)
        v = dot_nt(R.xn[pl.ds(HALO + i * Q, Q), :], R.wdt[...]) + bias
        dt = jnp.maximum(v, 0.0) + jnp.log1p(jnp.exp(-jnp.abs(v)))
        R.dt[rows, :] = dt
        R.dt_sig[rows, :] = jax.nn.sigmoid(v)
        logs = dot_exact(ones, dt * rate)
        R.logs[rows, :] = logs
        R.logsT[:, rows] = logs.T
        last = logs[Q - 1 : Q, :]
        R.ends[i : i + 1, :] = last
        R.dt_low[rows, :] = dt.astype(BF16)
        R.tail_low[rows, :] = jnp.exp(last - logs).astype(BF16)
        R.exp_low[rows, :] = jnp.exp(logs).astype(BF16)
    decay = jnp.exp(R.ends[...])
    high = decay.astype(BF16)
    low = (decay - high.astype(F32)).astype(BF16)
    R.decx[...] = dot(high, R.ex[...]) + dot(low, R.ex[...])


def local_states(R, band):
    cols = band_cols(R, band)
    chunks = R.x.shape[0] // Q

    @pl.loop(0, chunks)
    def _(i):
        rows = rows_at(i)
        spread = R.ex[:, cols]
        weighted = R.xh[rows, cols].astype(F32) * dot(R.dt_low[rows, :], spread)
        R.xt[rows, cols] = weighted.astype(BF16)
        ended = (weighted * dot(R.tail_low[rows, :], spread)).astype(BF16)
        R.sl[rows_at(i, LANES), cols] = dot(R.bm[rows, :].T, ended).astype(BF16)

    total = R.sl[0:LANES, cols].astype(F32)
    decay = R.decx[0:1, cols]
    for i in range(1, chunks):
        step = R.decx[i : i + 1, cols]
        total = total * step + R.sl[rows_at(i, LANES), cols].astype(F32)
        decay = decay * step
    R.piece[:, cols] = total
    R.piece_decay[:, cols] = decay


def lane_half(value, half):
    lane = lax.broadcasted_iota(jnp.int32, value.shape, 1)
    keep = lane < LANES // 2 if half == 0 else lane >= LANES // 2
    return jnp.where(keep, value, jnp.zeros_like(value))


def causal_mask(by_row):
    row = lax.broadcasted_iota(jnp.int32, (Q, Q), 0)
    col = lax.broadcasted_iota(jnp.int32, (Q, Q), 1)
    return row >= col if by_row else row <= col


def band_logs(R, rows, band):
    return pltpu.roll(R.logs[rows, :], lax.rem(LANES - SLOTS * band, LANES), 1)


def inside_forward(R, per_band, band):
    width = R.wx.shape[1] // BANDS

    @pl.loop(0, R.x.shape[0] // Q)
    def _(i):
        rows = rows_at(i)
        causal = causal_mask(True)
        logs = band_logs(R, rows, band)
        logsT = R.logsT[at(SLOTS * band, 8), rows]
        for pair in range(per_band // 2):
            cols = lanes(width * band + pair * LANES, LANES)
            xt = R.xt[rows, cols]
            total = None
            for half in range(2):
                head = 2 * pair + half
                gap = logs[:, head : head + 1] - logsT[head : head + 1, :]
                decay = jnp.exp(jnp.where(causal, gap, -1e30))
                part = dot((R.prod[rows, :] * decay).astype(BF16), lane_half(xt, half))
                total = part if total is None else total + part
            R.y[rows, cols] = total


def carried_forward(R, band):
    cols = band_cols(R, band)
    chunks = R.x.shape[0] // Q
    state = R.from_before[:, cols].astype(F32)
    for i in range(chunks):
        rows = pl.ds(i * Q, Q)
        block = rows_at(i, LANES)
        R.s_in[block, cols] = state.astype(BF16)
        spread = dot(R.exp_low[rows, :], R.ex[:, cols])
        R.expx[rows, cols] = spread.astype(BF16)
        R.y[rows, cols] += dot(R.cm[rows, :], R.s_in[block, cols]) * spread
        if i < chunks - 1:
            state = state * R.decx[i : i + 1, cols] + R.sl[block, cols].astype(F32)


def hidden_grad(R, band):
    cols = band_cols(R, band)
    R.dh[:, cols] = dot(R.g[...], R.wo[:, cols]).astype(BF16)


def gate(R):
    inner = R.wx.shape[1]
    R.gain_acc[...] = jnp.zeros_like(R.gain_acc)
    R.skip_acc[...] = jnp.zeros_like(R.skip_acc)

    @pl.loop(0, R.x.shape[0] // Q)
    def _(i):
        rows = rows_at(i)

        def first(c, sums):
            cols = cols_at(c)
            y = R.y[rows, cols] + R.par[6:7, cols] * R.xh[rows, cols].astype(F32)
            R.y[rows, cols] = y
            z = R.z[rows, cols]
            gated = (y * (z * sigmoid(z))).astype(BF16)
            R.gated[rows, cols] = gated
            gated = gated.astype(F32)
            return (
                sums[0] + gated * gated,
                sums[1] + gated * (R.dh[rows, cols].astype(F32) * R.par[5:6, cols]),
            )

        zero = jnp.zeros((Q, LANES), F32)
        squares, cross = lax.fori_loop(0, inner // LANES, first, (zero, zero))
        inv = lax.rsqrt(jnp.sum(squares, axis=-1, keepdims=True) / inner + EPSILON)
        cross = jnp.sum(cross, axis=-1, keepdims=True) * (inv * inv * inv / inner)
        inv = jnp.broadcast_to(inv, (Q, LANES))
        cross = jnp.broadcast_to(cross, (Q, LANES))

        @pl.loop(0, inner // LANES)
        def _(c):
            cols = cols_at(c)
            gated = R.gated[rows, cols].astype(F32)
            dh = R.dh[rows, cols].astype(F32)
            gain = R.par[5:6, cols]
            scaled = gated * inv
            R.hidden[rows, cols] = (scaled * gain).astype(BF16)
            R.gain_acc[:, cols] += fold8(dh * scaled)
            d_gated = dh * gain * inv - gated * cross
            z = R.z[rows, cols]
            sig = sigmoid(z)
            lin = z * sig
            dy = d_gated * lin
            R.dz[rows, cols] = (d_gated * R.y[rows, cols] * (sig + lin * (1.0 - sig))).astype(BF16)
            R.dyl[rows, cols] = (dy * R.expx[rows, cols].astype(F32)).astype(BF16)
            R.dy[rows, cols] = dy.astype(BF16)
            R.skip_acc[:, cols] += fold8(dy * R.xh[rows, cols].astype(F32))


def branch_out(R):
    width = R.x.shape[1]
    for j in range(width // TILE):
        cols = pl.ds(j * TILE, TILE)
        R.layer_out[:, cols] = (
            R.x[:, cols].astype(F32) + dot_nt(R.hidden[...], R.wo[cols, :])
        ).astype(BF16)


def grad_tiles(left, right, out):
    @pl.loop(0, right.shape[1] // TILE)
    def _(j):
        cols = cols_at(j, TILE)
        out[:, cols] = dot(left[...], right[:, cols]).astype(out.dtype)


def local_adjoints(R, band):
    cols = band_cols(R, band)
    chunks = R.x.shape[0] // Q
    total = None
    for i in range(chunks - 1, -1, -1):
        rows = pl.ds(i * Q, Q)
        pulled = dot(R.cm[rows, :].T, R.dyl[rows, cols])
        R.dl[rows_at(i, LANES), cols] = pulled.astype(BF16)
        total = pulled if total is None else total * R.decx[i : i + 1, cols] + pulled
    R.piece[:, cols] = total


def inside_backward(R, per_band, band):
    width = R.wx.shape[1] // BANDS

    @pl.loop(0, R.x.shape[0] // Q)
    def _(i):
        rows = rows_at(i)
        causal = causal_mask(False)
        logs = band_logs(R, rows, band)
        d_prod = jnp.zeros((Q, Q), F32)
        logsT = R.logsT[at(SLOTS * band, 8), rows]
        highs, lows, sums = [], [], []
        for pair in range(per_band // 2):
            cols = lanes(width * band + pair * LANES, LANES)
            xt = R.xt[rows, cols]
            dy = R.dy[rows, cols]
            total = None
            for half in range(2):
                head = 2 * pair + half
                gap = logsT[head : head + 1, :] - logs[:, head : head + 1]
                decay = jnp.exp(jnp.where(causal, gap, -1e30))
                dy_half = lane_half(dy, half)
                mix = R.prodT[rows, :] * decay
                part = dot(mix.astype(BF16), dy_half)
                total = part if total is None else total + part
                d_mix = dot_nt(xt, dy_half)
                d_prod = d_prod + decay * d_mix
                pull = mix * d_mix
                sums.append(jnp.sum(pull, axis=0, keepdims=True))
                high = pull.astype(BF16)
                highs.append(high)
                lows.append((pull - high.astype(F32)).astype(BF16))
            R.u[rows, cols] = total
        R.pullsT[at(SLOTS * band, 8), rows] = jnp.concatenate([*sums, jnp.zeros((8 - per_band, Q), F32)], axis=0)
        sums = dot(jnp.concatenate(highs, axis=1), R.pick[...]) + dot(jnp.concatenate(lows, axis=1), R.pick[...])
        sums = pltpu.roll(sums, SLOTS * band, 1)
        R.pulls[rows, :] += sums
        R.d_prod[rows, :] += d_prod


def backward_start(R):
    for ref in (R.pulls, R.pullsT, R.d_prod, R.d_log, R.d_tail, R.direct):
        ref[...] = jnp.zeros_like(ref)
    R.db[...] = jnp.zeros_like(R.db)
    R.dc[...] = jnp.zeros_like(R.dc)


def carried_backward(R, band):
    cols = band_cols(R, band)
    chunks = R.x.shape[0] // Q
    grad = R.from_after[:, cols].astype(F32)
    for i in range(chunks - 1, -1, -1):
        rows = pl.ds(i * Q, Q)
        block = rows_at(i, LANES)
        spread = R.ex[:, cols]
        low = grad.astype(BF16)
        dt, tail = dot(R.dt_low[rows, :], spread), dot(R.tail_low[rows, :], spread)
        xt = R.xt[rows, cols].astype(F32)
        pulled = dot(R.bm[rows, :], low) * tail
        u = R.u[rows, cols] + pulled
        R.d_tail[rows, :] += dot_nt((xt * pulled).astype(BF16), spread)
        R.db[rows, :] += dot_nt((xt * tail).astype(BF16), low)
        state = R.s_in[block, cols]
        dyl = R.dyl[rows, cols]
        R.dc[rows, :] += dot_nt(dyl, state)
        R.d_log[rows, :] += dot_nt((dyl.astype(F32) * dot(R.cm[rows, :], state)).astype(BF16), spread)
        decay = R.decx[i : i + 1, cols]
        R.kept[i : i + 1, cols] = jnp.sum(grad * state.astype(F32), axis=0, keepdims=True) * decay
        if i:
            grad = grad * decay + R.dl[block, cols].astype(F32)
        R.direct[rows, :] += dot_nt((R.xh[rows, cols].astype(F32) * u).astype(BF16), spread)
        dx = dt * u + R.par[6:7, cols] * R.dy[rows, cols].astype(F32)
        R.dpre[rows, cols] = dx * R.slope[rows, cols].astype(F32)


def step_grads(R):
    chunks = R.x.shape[0] // Q
    inner = R.wx.shape[1]
    later = lower_ones().T
    before = lower_ones(strict=True)
    high = R.kept[...].astype(BF16)
    low = (R.kept[...] - high.astype(F32)).astype(BF16)
    kept = dot_nt(high, R.ex[...]) + dot_nt(low, R.ex[...])
    rate_acc = jnp.zeros((8, LANES), F32)
    bias_acc = jnp.zeros((8, LANES), F32)
    for i in range(chunks):
        rows = pl.ds(i * Q, Q)
        sides = R.d_log[rows, :] + R.pullsT[:, rows].T - R.pulls[rows, :]
        d_decay = dot_exact(later, sides) + dot_exact(before, R.d_tail[rows, :]) + kept[i : i + 1, :]
        d_raw = (R.direct[rows, :] + R.rate[...] * d_decay) * R.dt_sig[rows, :]
        rate_acc = rate_acc + fold8(R.dt[rows, :] * d_decay)
        bias_acc = bias_acc + fold8(d_raw)
        R.d_raw[rows, :] = d_raw.astype(BF16)
        d_prod = R.d_prod[rows, :].astype(BF16)
        db = R.db[rows, :] + dot(d_prod, R.cm[rows, :])
        dc = R.dc[rows, :] + dot(d_prod.T, R.bm[rows, :])
        R.dpre[rows, inner : inner + LANES] = db * R.slope[rows, inner : inner + LANES].astype(F32)
        R.dpre[rows, inner + LANES :] = dc * R.slope[rows, inner + LANES :].astype(F32)
    R.rate_acc[...] = rate_acc
    R.bias_acc[...] = bias_acc


def conv_backward(R, taps, first, width):
    length = R.x.shape[0]
    halo = lanes(first, width)
    R.dpre[pl.ds(length, HALO), halo] = R.dpre_halo[:, halo].astype(F32)

    @pl.loop(0, width // LANES)
    def _(c):
        cols = lanes(first + c * LANES, LANES)
        sums = [jnp.zeros((8, LANES), F32) for _ in range(taps + 1)]
        for i in range(length // Q):
            base = i * Q
            conv_in = R.cib[pl.ds(base, Q), cols].astype(F32)
            d_conv = None
            for k in range(taps):
                ahead = R.dpre[pl.ds(base + taps - 1 - k, Q), cols]
                sums[k] = sums[k] + fold8(ahead * conv_in)
                term = R.par[k : k + 1, cols] * ahead
                d_conv = term if d_conv is None else d_conv + term
            sums[taps] = sums[taps] + fold8(ahead)
            R.dconv[pl.ds(base, Q), cols] = d_conv.astype(BF16)
        for k in range(taps + 1):
            R.vec[k : k + 1, cols] = jnp.sum(sums[k], axis=0, keepdims=True)


def input_side(R):
    width = R.x.shape[1]
    inner = R.wx.shape[1]
    for j in range(width // TILE):
        cols = pl.ds(j * TILE, TILE)
        R.input_grad[:, cols] = (
            dot_nt(R.dz[...], R.wz[cols, :])
            + dot_nt(R.dconv[:, 0:inner], R.wx[cols, :])
            + dot_nt(R.dconv[:, inner:], R.wbc[cols, :])
            + dot(R.d_raw[...], R.wdt[:, cols])
        )
    gain = R.gain[...]
    R.norm_acc[...] = jnp.zeros_like(R.norm_acc)

    @pl.loop(0, R.x.shape[0] // 64)
    def _(i):
        rows = rows_at(i, 64)
        d_normed = R.input_grad[rows, :]
        x = R.x[rows, :].astype(F32)
        inv = R.inv_rms[rows, :]
        pulled = d_normed * x
        R.norm_acc[...] += fold8(pulled * inv)
        middle = jnp.sum(pulled * gain, axis=-1, keepdims=True) * (inv * inv * inv / width)
        R.input_grad[rows, :] = R.g[rows, :].astype(F32) + (d_normed * gain) * inv - x * middle


def small_sums(R):
    inner = R.wx.shape[1]
    width = R.gain.shape[1]
    R.vec[5:8, :] = jnp.zeros((3, R.vec.shape[1]), F32)
    R.vec[5:6, 0:inner] = jnp.sum(R.gain_acc[...], axis=0, keepdims=True)
    R.vec[6:7, 0:width] = jnp.sum(R.norm_acc[...], axis=0, keepdims=True)
    R.vec[5:6, inner : inner + LANES] = jnp.sum(R.bias_acc[...], axis=0, keepdims=True)
    R.vec[5:6, inner + LANES :] = jnp.sum(R.rate_acc[...], axis=0, keepdims=True) * R.rate[...]
    skip = R.skip_acc[...]
    high = skip.astype(BF16)
    low = (skip - high.astype(F32)).astype(BF16)
    R.vec[6:7, width : width + LANES] = jnp.sum(
        dot_nt(high, R.ex[...]) + dot_nt(low, R.ex[...]), axis=0, keepdims=True
    )


SEMS = 256


class Wires:
    def __init__(self, R):
        self.R, self.used, self.started = R, 0, []

    def new(self):
        self.used += 1
        return self.used - 1

    def copy(self, src, dst, sem, where):
        return pltpu.make_async_remote_copy(
            src_ref=src,
            dst_ref=dst,
            send_sem=self.R.send_sem.at[sem],
            recv_sem=self.R.recv_sem.at[sem],
            device_id=where,
            device_id_type=pl.DeviceIdType.MESH,
        )

    def start(self, src, dst, sem, where):
        copy = self.copy(src, dst, sem, where)
        copy.start()
        self.started.append(copy)

    def arrived(self, dst, sem, where):
        self.copy(dst, dst, sem, where).wait_recv()

    def drain(self):
        for copy in self.started:
            copy.wait_send()


class Place:
    def __init__(self):
        self.seq, self.a, self.b = lax.axis_index("seq"), lax.axis_index("wa"), lax.axis_index("wb")
        self.bands, self.rows = lax.axis_size("wb"), lax.axis_size("wa")
        self.c = lax.rem(self.seq, 2)
        self.y = lax.div(self.seq, 2)
        self.core = {"seq": self.seq + 1 - 2 * self.c}
        self.over_y = {"seq": lax.rem(self.seq + 2, 4)}
        self.over_x = {"wa": 1 - self.a}

    def band(self, k):
        return lax.rem(self.b + k + self.bands, self.bands)

    def over_z(self, k):
        return {"wb": self.band(k)}

    def greet(self):
        barrier = pltpu.get_barrier_semaphore()
        peers = [{"seq": lax.rem(self.seq + k, 4)} for k in range(1, 4)]
        peers += [self.over_z(k) for k in range(1, self.bands)] + [self.over_x]
        for peer in peers:
            pl.semaphore_signal(barrier, 1, device_id=peer, device_id_type=pl.DeviceIdType.MESH)
        pl.semaphore_wait(barrier, len(peers))


class Grid:
    def __init__(self, row, col, half, own, width):
        self.row, self.col, self.half, self.own, self.width = row, col, half, own, width
        self.span = half - own

    def cols(self, band):
        return lanes(self.col(band), self.width)

    def half_rows(self, a, band, c):
        return at(self.row(a, band) + self.half * c, self.half)

    def span_rows(self, a, band, p):
        return at(self.row(a, band) + self.half * p.c + self.own * p.y, self.span)

    def own_rows(self, a, band, p, y):
        return at(self.row(a, band) + self.half * p.c + (self.half - self.own) * y, self.own)


class Gather:
    def __init__(self, wires, p, shard, whole, grid, local_sem):
        self.w, self.p, self.shard, self.whole, self.g = wires, p, shard, whole, grid
        self.z = [wires.new() for _ in range(p.bands)]
        self.x = [wires.new() for _ in range(p.bands)]
        self.y = [[wires.new() for _ in range(p.bands)] for _ in range(2)]
        self.c = [[wires.new() for _ in range(p.bands)] for _ in range(2)]
        self.local = pltpu.make_async_copy(
            shard, whole.at[at(grid.row(p.a, p.b), shard.shape[0]), grid.cols(p.b)], local_sem
        )

    def here(self, rows, k):
        return self.whole.at[rows, self.g.cols(self.p.band(-k))]

    def own_span(self):
        return self.shard.at[at(self.g.half * self.p.c + self.g.own * self.p.y, self.g.span), :]

    def start(self):
        p, g = self.p, self.g
        rows = g.span_rows(p.a, p.b, p)
        for k in range(1, p.bands):
            self.w.start(self.own_span(), self.here(rows, 0), self.z[k], p.over_z(k))
        self.w.start(self.own_span(), self.here(rows, 0), self.x[0], p.over_x)
        self.local.start()

    def over_x(self, k):
        if k == 0:
            return
        p, g = self.p, self.g
        rows = g.span_rows(p.a, p.b, p)
        self.w.arrived(self.here(rows, k), self.z[k], p.over_z(k))
        self.w.start(self.here(rows, k), self.here(rows, k), self.x[k], p.over_x)
        mine = self.here(g.own_rows(p.a, p.b, p, p.y), k)
        self.w.start(mine, mine, self.y[0][k], p.over_y)

    def over_y(self, k):
        p, g = self.p, self.g
        self.w.arrived(self.here(g.span_rows(1 - p.a, p.b, p), k), self.x[k], p.over_x)
        mine = self.here(g.own_rows(1 - p.a, p.b, p, p.y), k)
        self.w.start(mine, mine, self.y[1][k], p.over_y)

    def sides(self, k):
        return [(0, self.p.a), (1, 1 - self.p.a)] if k else [(1, 1 - self.p.a)]

    def over_core(self, k):
        p, g = self.p, self.g
        for side, a in self.sides(k):
            self.w.arrived(self.here(g.own_rows(a, p.b, p, 1 - p.y), k), self.y[side][k], p.over_y)
            mine = self.here(g.half_rows(a, p.b, p.c), k)
            self.w.start(mine, mine, self.c[side][k], p.core)

    def finish(self, k):
        p, g = self.p, self.g
        for side, a in self.sides(k):
            self.w.arrived(self.here(g.half_rows(a, p.b, 1 - p.c), k), self.c[side][k], p.core)
        if k == 0:
            self.local.wait()

    def each(self, step):
        for k in range(self.p.bands):
            step(k)


class Scatter:
    def __init__(self, wires, p, grad, grid, spaces):
        self.w, self.p, self.grad, self.g = wires, p, grad, grid
        self.rc, self.ry, self.rx, self.rz, self.mine, self.peer = spaces
        self.order = [*range(1, p.bands), 0]
        self.c = [[wires.new() for _ in range(p.bands)] for _ in range(2)]
        self.y = [[wires.new() for _ in range(p.bands)] for _ in range(2)]
        self.x = [wires.new() for _ in range(p.bands)]
        self.z = [wires.new() for _ in range(p.bands)]
        self.last, self.share = wires.new(), wires.new()

    @staticmethod
    def spaces(bands, grid):
        half, own, span, width = grid.half, grid.own, grid.span, grid.width
        return [
            (2, bands, half, width),
            (2, bands, own, width),
            (bands, span, width),
            (bands, span, width),
            (span, width),
            (span, width),
        ]

    def here(self, rows, k):
        return self.grad.at[rows, self.g.cols(self.p.band(k))]

    def add(self, rows, k, part):
        spot = self.here(rows, k)
        spot[...] = (spot[...].astype(F32) + part.astype(F32)).astype(BF16)

    def start_c(self, ks=None):
        p, g = self.p, self.g
        for k in self.order if ks is None else ks:
            for a in range(2):
                rows = g.half_rows(a, p.band(k), 1 - p.c)
                self.w.start(self.here(rows, k), self.rc.at[a, k], self.c[a][k], p.core)

    def start_y(self, ks=None):
        p, g = self.p, self.g
        for k in self.order if ks is None else ks:
            for a in range(2):
                self.w.arrived(self.rc.at[a, k], self.c[a][k], p.core)
                self.add(g.half_rows(a, p.band(k), p.c), k, self.rc[a, k])
                rows = g.own_rows(a, p.band(k), p, 1 - p.y)
                self.w.start(self.here(rows, k), self.ry.at[a, k], self.y[a][k], p.over_y)

    def start_x(self, ks=None):
        p, g = self.p, self.g
        for k in self.order if ks is None else ks:
            for a in range(2):
                self.w.arrived(self.ry.at[a, k], self.y[a][k], p.over_y)
                self.add(g.own_rows(a, p.band(k), p, p.y), k, self.ry[a, k])
            rows = g.span_rows(1 - p.a, p.band(k), p)
            self.w.start(self.here(rows, k), self.rx.at[k], self.x[k], p.over_x)

    def start_z(self, ks=None):
        p, g = self.p, self.g
        for k in self.order if ks is None else ks:
            rows = g.span_rows(p.a, p.band(k), p)
            self.w.arrived(self.rx.at[k], self.x[k], p.over_x)
            self.add(rows, k, self.rx[k])
            if k:
                self.w.start(self.here(rows, k), self.rz.at[k], self.z[k], p.over_z(k))

    def start_last(self):
        p, g = self.p, self.g
        total = self.here(g.span_rows(p.a, p.b, p), 0)[...].astype(F32)
        for k in range(1, p.bands):
            self.w.arrived(self.rz.at[k], self.z[k], p.over_z(k))
            total = total + self.rz[k].astype(F32)
        self.mine[...] = total.astype(BF16)
        self.w.start(self.mine, self.peer, self.last, p.over_y)

    def result(self, out, first):
        p, g = self.p, self.g
        self.w.arrived(self.peer, self.last, p.over_y)
        both = g.span - g.own
        middle = self.mine[at(g.own * (1 - p.y), both), :].astype(F32) + self.peer[at(g.own * p.y, both), :].astype(F32)
        out[at(first + g.own, both), :] = middle.astype(out.dtype)
        far = (g.half - g.own) * p.y
        out[at(first + far, g.own), :] = self.mine[at(both * p.y, g.own), :].astype(out.dtype)
        far = (g.half - g.own) * (1 - p.y)
        out[at(first + far, g.own), :] = self.peer[at(both * (1 - p.y), g.own), :].astype(out.dtype)

    def start_share(self, out):
        p, g = self.p, self.g
        self.result(out, g.half * p.c)
        mine = out.at[at(g.half * p.c, g.half), :]
        self.w.start(mine, mine, self.share, p.core)

    def finish(self, out):
        p, g = self.p, self.g
        self.w.arrived(out.at[at(g.half * (1 - p.c), g.half), :], self.share, p.core)


class Exchange:
    def __init__(self, wires, p, value, spaces):
        self.w, self.p, self.value, self.spaces = wires, p, value, spaces
        self.sems = [wires.new() for _ in range(3)]

    def start(self, step, where, src=None):
        self.w.start(self.value if src is None else src, self.spaces[step], self.sems[step], where)
        self.sent = self.w.started.pop()

    def add(self, step, where, spot=None):
        self.w.arrived(self.spaces[step], self.sems[step], where)
        self.sent.wait_send()
        spot = self.value if spot is None else spot
        total = spot[...].astype(F32) + self.spaces[step][...].astype(F32)
        spot[...] = total.astype(spot.dtype)


class Chain:
    def __init__(self, R, wires, landing, place, count, step):
        self.R, self.w, self.landing, self.step, self.place = R, wires, landing, step, place
        self.has_from = place > 0 if step > 0 else place < count - 1
        self.has_to = place < count - 1 if step > 0 else place > 0
        self.sems = [wires.new() for _ in range(BANDS)]

    def copy(self, k, band):
        cols = band_cols(self.R, band)
        where = {"seq": self.place + self.step}
        return cols, self.w.copy(self.R.outgoing.at[:, cols], self.landing.at[:, cols], self.sems[k], where)

    def run(self, k, band):
        R = self.R
        cols, copy = self.copy(k, band)

        @pl.when(self.has_from)
        def _():
            copy.wait_recv()

        @pl.when(self.has_to)
        def _():
            incoming = self.landing[:, cols].astype(F32)
            R.outgoing[:, cols] = (R.piece[:, cols] + R.piece_decay[:, cols] * incoming).astype(BF16)
            copy.start()

    def sent(self, bands):
        @pl.when(self.has_to)
        def _():
            for k, band in enumerate(bands):
                self.copy(k, band)[1].wait_send()


class Halo:
    def __init__(self, R, wires, first, last, place):
        self.R, self.w, self.first, self.last, self.place = R, wires, first, last, place
        self.copies = []

    def send(self, cols):
        R = self.R
        R.dpre_out[:, cols] = R.dpre[0:HALO, cols].astype(BF16)
        copy = self.w.copy(
            R.dpre_out.at[:, cols], R.dpre_halo.at[:, cols], self.w.new(), {"seq": self.place - 1}
        )
        self.copies.append(copy)

        @pl.when(jnp.logical_not(self.first))
        def _():
            copy.start()

        return copy

    def arrived(self, copy):
        @pl.when(jnp.logical_not(self.last))
        def _():
            copy.wait_recv()

    def sent(self):
        @pl.when(jnp.logical_not(self.first))
        def _():
            for copy in self.copies:
                copy.wait_send()


def alias(R, fused):
    half = R.states.shape[0] // 2
    R.sl, R.s_in = R.states.at[0:half, :], R.states.at[half : 2 * half, :]
    R.dl, R.u, R.dyl, R.dconv, R.dpre, R.dz, R.dy = R.sl, R.z, R.gated, R.slope, R.ci, R.dh, R.expx
    R.y = R.dpre.at[0 : R.x.shape[0], 0 : R.wx.shape[1]]
    if fused:
        R.gx = R.states.at[0 : R.wx.shape[0], :]


def own_params(R, p, taps, head_dim):
    cols, width = R.x_kernel.shape[1], R.x.shape[1]
    inner, state = R.wx.shape[1], R.bc_kernel.shape[2]
    row = lambda ref: ref[...].astype(F32).reshape(1, ref.shape[0])
    lane = lax.broadcasted_iota(jnp.int32, (1, cols), 1)
    skip = jnp.zeros((1, cols), F32)
    heads = R.d_skip.shape[0]
    for head in range(heads):
        hit = lax.shift_right_arithmetic(lane, head_dim.bit_length() - 1) == head
        skip = jnp.where(hit, row(R.d_skip)[:, head : head + 1], skip)
    pad = jnp.zeros((1, cols - heads), F32)
    block = [R.x_kernel[...].astype(F32), row(R.x_offset), row(R.gate_gain), skip, jnp.zeros((1, cols), F32)]
    block += [jnp.concatenate([row(ref), pad], axis=1) for ref in (R.dt_bias, R.a_log)]
    R.par[:, lanes(cols * p.b, cols)] = jnp.concatenate([*block, jnp.zeros((6, cols), F32)], axis=0)
    kernel, offset = R.bc_kernel[...].astype(F32), R.bc_offset[...].astype(F32)
    for half in range(2):
        rows = [kernel[:, half, :], offset[half : half + 1, :], jnp.zeros((16 - taps - 1, state), F32)]
        R.par[:, pl.ds(inner + half * state, state)] = jnp.concatenate(rows, axis=0)
    rows, slot = R.w_bc.shape[0], R.w_dt.shape[0]
    w_bc = R.w_bc[...].astype(F32)
    for half in range(2):
        R.wbc[at(rows * p.a, rows), pl.ds(half * state, state)] = w_bc[:, half, :].astype(BF16)
    w_dt = jnp.concatenate([R.w_dt[...].astype(F32), jnp.zeros((SLOTS - slot, rows), F32)], axis=0)
    R.wdt[at(SLOTS * p.b, SLOTS), lanes(rows * p.a, rows)] = w_dt.astype(BF16)
    R.wdt[BANDS * SLOTS :, :] = jnp.zeros((LANES - BANDS * SLOTS, width), BF16)


def layer(names, fused, head_dim, taps, *refs):
    R = types.SimpleNamespace(**dict(zip(names, refs)))
    alias(R, fused)
    inner = R.wx.shape[1]
    width = R.wx.shape[0]
    count = lax.axis_size("seq")
    place = lax.axis_index("seq")
    per_band = inner // head_dim // BANDS
    length = R.x.shape[0]
    first, last = place == 0, place == count - 1
    wires = Wires(R)

    if fused:
        p = Place()
        p.greet()
        order = [p.band(-k) for k in range(BANDS)]
        back = [(k, p.band(k)) for k in (*range(1, BANDS), 0)]
    else:
        order = list(range(BANDS))
        back = [(k, k) for k in range(BANDS)]
        barrier = pltpu.get_barrier_semaphore()

        @pl.when(jnp.logical_not(last))
        def _():
            pl.semaphore_signal(barrier, 1, device_id={"seq": place + 1}, device_id_type=pl.DeviceIdType.MESH)

        @pl.when(jnp.logical_not(first))
        def _():
            pl.semaphore_signal(barrier, 1, device_id={"seq": place - 1}, device_id_type=pl.DeviceIdType.MESH)

        pl.semaphore_wait(barrier, jnp.where(first | last, 1, 2))

    x_copy = wires.copy(R.x.at[pl.ds(length - HALO, HALO), :], R.x_halo, wires.new(), {"seq": place + 1})

    if fused:
        rows, cols = R.w_out.shape
        grid = Grid(lambda a, band: rows * a, lambda band: cols * band, rows // 2, rows // 6, cols)
        gx, gz, go = (
            Gather(wires, p, shard, whole, grid, R.local_sem.at[i])
            for i, (shard, whole) in enumerate(((R.w_zx.at[1], R.wx), (R.w_zx.at[0], R.wz), (R.w_out, R.wo)))
        )
        gx.start()
        own_params(R, p, taps, head_dim)
        dt_here = lambda k: R.wdt.at[at(SLOTS * p.band(-k), SLOTS), lanes(rows * p.a, rows)]
        par_here = lambda k: R.par.at[:, grid.cols(p.band(-k))]
        dt_z, par_z = ([wires.new() for _ in range(p.bands)] for _ in range(2))
        dt_x, bc_x, bc_c = wires.new(), wires.new(), wires.new()
        half = rows // 2
        bc_half = lambda a, c: R.wbc.at[at(rows * a + half * c, half), :]
        dt_col = lambda a: R.wdt.at[pl.ds(0, BANDS * SLOTS), lanes(rows * a, rows)]
        wires.start(bc_half(p.a, p.c), bc_half(p.a, p.c), bc_x, p.over_x)
        for k in range(1, p.bands):
            wires.start(dt_here(0), dt_here(0), dt_z[k], p.over_z(k))
            wires.start(par_here(0), par_here(0), par_z[k], p.over_z(k))

    @pl.when(jnp.logical_not(last))
    def _():
        x_copy.start()

    @pl.when(first)
    def _():
        R.x_halo[...] = jnp.zeros_like(R.x_halo)
        R.from_before[...] = jnp.zeros_like(R.from_before)

    @pl.when(last)
    def _():
        R.from_after[...] = jnp.zeros_like(R.from_after)
        R.dpre_halo[...] = jnp.zeros_like(R.dpre_halo)

    R.gain[...] = R.norm_gain[...].astype(F32).reshape(1, width)
    norm_rows(R)

    @pl.when(jnp.logical_not(first))
    def _():
        x_copy.wait_recv()

    norm_halo(R)
    if fused:
        for k in range(1, p.bands):
            wires.arrived(dt_here(k), dt_z[k], p.over_z(k))
        wires.start(dt_col(p.a), dt_col(p.a), dt_x, p.over_x)
        gx.over_y(0)
        gx.over_x(1)
        wires.arrived(bc_half(1 - p.a, p.c), bc_x, p.over_x)
        wires.start(bc_half(1 - p.a, p.c), bc_half(1 - p.a, p.c), bc_c, p.core)
        gx.over_x(2)
        gx.over_x(3)
        gz.start()
    head_spread(R, head_dim)
    if fused:
        gx.over_core(0)
        gx.over_y(1)
        for k in range(1, p.bands):
            wires.arrived(par_here(k), par_z[k], p.over_z(k))
        wires.arrived(bc_half(1 - p.a, 1 - p.c), bc_c, p.core)
        wires.arrived(dt_col(1 - p.a), dt_x, p.over_x)
    project_bc(R)
    convolve_bc(R, taps)
    if fused:
        gx.over_core(1)
        gx.over_y(2)
    step_sizes(R, per_band)

    early = place < count // 2
    forward = Chain(R, wires, R.from_before, place, count, 1)
    backward = Chain(R, wires, R.from_after, place, count, -1)
    for k, band in enumerate(order):
        if fused:
            gx.finish(k)
            if k + 2 < BANDS:
                gx.over_core(k + 2)
            if k + 3 < BANDS:
                gx.over_y(k + 3)
        project_x(R, band)
        convolve(R, taps, band)
        local_states(R, band)

        @pl.when(early)
        def _():
            forward.run(k, band)

        if fused:
            if k == 0:
                gz.each(gz.over_x)
                go.start()
            if k == 1:
                gz.each(gz.over_y)
            if k == 2:
                go.each(go.over_x)
                gz.each(gz.over_core)
            if k == 3:
                go.each(go.over_y)
        inside_forward(R, per_band, band)
    for k, band in enumerate(order):
        if fused:
            gz.finish(k)
        project_z(R, band)
    if fused:
        go.each(go.over_core)

    @pl.when(jnp.logical_not(early))
    def _():
        for k, band in enumerate(order):
            forward.run(k, band)

    for band in order:
        carried_forward(R, band)
    forward.sent(order)
    for k, band in enumerate(order):
        if fused:
            go.finish(k)
        hidden_grad(R, band)
    gate(R)
    for k, (_, band) in enumerate(back):
        local_adjoints(R, band)

        @pl.when(jnp.logical_not(early))
        def _():
            backward.run(k, band)

    grad_tiles(R.gT, R.hidden, R.go)
    if fused:
        grid = Grid(lambda a, band: rows * a, lambda band: cols * band, rows // 2, rows // 8, cols)
        bc_rows = rows // p.bands
        bc_grid = Grid(lambda a, band: rows * a + bc_rows * band, lambda band: 0, bc_rows // 2, 16, R.wbc.shape[1])
        spaces = lambda name: [getattr(R, f"{name}{i}") for i in range(6)]
        so, sz, sx = (
            Scatter(wires, p, grad, grid, spaces(name)) for grad, name in ((R.go, "so"), (R.gz, "sz"), (R.gx, "sx"))
        )
        sbc = Scatter(wires, p, R.gbc, bc_grid, spaces("sbc"))
        so.start_c()
    grad_tiles(R.xnT, R.dz, R.gz)
    if fused:
        sz.start_c()
        so.start_y()
    branch_out(R)
    backward_start(R)
    for k, (_, band) in enumerate(back):
        inside_backward(R, per_band, band)
        if fused:
            if k == 0:
                so.start_x()
            if k == 1:
                sz.start_y()
            if k == 2:
                so.start_z()
            if k == 3:
                sz.start_x()

    @pl.when(early)
    def _():
        for k, (_, band) in enumerate(back):
            backward.run(k, band)

    halo = Halo(R, wires, first, last, place)
    band_width = inner // BANDS

    def after_halo(k, band, copy):
        halo.arrived(copy)
        conv_backward(R, taps, band_width * band, band_width)
        R.gx[:, band_cols(R, band)] = dot(R.xnT[...], R.dconv[:, band_cols(R, band)]).astype(R.gx.dtype)
        if fused:
            sx.start_c([k])

    waiting = None
    for i, (k, band) in enumerate(back):
        carried_backward(R, band)
        now = (k, band, halo.send(band_cols(R, band)))
        if waiting is not None:
            after_halo(*waiting)
        waiting = now
        if fused:
            if i == 0:
                so.start_last()
                sz.start_z()
            if i == 1:
                so.start_share(R.oo)
            if i == 2:
                sx.start_y([back[0][0]])
                sz.start_last()
            if i == 3:
                sx.start_y([back[1][0]])
                sx.start_x([back[0][0]])
                sz.start_share(R.oz)
    backward.sent([band for _, band in back])
    step_grads(R)
    bc_copy = halo.send(pl.ds(inner, R.wbc.shape[1]))
    after_halo(*waiting)
    if fused:
        sx.start_y([back[2][0]])
        sx.start_x([back[1][0]])
        sx.start_z([back[0][0]])
    halo.arrived(bc_copy)
    conv_backward(R, taps, inner, R.wbc.shape[1])
    R.gbc[...] = dot(R.xnT[...], R.dconv[:, inner:]).astype(R.gbc.dtype)
    R.gdt[...] = dot(R.d_raw[...].T, R.xn[HALO:, :])[0 : R.gdt.shape[0], :].astype(R.gdt.dtype)
    if fused:
        sbc.start_c()
        dts = Exchange(wires, p, R.gdt, [R.dt_c, R.dt_y, R.dt_x])
        dts.start(0, p.core)
        sx.start_y([0])
        sx.start_x([back[2][0]])
        sx.start_z([back[1][0]])
        sbc.start_y()
        dts.add(0, p.core)
        dts.start(1, p.over_y)
    input_side(R)
    small_sums(R)
    if fused:
        vecs = Exchange(wires, p, R.vec, [R.vec_c, R.vec_y, R.vec_x])
        vecs.start(0, p.core)
        sx.start_x([0])
        sx.start_z([back[2][0]])
        sbc.start_x()
        vecs.add(0, p.core)
        vecs.start(1, p.over_y)
        dts.add(1, p.over_y)
        dt_cols = lambda a: R.gdt.at[:, lanes(rows * a, rows)]
        dts.start(2, p.over_x, dt_cols(1 - p.a))
        sx.start_z([0])
        sx.start_last()
        sbc.start_z()
        vecs.add(1, p.over_y)
        vecs.start(2, p.over_x)
        dts.add(2, p.over_x, dt_cols(p.a))
        dt_rows = lambda band: R.gdt.at[at(SLOTS * band, SLOTS), lanes(rows * p.a, rows)]
        dt_z, vec_z, bc_z, bc_c = ([wires.new() for _ in range(p.bands)] for _ in range(4))
        for k in range(1, p.bands):
            wires.start(dt_rows(p.band(k)), R.dt_zs.at[k], dt_z[k], p.over_z(k))
        sbc.start_last()
        sx.start_share(R.ox)
        vecs.add(2, p.over_x)
        R.vec_zs[p.b] = R.vec[...]
        for k in range(1, p.bands):
            wires.start(R.vec, R.vec_zs.at[p.b], vec_z[k], p.over_z(k))
        bc_out = lambda band, c: R.obc_low.at[at(bc_rows * band + bc_rows // 2 * c, bc_rows // 2), :]
        sbc.result(R.obc_low, bc_rows * p.b + bc_rows // 2 * p.c)
        for k in range(1, p.bands):
            wires.start(bc_out(p.b, p.c), bc_out(p.b, p.c), bc_z[k], p.over_z(k))
        total = dt_rows(p.b)[...].astype(F32)
        for k in range(1, p.bands):
            wires.arrived(R.dt_zs.at[k], dt_z[k], p.over_z(k))
            total = total + R.dt_zs[k].astype(F32)
        R.odt[...] = total
        wires.start(bc_out(p.b, p.c), bc_out(p.b, p.c), bc_c[0], p.core)
        for k in range(1, p.bands):
            spot = bc_out(p.band(-k), p.c)
            wires.arrived(spot, bc_z[k], p.over_z(k))
            wires.start(spot, spot, bc_c[k], p.core)
        for k in range(1, p.bands):
            wires.arrived(R.vec_zs.at[p.band(-k)], vec_z[k], p.over_z(k))
        total = R.vec_zs[0]
        for band in range(1, p.bands):
            total = total + R.vec_zs[band]
        R.ovec[...] = total
        R.oband[...] = R.ovec[:, grid.cols(p.b)]
        lane_rows = jnp.concatenate(
            [
                total[5:6, inner : inner + LANES],
                total[5:6, inner + LANES :],
                total[6:7, width : width + LANES],
                jnp.zeros((5, LANES), F32),
            ],
            axis=0,
        )
        R.oheads[...] = pltpu.roll(lane_rows, lax.rem(LANES - SLOTS * p.b, LANES), 1)
        for k in range(p.bands):
            wires.arrived(bc_out(p.band(-k), 1 - p.c), bc_c[k], p.core)
        R.obc[...] = R.obc_low[...].astype(F32)
        so.finish(R.oo)
        sz.finish(R.oz)
        sx.finish(R.ox)

    wires.drain()
    halo.sent()

    @pl.when(jnp.logical_not(last))
    def _():
        x_copy.wait_send()


def hand_out(taps, width, n_in, *refs):
    (layer_out, input_grad, oz, ox, oo, obc, odt, ovec, oband, oheads) = refs[:n_in]
    (
        layer_to, input_to, norm_gain, zx, bc, dt, x_kernel, x_offset, bc_kernel, bc_offset,
        dt_bias, a_log, d_skip, gate_gain, out_to, sems,
    ) = refs[n_in:]
    copies = [(layer_out, layer_to), (input_grad, input_to), (oo, out_to)]
    copies = [pltpu.make_async_copy(*pair, sems.at[i]) for i, pair in enumerate(copies)]
    for copy in copies:
        copy.start()
    state = bc.shape[2]
    inner = ovec.shape[1] - 2 * state
    zx[:, 0, :] = oz[...]
    zx[:, 1, :] = ox[...]
    for half in range(2):
        bc[:, half, :] = obc[:, half * state : (half + 1) * state]
        bc_kernel[:, half, :] = ovec[0:taps, inner + half * state : inner + (half + 1) * state]
        bc_offset[half : half + 1, :] = ovec[4:5, inner + half * state : inner + (half + 1) * state]
    dt[...] = odt[0 : dt.shape[0], :]
    norm_gain[...] = ovec[6, 0:width]
    x_kernel[...] = oband[0:taps, :]
    x_offset[...] = oband[4, :]
    gate_gain[...] = oband[5, :]
    for row, ref in enumerate((dt_bias, a_log, d_skip)):
        ref[...] = oheads[row, 0 : ref.shape[0]]
    for copy in copies:
        copy.wait()


def run_layer(fused, ins, head_dim, taps):
    length, width = ins["x"].shape
    inner, state2 = ins["inner"], ins["state2"]
    conv = inner + state2
    ins = {k: v for k, v in ins.items() if k not in ("inner", "state2")}
    per_band = inner // head_dim // BANDS
    chunks = length // Q
    weights = dict(
        wz=((width, inner), BF16),
        wx=((width, inner), BF16),
        wbc=((width, state2), BF16),
        wdt=((LANES, width), BF16),
        wo=((width, inner), BF16),
        par=((16, conv), F32),
    )
    grads = dict(
        gz=((width, inner), BF16),
        gx=((width, inner), BF16),
        go=((width, inner), BF16),
        gbc=((width, state2), BF16),
        gdt=((BANDS * SLOTS, width), BF16),
        vec=((8, conv), F32),
    )
    outs = dict(layer_out=((length, width), BF16), input_grad=((length, width), F32))
    scratch = dict(
        gain=((1, width), F32),
        ex=((LANES, inner), BF16),
        pick=((per_band * Q, LANES), BF16),
        xn=((HALO + length, width), BF16),
        xnT=((width, length), BF16),
        gT=((width, length), BF16),
        inv_rms=((length, 1), F32),
        x_halo=((HALO, width), BF16),
        ci=((HALO + length, conv), F32),
        cib=((length, conv), BF16),
        z=((length, inner), F32),
        xh=((length, inner), BF16),
        xt=((length, inner), BF16),
        bm=((length, LANES), BF16),
        cm=((length, LANES), BF16),
        prod=((length, Q), F32),
        prodT=((length, Q), F32),
        slope=((length, conv), BF16),
        rate=((1, LANES), F32),
        heads=((8, LANES), F32),
        dt=((length, LANES), F32),
        dt_sig=((length, LANES), F32),
        dt_low=((length, LANES), BF16),
        tail_low=((length, LANES), BF16),
        exp_low=((length, LANES), BF16),
        logs=((length, LANES), F32),
        logsT=((LANES, length), F32),
        ends=((8, LANES), F32),
        decx=((8, inner), F32),
        kept=((8, inner), F32),
        expx=((length, inner), BF16),
        states=((2 * chunks * LANES, inner), BF16),
        piece=((LANES, inner), F32),
        piece_decay=((1, inner), F32),
        outgoing=((LANES, inner), BF16),
        from_before=((LANES, inner), BF16),
        from_after=((LANES, inner), BF16),
        dh=((length, inner), BF16),
        gated=((length, inner), BF16),
        hidden=((length, inner), BF16),
        gain_acc=((8, inner), F32),
        skip_acc=((8, inner), F32),
        norm_acc=((8, width), F32),
        rate_acc=((8, LANES), F32),
        bias_acc=((8, LANES), F32),
        pulls=((length, LANES), F32),
        pullsT=((LANES, length), F32),
        d_prod=((length, Q), F32),
        d_log=((length, LANES), F32),
        d_tail=((length, LANES), F32),
        direct=((length, LANES), F32),
        db=((length, LANES), F32),
        dc=((length, LANES), F32),
        d_raw=((length, LANES), BF16),
        dpre_out=((HALO, conv), BF16),
        dpre_halo=((HALO, conv), BF16),
    )
    if fused:
        rows, cols = ins["w_out"].shape
        bands = inner // cols
        outs.update(
            oz=((rows, cols), F32),
            ox=((rows, cols), F32),
            oo=((rows, cols), F32),
            obc=((rows, state2), F32),
            odt=((SLOTS, rows), F32),
            ovec=((8, conv), F32),
            oband=((8, cols), F32),
            oheads=((8, LANES), F32),
        )
        scratch.update(weights)
        scratch.update({k: v for k, v in grads.items() if k != "gx"})
        main = Scatter.spaces(bands, Grid(None, None, rows // 2, rows // 8, cols))
        small = Scatter.spaces(bands, Grid(None, None, rows // bands // 2, 16, state2))
        for name, shapes in (("so", main), ("sz", main), ("sx", main), ("sbc", small)):
            scratch.update({f"{name}{i}": (shape, BF16) for i, shape in enumerate(shapes)})
        scratch.update(
            obc_low=((rows, state2), BF16),
            dt_c=((BANDS * SLOTS, width), BF16),
            dt_y=((BANDS * SLOTS, width), BF16),
            dt_x=((BANDS * SLOTS, rows), BF16),
            dt_zs=((bands, SLOTS, rows), BF16),
            vec_c=((8, conv), F32),
            vec_y=((8, conv), F32),
            vec_x=((8, conv), F32),
            vec_zs=((bands, 8, conv), F32),
        )
    else:
        outs.update(grads)
    names = (*ins, *outs, *scratch, "send_sem", "recv_sem", "local_sem")
    results = pl.pallas_call(
        functools.partial(layer, names, fused, head_dim, taps),
        out_shape=[jax.ShapeDtypeStruct(*v) for v in outs.values()],
        in_specs=[pl.BlockSpec(memory_space=pl.ANY if fused and name in ("w_zx", "w_out") else pltpu.VMEM) for name in ins],
        out_specs=[pl.BlockSpec(memory_space=pltpu.VMEM)] * len(outs),
        scratch_shapes=[pltpu.VMEM(*v) for v in scratch.values()]
        + [pltpu.SemaphoreType.DMA((SEMS,)), pltpu.SemaphoreType.DMA((SEMS,)), pltpu.SemaphoreType.DMA((8,))],
        compiler_params=pltpu.CompilerParams(
            collective_id=0, has_side_effects=True, vmem_limit_bytes=VMEM_BYTES
        ),
    )(*ins.values())
    return dict(zip(outs, results))


VMEM_BYTES = 64 * 2**20 - 2**18


def body(residual, cotangent, norm_gain, w_zx, w_bc, w_dt, x_kernel, x_offset, bc_kernel, bc_offset, dt_bias, a_log, d_skip, gate_gain, w_out):
    _, length, width = residual.shape
    bands = lax.axis_size("wb")
    rows_own, heads_own, inner_own, state = w_zx.shape[0], w_dt.shape[1], w_zx.shape[2], w_bc.shape[2]
    heads, inner = heads_own * bands, inner_own * bands
    head_dim = inner_own // heads_own
    taps = x_kernel.shape[0]
    fused = (lax.axis_size("seq"), lax.axis_size("wa"), bands) == (4, 2, BANDS) and inner_own % LANES == 0
    per = heads // BANDS
    ins = dict(
        x=residual.reshape(length, width),
        g=cotangent.reshape(length, width),
        norm_gain=norm_gain,
        inner=inner,
        state2=2 * state,
    )

    if fused:
        ins.update(
            w_zx=jnp.swapaxes(w_zx, 0, 1), w_out=w_out, w_bc=w_bc, w_dt=w_dt.T, x_kernel=x_kernel, x_offset=x_offset,
            bc_kernel=bc_kernel, bc_offset=bc_offset, dt_bias=dt_bias, a_log=a_log, d_skip=d_skip, gate_gain=gate_gain,
        )
        out = run_layer(True, ins, head_dim, taps)
        any_space, vmem = pl.BlockSpec(memory_space=pl.ANY), pl.BlockSpec(memory_space=pltpu.VMEM)
        shapes = [
            ((length, width), BF16), ((length, width), F32), ((width,), F32), (w_zx.shape, F32), (w_bc.shape, F32),
            (w_dt.shape[::-1], F32), (x_kernel.shape, F32), (x_offset.shape, F32), (bc_kernel.shape, F32),
            (bc_offset.shape, F32), (dt_bias.shape, F32), (a_log.shape, F32), (d_skip.shape, F32), (gate_gain.shape, F32),
            (w_out.shape, F32),
        ]
        results = pl.pallas_call(
            functools.partial(hand_out, taps, width, len(out)),
            out_shape=[jax.ShapeDtypeStruct(*shape) for shape in shapes],
            in_specs=[vmem] * len(out),
            out_specs=[any_space if i in (0, 1, 14) else vmem for i in range(15)],
            scratch_shapes=[pltpu.SemaphoreType.DMA((3,))],
        )(*out.values())
        results = list(results)
        results[0] = results[0].reshape(residual.shape)
        results[1] = results[1].reshape(residual.shape)
        results[5] = results[5].T
        return tuple(results)

    own = jnp.concatenate(
        [x_kernel.astype(F32), x_offset.astype(F32)[None], gate_gain.astype(F32)[None], jnp.repeat(d_skip, head_dim)[None]]
    )
    par_bc = jnp.concatenate([bc_kernel.reshape(taps, 2 * state), bc_offset.reshape(1, 2 * state)], axis=0).astype(F32)
    par_bc = jnp.pad(par_bc, ((0, 16 - taps - 1), (0, 0)))
    wzx = lax.all_gather(lax.all_gather(w_zx, "wa", axis=0, tiled=True), "wb", axis=2, tiled=True)
    wdt = lax.all_gather(lax.all_gather(w_dt, "wa", axis=0, tiled=True), "wb", axis=1, tiled=True)
    wdt = jnp.pad(wdt.T.reshape(BANDS, per, width), ((0, 0), (0, SLOTS - per), (0, 0))).reshape(-1, width)
    small = lax.all_gather(jnp.stack([dt_bias, a_log]), "wb", axis=1, tiled=True).reshape(2, BANDS, per)
    small = jnp.pad(small, ((0, 6), (0, 0), (0, inner // BANDS - per))).reshape(8, inner)
    wide = jnp.pad(lax.all_gather(own, "wb", axis=1, tiled=True), ((0, 1), (0, 0)))
    ins.update(
        wz=wzx[:, 0],
        wx=wzx[:, 1],
        wo=lax.all_gather(lax.all_gather(w_out, "wa", axis=0, tiled=True), "wb", axis=1, tiled=True),
        wbc=lax.all_gather(w_bc, "wa", axis=0, tiled=True).reshape(width, 2 * state),
        wdt=jnp.pad(wdt, ((0, LANES - BANDS * SLOTS), (0, 0))),
        par=jnp.concatenate([jnp.concatenate([wide, small], axis=0), par_bc], axis=1),
    )
    out = run_layer(False, ins, head_dim, taps)

    def share(grad, columns=True):
        grad = lax.psum_scatter(grad.astype(F32), "wa", scatter_dimension=0, tiled=True)
        if columns:
            grad = lax.psum_scatter(grad, "wb", scatter_dimension=grad.ndim - 1, tiled=True)
        else:
            grad = lax.psum(grad, "wb")
        return lax.psum(grad, "seq")

    gdt = out["gdt"].reshape(BANDS, SLOTS, width)[:, :per].reshape(heads, width)
    vec = lax.psum(out["vec"], ("seq", "wa", "wb"))
    mine = lax.axis_index("wb")
    band = lax.dynamic_slice_in_dim(vec[:, :inner], mine * inner_own, inner_own, 1)
    by_head = jnp.stack([vec[5, inner : inner + LANES], vec[5, inner + LANES :], vec[6, width : width + LANES]])
    by_head = by_head[:, : BANDS * SLOTS].reshape(3, BANDS, SLOTS)[:, :, :per].reshape(3, heads)
    by_head = lax.dynamic_slice_in_dim(by_head, mine * heads_own, heads_own, 1)
    return (
        out["layer_out"].reshape(residual.shape),
        out["input_grad"].reshape(residual.shape),
        vec[6, :width],
        share(jnp.stack([out["gz"], out["gx"]], axis=1)),
        share(out["gbc"], False).reshape(-1, 2, state),
        share(gdt.T),
        band[0:taps],
        band[4],
        vec[0:taps, inner:].reshape(taps, 2, state),
        vec[4, inner:].reshape(2, state),
        by_head[0],
        by_head[1],
        by_head[2],
        band[5],
        share(out["go"]),
    )


def solution(mesh):
    batch = P(("wa", "wb"), "seq", None)
    ins = (
        batch, batch, P(), P("wa", None, "wb"), P("wa", None, None), P("wa", "wb"), P(None, "wb"), P("wb"), P(), P(),
        P("wb"), P("wb"), P("wb"), P("wb"), P("wa", "wb"),
    )
    outs = (
        batch, batch, P(), P("wa", None, "wb"), P("wa", None, None), P("wa", "wb"), P(None, "wb"), P("wb"), P(), P(),
        P("wb"), P("wb"), P("wb"), P("wb"), P("wa", "wb"),
    )
    return jax.shard_map(body, mesh=mesh, in_specs=ins, out_specs=outs, check_vma=False)
```

```python
import functools
import types

import jax
import jax.numpy as jnp
from jax import lax
from jax.experimental import pallas as pl
from jax.experimental.pallas import tpu as pltpu
from jax.sharding import PartitionSpec as P

F32, BF16 = jnp.float32, jnp.bfloat16
EPSILON = 1e-05
Q = 128
LANES = 128
HALO = 16
SLOTS = 16
TILE = 256
BANDS = 4
NT = (((1,), (1,)), ((), ()))


def dot(a, b):
    return jnp.dot(a, b, preferred_element_type=F32)


def dot_nt(a, b):
    return lax.dot_general(a, b, NT, preferred_element_type=F32)


def dot_exact(a, b):
    return jnp.dot(a, b, precision=lax.Precision.HIGHEST, preferred_element_type=F32)


def sigmoid(v):
    return 0.5 + 0.5 * jnp.tanh(0.5 * v)


def fold8(v):
    return v.reshape(v.shape[0] // 8, 8, v.shape[1]).sum(axis=0)


def at(start, size):
    return pl.ds(pl.multiple_of(start, 16), size)


def lanes(start, size):
    return pl.ds(pl.multiple_of(start, LANES), size)


def rows_at(i, size=Q, base=0):
    return at(i * size + base, size)


def cols_at(i, size=LANES):
    return lanes(i * size, size)


def band_cols(R, band):
    width = R.wx.shape[1] // BANDS
    return lanes(width * band, width)


class Columns:
    def __init__(self, R, bands):
        self.parts = [band_cols(R, band) for band in bands]
        self.width = R.wx.shape[1] // BANDS

    def get(self, ref, rows=slice(None)):
        return jnp.concatenate([ref[rows, cols] for cols in self.parts], axis=1)

    def put(self, ref, rows, value):
        for n, cols in enumerate(self.parts):
            ref[rows, cols] = value[:, n * self.width : (n + 1) * self.width]


def head_spread(R, head_dim):
    inner = R.ex.shape[1]
    per_band = inner // BANDS
    row = lax.broadcasted_iota(jnp.int32, (LANES, LANES), 0)

    @pl.loop(0, inner // LANES)
    def _(c):
        lane = lax.broadcasted_iota(jnp.int32, (LANES, LANES), 1) + c * LANES
        hit = jnp.zeros((LANES, LANES), jnp.bool_)
        for band in range(BANDS):
            first = lane - band * per_band
            inside = (first >= 0) & (first < per_band)
            head = lax.shift_right_arithmetic(first, head_dim.bit_length() - 1)
            hit = hit | (inside & (row == band * SLOTS + head))
        R.ex[:, cols_at(c)] = jnp.where(hit, 1.0, 0.0).astype(BF16)

    lane = lax.broadcasted_iota(jnp.int32, (Q, LANES), 1)
    for head in range(R.pick.shape[0] // Q):
        R.pick[pl.ds(head * Q, Q), :] = jnp.where(lane == head, 1.0, 0.0).astype(BF16)


def norm_rows(R):
    gain = R.gain[...]

    @pl.loop(0, R.x.shape[0] // Q)
    def _(i):
        rows = R.x[rows_at(i), :].astype(F32)
        inv = lax.rsqrt(jnp.mean(rows * rows, axis=-1, keepdims=True) + EPSILON)
        value = (rows * inv * gain).astype(BF16)
        R.xn[rows_at(i, base=HALO), :] = value
        R.inv_rms[rows_at(i), :] = inv
        R.xnT[:, cols_at(i)] = value.T
        R.gT[:, cols_at(i)] = R.g[rows_at(i), :].T


def norm_halo(R):
    rows = R.x_halo[...].astype(F32)
    inv = lax.rsqrt(jnp.mean(rows * rows, axis=-1, keepdims=True) + EPSILON)
    R.xn[0:HALO, :] = (rows * inv * R.gain[...]).astype(BF16)


def project(R, left, right, out, band):
    cols = band_cols(R, band)
    out[:, cols] = dot(left[...], right[:, cols]).astype(out.dtype)


def grad_of(left, right, out):
    for j in range(out.shape[1] // (2 * TILE)):
        cols = pl.ds(j * 2 * TILE, 2 * TILE)
        out[:, cols] = dot(left[...], right[:, cols]).astype(out.dtype)


def project_bc(R):
    R.ci[:, R.wx.shape[1] :] = dot(R.xn[...], R.wbc[...])


def conv_tile(R, taps, cols, put):
    for i in range(R.x.shape[0] // Q):
        rows = pl.ds(i * Q, Q)
        pre = R.par[4:5, cols]
        for k in range(taps):
            conv_in = R.ci[pl.ds(HALO - (taps - 1) + k + i * Q, Q), cols]
            pre = pre + R.par[k : k + 1, cols] * conv_in
        R.cib[rows, cols] = conv_in.astype(BF16)
        sig = sigmoid(pre)
        act = pre * sig
        put(rows, act.astype(BF16))
        R.slope[rows, cols] = (sig + act * (1.0 - sig)).astype(BF16)


def convolve(R, taps, band):
    width = R.wx.shape[1] // BANDS
    for c in range(width // LANES):
        cols = lanes(width * band + c * LANES, LANES)

        def put(rows, act):
            R.xh[rows, cols] = act

        conv_tile(R, taps, cols, put)
    for i in range(R.x.shape[0] // Q):
        rows, cols = pl.ds(i * Q, Q), band_cols(R, band)
        dt = dot(R.dt_low[rows, :], R.ex[:, cols])
        R.xt[rows, cols] = (R.xh[rows, cols].astype(F32) * dt).astype(BF16)


def convolve_bc(R, taps):
    inner = R.wx.shape[1]

    def put_b(rows, act):
        R.bm[rows, :] = act

    def put_c(rows, act):
        R.cm[rows, :] = act

    conv_tile(R, taps, pl.ds(inner, LANES), put_b)
    conv_tile(R, taps, pl.ds(inner + LANES, LANES), put_c)

    for i in range(R.x.shape[0] // Q):
        rows = pl.ds(i * Q, Q)
        R.prod[rows, :] = dot_nt(R.cm[rows, :], R.bm[rows, :])
        R.prodT[rows, :] = dot_nt(R.bm[rows, :], R.cm[rows, :])


def lower_ones(strict=False):
    row = lax.broadcasted_iota(jnp.int32, (Q, Q), 0)
    col = lax.broadcasted_iota(jnp.int32, (Q, Q), 1)
    return jnp.where(row > col if strict else row >= col, 1.0, 0.0).astype(F32)


def step_sizes(R, per_band):
    cols = R.wx.shape[1] // BANDS
    lane = lax.broadcasted_iota(jnp.int32, (8, LANES), 1)
    heads = jnp.zeros((8, LANES), F32)
    for band in range(BANDS):
        block = R.par[8:16, pl.ds(band * cols, LANES)]
        heads = heads + pltpu.roll(jnp.where(lane < per_band, block, 0.0), band * SLOTS, 1)
    R.heads[...] = heads
    R.rate[...] = -jnp.exp(R.heads[1:2, :])
    bias, rate = R.heads[0:1, :], R.rate[...]
    ones = lower_ones()
    chunks = R.x.shape[0] // Q
    R.ends[...] = jnp.zeros_like(R.ends)
    for i in range(chunks):
        rows = pl.ds(i * Q, Q)
        v = dot_nt(R.xn[pl.ds(HALO + i * Q, Q), :], R.wdt[...]) + bias
        dt = jnp.maximum(v, 0.0) + jnp.log1p(jnp.exp(-jnp.abs(v)))
        R.dt[rows, :] = dt
        R.dt_sig[rows, :] = jax.nn.sigmoid(v)
        logs = dot_exact(ones, dt * rate)
        R.logs[rows, :] = logs
        R.logsT[:, rows] = logs.T
        last = logs[Q - 1 : Q, :]
        R.ends[i : i + 1, :] = last
        R.dt_low[rows, :] = dt.astype(BF16)
        R.tail_low[rows, :] = jnp.exp(last - logs).astype(BF16)
        R.exp_low[rows, :] = jnp.exp(logs).astype(BF16)
    decay = jnp.exp(R.ends[...])
    high = decay.astype(BF16)
    low = (decay - high.astype(F32)).astype(BF16)
    R.decx[...] = dot(high, R.ex[...]) + dot(low, R.ex[...])


def local_states(R, bands):
    chunks = R.x.shape[0] // Q
    columns = Columns(R, bands)
    get, put = columns.get, columns.put
    spread = get(R.ex)
    total = decay = None
    for i in range(chunks):
        rows = pl.ds(i * Q, Q)
        ended = get(R.xt, rows).astype(F32) * dot(R.tail_low[rows, :], spread)
        fresh = dot(R.bm[rows, :].T, ended.astype(BF16))
        put(R.sl, rows_at(i, LANES), fresh.astype(BF16))
        step = get(R.decx, slice(i, i + 1))
        total = fresh if total is None else total * step + fresh
        decay = step if decay is None else decay * step
    put(R.piece, slice(None), total)
    put(R.piece_decay, slice(None), decay)


def halves(value):
    first = lax.broadcasted_iota(jnp.int32, value.shape, 1) < LANES // 2
    zero = jnp.zeros_like(value)
    return jnp.concatenate([jnp.where(first, value, zero), jnp.where(first, zero, value)], axis=0)


def causal_mask(by_row):
    row = lax.broadcasted_iota(jnp.int32, (Q, Q), 0)
    col = lax.broadcasted_iota(jnp.int32, (Q, Q), 1)
    return row >= col if by_row else row <= col


def band_logs(R, rows, band):
    return pltpu.roll(R.logs[rows, :], lax.rem(LANES - SLOTS * band, LANES), 1)


def inside_forward(R, per_band, band):
    width = R.wx.shape[1] // BANDS
    causal = causal_mask(True)
    for i in range(R.x.shape[0] // Q):
        rows = pl.ds(i * Q, Q)
        logs = band_logs(R, rows, band)
        logsT = R.logsT[at(SLOTS * band, 8), rows]
        for pair in range(per_band // 2):
            cols = lanes(width * band + pair * LANES, LANES)
            mixes = []
            for head in (2 * pair, 2 * pair + 1):
                gap = logs[:, head : head + 1] - logsT[head : head + 1, :]
                decay = jnp.exp(jnp.where(causal, gap, -1e30))
                mixes.append((R.prod[rows, :] * decay).astype(BF16))
            R.y[rows, cols] = dot(jnp.concatenate(mixes, axis=1), halves(R.xt[rows, cols]))


def carried_forward(R):
    chunks = R.x.shape[0] // Q
    state = R.from_before[...].astype(F32)
    for i in range(chunks):
        rows = pl.ds(i * Q, Q)
        block = rows_at(i, LANES)
        low = state.astype(BF16)
        R.s_in[block, :] = low
        spread = dot(R.exp_low[rows, :], R.ex[...])
        R.expx[rows, :] = spread.astype(BF16)
        R.y[rows, :] += dot(R.cm[rows, :], low) * spread
        if i < chunks - 1:
            state = state * R.decx[i : i + 1, :] + R.sl[block, :].astype(F32)


def gate_forward(R):
    inner = R.wx.shape[1]
    block = 64

    @pl.loop(0, R.x.shape[0] // block)
    def _(i):
        rows = rows_at(i, block)
        squares = jnp.zeros((block, LANES), F32)
        for c in range(inner // LANES):
            cols = pl.ds(c * LANES, LANES)
            y = R.y[rows, cols] + R.par[6:7, cols] * R.xh[rows, cols].astype(F32)
            R.y[rows, cols] = y
            z = R.z[rows, cols]
            gated = (y * (z * sigmoid(z))).astype(BF16)
            R.gated[rows, cols] = gated
            gated = gated.astype(F32)
            squares = squares + gated * gated
        inv = lax.rsqrt(jnp.sum(squares, axis=-1, keepdims=True) / inner + EPSILON)
        R.inv_gate[rows, :] = inv
        inv = jnp.broadcast_to(inv, (block, LANES))
        for c in range(inner // LANES):
            cols = pl.ds(c * LANES, LANES)
            R.hidden[rows, cols] = (R.gated[rows, cols].astype(F32) * inv * R.par[5:6, cols]).astype(BF16)


def gate_backward(R, part, parts):
    inner = R.wx.shape[1]
    block = 64
    count = R.x.shape[0] // block // parts
    if part == 0:
        R.gain_acc[...] = jnp.zeros_like(R.gain_acc)
        R.skip_acc[...] = jnp.zeros_like(R.skip_acc)

    @pl.loop(part * count, (part + 1) * count)
    def _(i):
        rows = rows_at(i, block)
        cross = jnp.zeros((block, LANES), F32)
        for c in range(inner // LANES):
            cols = pl.ds(c * LANES, LANES)
            cross = cross + R.gated[rows, cols].astype(F32) * (R.dh[rows, cols].astype(F32) * R.par[5:6, cols])
        inv = R.inv_gate[rows, :]
        cross = jnp.sum(cross, axis=-1, keepdims=True) * (inv * inv * inv / inner)
        inv = jnp.broadcast_to(inv, (block, LANES))
        cross = jnp.broadcast_to(cross, (block, LANES))
        for c in range(inner // LANES):
            cols = pl.ds(c * LANES, LANES)
            gated = R.gated[rows, cols].astype(F32)
            dh = R.dh[rows, cols].astype(F32) * inv
            R.gain_acc[:, cols] += fold8(dh * gated)
            d_gated = dh * R.par[5:6, cols] - gated * cross
            z = R.z[rows, cols]
            sig = sigmoid(z)
            lin = z * sig
            dy = d_gated * lin
            R.dz[rows, cols] = (d_gated * R.y[rows, cols] * (sig + lin * (1.0 - sig))).astype(BF16)
            R.dyl[rows, cols] = (dy * R.expx[rows, cols].astype(F32)).astype(BF16)
            R.dy[rows, cols] = dy.astype(BF16)
            R.skip_acc[:, cols] += fold8(dy * R.xh[rows, cols].astype(F32))


def branch_out(R):
    width = R.x.shape[1]
    for j in range(width // TILE):
        cols = pl.ds(j * TILE, TILE)
        R.layer_out[:, cols] = (
            R.x[:, cols].astype(F32) + dot_nt(R.hidden[...], R.wo[cols, :])
        ).astype(BF16)


def local_adjoints(R):
    chunks = R.x.shape[0] // Q
    total = None
    for i in range(chunks - 1, -1, -1):
        pulled = dot(R.cm[pl.ds(i * Q, Q), :].T, R.dyl[pl.ds(i * Q, Q), :])
        R.dl[rows_at(i, LANES), :] = pulled.astype(BF16)
        total = pulled if total is None else total * R.decx[i : i + 1, :] + pulled
    R.piece[...] = total


def inside_backward(R, per_band, band):
    width = R.wx.shape[1] // BANDS
    causal = causal_mask(False)
    for i in range(R.x.shape[0] // Q):
        rows = pl.ds(i * Q, Q)
        logs = band_logs(R, rows, band)
        logsT = R.logsT[at(SLOTS * band, 8), rows]
        d_prod = R.d_prod[rows, :]
        pulls, sums = [], []
        for pair in range(per_band // 2):
            cols = lanes(width * band + pair * LANES, LANES)
            dy = R.dy[rows, cols]
            d_both = dot_nt(halves(R.xt[rows, cols]), dy)
            mixes = []
            for half in range(2):
                head = 2 * pair + half
                gap = logsT[head : head + 1, :] - logs[:, head : head + 1]
                decay = jnp.exp(jnp.where(causal, gap, -1e30))
                mix = R.prodT[rows, :] * decay
                mixes.append(mix.astype(BF16))
                d_mix = d_both[half * Q : (half + 1) * Q, :]
                d_prod = d_prod + decay * d_mix
                pull = (mix * d_mix).astype(BF16)
                pulls.append(pull)
                sums.append(jnp.sum(pull.astype(F32), axis=0, keepdims=True))
            R.u[rows, cols] = dot(jnp.concatenate(mixes, axis=1), halves(dy))
        R.d_prod[rows, :] = d_prod
        R.pullsT[at(SLOTS * band, 8), rows] = jnp.concatenate([*sums, jnp.zeros((8 - per_band, Q), F32)], axis=0)
        R.pulls[rows, :] += pltpu.roll(dot(jnp.concatenate(pulls, axis=1), R.pick[...]), SLOTS * band, 1)


def backward_start(R):
    for ref in (R.pulls, R.pullsT, R.d_prod, R.d_tail, R.db, R.dc, R.d_log, R.direct):
        ref[...] = jnp.zeros_like(ref)


def carried_backward(R, i, bands):
    columns = Columns(R, bands)
    get, put = columns.get, columns.put
    spread = get(R.ex)
    grad = get(R.from_after).astype(F32) if i == R.x.shape[0] // Q - 1 else get(R.piece)
    rows = pl.ds(i * Q, Q)
    block = rows_at(i, LANES)

    def add(ref, value):
        ref[rows, :] += value

    low = grad.astype(BF16)
    tail = dot(R.tail_low[rows, :], spread)
    xt = get(R.xt, rows).astype(F32)
    pulled = dot(R.bm[rows, :], low) * tail
    u = get(R.u, rows) + pulled
    add(R.d_tail, dot_nt((xt * pulled).astype(BF16), spread))
    add(R.db, dot_nt((xt * tail).astype(BF16), low))
    state = get(R.s_in, block)
    dyl = get(R.dyl, rows)
    add(R.dc, dot_nt(dyl, state))
    add(R.d_log, dot_nt((dyl.astype(F32) * dot(R.cm[rows, :], state)).astype(BF16), spread))
    decay = get(R.decx, slice(i, i + 1))
    put(R.kept, slice(i, i + 1), jnp.sum(grad * state.astype(F32), axis=0, keepdims=True) * decay)
    if i:
        put(R.piece, slice(None), grad * decay + get(R.dl, block).astype(F32))
    add(R.direct, dot_nt((get(R.xh, rows).astype(F32) * u).astype(BF16), spread))
    dx = dot(R.dt_low[rows, :], spread) * u + get(R.par, slice(6, 7)) * get(R.dy, rows).astype(F32)
    put(R.dpre, rows, dx * get(R.slope, rows).astype(F32))


def step_grads(R):
    chunks = R.x.shape[0] // Q
    inner = R.wx.shape[1]
    later = lower_ones().T
    before = lower_ones(strict=True)
    high = R.kept[...].astype(BF16)
    low = (R.kept[...] - high.astype(F32)).astype(BF16)
    kept = dot_nt(high, R.ex[...]) + dot_nt(low, R.ex[...])
    rate_acc = jnp.zeros((8, LANES), F32)
    bias_acc = jnp.zeros((8, LANES), F32)
    for i in range(chunks):
        rows = pl.ds(i * Q, Q)
        sides = R.d_log[rows, :] + R.pullsT[:, rows].T - R.pulls[rows, :]
        d_decay = dot_exact(later, sides) + dot_exact(before, R.d_tail[rows, :]) + kept[i : i + 1, :]
        d_raw = (R.direct[rows, :] + R.rate[...] * d_decay) * R.dt_sig[rows, :]
        rate_acc = rate_acc + fold8(R.dt[rows, :] * d_decay)
        bias_acc = bias_acc + fold8(d_raw)
        R.d_raw[rows, :] = d_raw.astype(BF16)
        d_prod = R.d_prod[rows, :].astype(BF16)
        db = R.db[rows, :] + dot(d_prod, R.cm[rows, :])
        dc = R.dc[rows, :] + dot(d_prod.T, R.bm[rows, :])
        R.dpre[rows, inner : inner + LANES] = db * R.slope[rows, inner : inner + LANES].astype(F32)
        R.dpre[rows, inner + LANES :] = dc * R.slope[rows, inner + LANES :].astype(F32)
    R.rate_acc[...] = rate_acc
    R.bias_acc[...] = bias_acc


def conv_backward(R, taps, first, width):
    length = R.x.shape[0]
    halo = lanes(first, width)
    R.dpre[pl.ds(length, HALO), halo] = R.dpre_halo[:, halo].astype(F32)

    @pl.loop(0, width // LANES)
    def _(c):
        cols = lanes(first + c * LANES, LANES)
        sums = [jnp.zeros((8, LANES), F32) for _ in range(taps + 1)]
        for i in range(length // Q):
            base = i * Q
            conv_in = R.cib[pl.ds(base, Q), cols].astype(F32)
            d_conv = None
            for k in range(taps):
                ahead = R.dpre[pl.ds(base + taps - 1 - k, Q), cols]
                sums[k] = sums[k] + fold8(ahead * conv_in)
                term = R.par[k : k + 1, cols] * ahead
                d_conv = term if d_conv is None else d_conv + term
            sums[taps] = sums[taps] + fold8(ahead)
            R.dconv[pl.ds(base, Q), cols] = d_conv.astype(BF16)
        for k in range(taps + 1):
            R.vec[k : k + 1, cols] = jnp.sum(sums[k], axis=0, keepdims=True)


def input_first(R):
    for j in range(R.x.shape[1] // TILE):
        cols = pl.ds(j * TILE, TILE)
        R.input_grad[:, cols] = dot_nt(R.dz[...], R.wz[cols, :])


def input_second(R):
    inner = R.wx.shape[1]
    for j in range(R.x.shape[1] // TILE):
        cols = pl.ds(j * TILE, TILE)
        R.input_grad[:, cols] += (
            dot_nt(R.dconv[:, 0:inner], R.wx[cols, :])
            + dot_nt(R.dconv[:, inner:], R.wbc[cols, :])
            + dot(R.d_raw[...], R.wdt[:, cols])
        )


def input_last(R):
    width = R.x.shape[1]
    gain = R.gain[...]
    R.norm_acc[...] = jnp.zeros_like(R.norm_acc)

    @pl.loop(0, R.x.shape[0] // 64)
    def _(i):
        rows = rows_at(i, 64)
        d_normed = R.input_grad[rows, :]
        x = R.x[rows, :].astype(F32)
        inv = R.inv_rms[rows, :]
        pulled = d_normed * x
        R.norm_acc[...] += fold8(pulled * inv)
        middle = jnp.sum(pulled * gain, axis=-1, keepdims=True) * (inv * inv * inv / width)
        R.input_grad[rows, :] = R.g[rows, :].astype(F32) + (d_normed * gain) * inv - x * middle


def small_sums(R):
    inner = R.wx.shape[1]
    width = R.gain.shape[1]
    R.vec[5:8, :] = jnp.zeros((3, R.vec.shape[1]), F32)
    R.vec[5:6, 0:inner] = jnp.sum(R.gain_acc[...], axis=0, keepdims=True)
    R.vec[6:7, 0:width] = jnp.sum(R.norm_acc[...], axis=0, keepdims=True)
    R.vec[5:6, inner : inner + LANES] = jnp.sum(R.bias_acc[...], axis=0, keepdims=True)
    R.vec[5:6, inner + LANES :] = jnp.sum(R.rate_acc[...], axis=0, keepdims=True) * R.rate[...]
    skip = R.skip_acc[...]
    high = skip.astype(BF16)
    low = (skip - high.astype(F32)).astype(BF16)
    R.vec[6:7, width : width + LANES] = jnp.sum(
        dot_nt(high, R.ex[...]) + dot_nt(low, R.ex[...]), axis=0, keepdims=True
    )


SEMS = 256
WINDOW = {"x": 3, "y": 4, "z": 2}


class Wires:
    def __init__(self, R):
        self.R, self.used, self.started = R, 0, []
        self.leaving = {link: [] for link in WINDOW}

    def new(self):
        self.used += 1
        return self.used - 1

    def copy(self, src, dst, sem, where):
        return pltpu.make_async_remote_copy(
            src_ref=src,
            dst_ref=dst,
            send_sem=self.R.send_sem.at[sem],
            recv_sem=self.R.recv_sem.at[sem],
            device_id=where,
            device_id_type=pl.DeviceIdType.MESH,
        )

    def start(self, src, dst, sem, where, link=None):
        copy = self.copy(src, dst, sem, where)
        if link is None:
            self.started.append(copy)
        else:
            leaving = self.leaving[link]
            if len(leaving) == WINDOW[link]:
                leaving.pop(0).wait_send()
            leaving.append(copy)
        copy.start()

    def arrived(self, dst, sem, where):
        self.copy(dst, dst, sem, where).wait_recv()

    def drain(self):
        for copy in sum(self.leaving.values(), self.started):
            copy.wait_send()


class Place:
    def __init__(self):
        self.seq, self.a, self.b = lax.axis_index("seq"), lax.axis_index("wa"), lax.axis_index("wb")
        self.bands, self.rows = lax.axis_size("wb"), lax.axis_size("wa")
        self.c = lax.rem(self.seq, 2)
        self.y = lax.div(self.seq, 2)
        self.core = {"seq": self.seq + 1 - 2 * self.c}
        self.over_y = {"seq": lax.rem(self.seq + 2, 4)}
        self.over_x = {"wa": 1 - self.a}

    def band(self, k):
        return lax.rem(self.b + k + self.bands, self.bands)

    def over_z(self, k):
        return {"wb": self.band(k)}

    def greet(self):
        barrier = pltpu.get_barrier_semaphore()
        peers = [{"seq": lax.rem(self.seq + k, 4)} for k in range(1, 4)]
        peers += [self.over_z(k) for k in range(1, self.bands)] + [self.over_x]
        for peer in peers:
            pl.semaphore_signal(barrier, 1, device_id=peer, device_id_type=pl.DeviceIdType.MESH)
        return lambda: pl.semaphore_wait(barrier, len(peers))


class Grid:
    def __init__(self, row, col, half, own, width):
        self.row, self.col, self.half, self.own, self.width = row, col, half, own, width
        self.span = half - own

    def cols(self, band):
        return lanes(self.col(band), self.width)

    def half_rows(self, a, band, c):
        return at(self.row(a, band) + self.half * c, self.half)

    def span_rows(self, a, band, p):
        return at(self.row(a, band) + self.half * p.c + self.own * p.y, self.span)

    def own_rows(self, a, band, p, y):
        return at(self.row(a, band) + self.half * p.c + (self.half - self.own) * y, self.own)


class Gather:
    def __init__(self, wires, p, whole, grid):
        self.w, self.p, self.whole, self.g = wires, p, whole, grid
        self.z = [wires.new() for _ in range(p.bands)]
        self.x = [wires.new() for _ in range(p.bands)]
        self.y = [[wires.new() for _ in range(p.bands)] for _ in range(2)]
        self.c = [[wires.new() for _ in range(p.bands)] for _ in range(2)]

    def here(self, rows, k):
        return self.whole.at[rows, self.g.cols(self.p.band(-k))]

    def start(self):
        mine = self.here(self.g.span_rows(self.p.a, self.p.b, self.p), 0)
        self.w.start(mine, mine, self.x[0], self.p.over_x, "x")

    def start_z(self, k):
        mine = self.here(self.g.span_rows(self.p.a, self.p.b, self.p), 0)
        self.w.start(mine, mine, self.z[k], self.p.over_z(k), "z")

    def over_x(self, k):
        if k == 0:
            return
        p, g = self.p, self.g
        rows = g.span_rows(p.a, p.b, p)
        self.w.arrived(self.here(rows, k), self.z[k], p.over_z(k))
        self.w.start(self.here(rows, k), self.here(rows, k), self.x[k], p.over_x, "x")
        mine = self.here(g.own_rows(p.a, p.b, p, p.y), k)
        self.w.start(mine, mine, self.y[0][k], p.over_y, "y")

    def over_y(self, k):
        p, g = self.p, self.g
        self.w.arrived(self.here(g.span_rows(1 - p.a, p.b, p), k), self.x[k], p.over_x)
        mine = self.here(g.own_rows(1 - p.a, p.b, p, p.y), k)
        self.w.start(mine, mine, self.y[1][k], p.over_y, "y")

    def sides(self, k):
        return [(0, self.p.a), (1, 1 - self.p.a)] if k else [(1, 1 - self.p.a)]

    def over_core(self, k):
        p, g = self.p, self.g
        for side, a in self.sides(k):
            self.w.arrived(self.here(g.own_rows(a, p.b, p, 1 - p.y), k), self.y[side][k], p.over_y)
            mine = self.here(g.half_rows(a, p.b, p.c), k)
            self.w.start(mine, mine, self.c[side][k], p.core)

    def finish(self, k):
        p, g = self.p, self.g
        for side, a in self.sides(k):
            self.w.arrived(self.here(g.half_rows(a, p.b, 1 - p.c), k), self.c[side][k], p.core)

class Scatter:
    def __init__(self, wires, p, grad, grid, spaces, large):
        self.w, self.p, self.grad, self.g = wires, p, grad, grid
        self.links = ("y", "x", "z") if large else (None,) * 3
        self.rc, self.ry, self.rx, self.rz, self.mine, self.peer = spaces
        self.order = [*range(1, p.bands), 0]
        self.c = [[wires.new() for _ in range(p.bands)] for _ in range(2)]
        self.y = [[wires.new() for _ in range(p.bands)] for _ in range(2)]
        self.x = [wires.new() for _ in range(p.bands)]
        self.z = [wires.new() for _ in range(p.bands)]
        self.last, self.share = wires.new(), wires.new()

    @staticmethod
    def spaces(bands, grid):
        half, own, span, width = grid.half, grid.own, grid.span, grid.width
        return [
            (2, bands, half, width),
            (2, bands, own, width),
            (bands, span, width),
            (bands, span, width),
            (span, width),
            (span, width),
        ]

    def here(self, rows, k):
        return self.grad.at[rows, self.g.cols(self.p.band(k))]

    def add(self, rows, k, part):
        spot = self.here(rows, k)
        spot[...] = (spot[...].astype(F32) + part.astype(F32)).astype(BF16)

    def start_c(self, ks=None):
        p, g = self.p, self.g
        for k in self.order if ks is None else ks:
            for a in range(2):
                rows = g.half_rows(a, p.band(k), 1 - p.c)
                self.w.start(self.here(rows, k), self.rc.at[a, k], self.c[a][k], p.core)

    def start_y(self, ks=None):
        p, g = self.p, self.g
        for k in self.order if ks is None else ks:
            for a in range(2):
                self.w.arrived(self.rc.at[a, k], self.c[a][k], p.core)
                self.add(g.half_rows(a, p.band(k), p.c), k, self.rc[a, k])
                rows = g.own_rows(a, p.band(k), p, 1 - p.y)
                self.w.start(self.here(rows, k), self.ry.at[a, k], self.y[a][k], p.over_y, self.links[0])

    def start_x(self, ks=None):
        p, g = self.p, self.g
        for k in self.order if ks is None else ks:
            for a in range(2):
                self.w.arrived(self.ry.at[a, k], self.y[a][k], p.over_y)
                self.add(g.own_rows(a, p.band(k), p, p.y), k, self.ry[a, k])
            rows = g.span_rows(1 - p.a, p.band(k), p)
            self.w.start(self.here(rows, k), self.rx.at[k], self.x[k], p.over_x, self.links[1])

    def start_z(self, ks=None):
        p, g = self.p, self.g
        for k in self.order if ks is None else ks:
            rows = g.span_rows(p.a, p.band(k), p)
            self.w.arrived(self.rx.at[k], self.x[k], p.over_x)
            self.add(rows, k, self.rx[k])
            if k:
                self.w.start(self.here(rows, k), self.rz.at[k], self.z[k], p.over_z(k), self.links[2])

    def start_last(self):
        p, g = self.p, self.g
        total = self.here(g.span_rows(p.a, p.b, p), 0)[...].astype(F32)
        for k in range(1, p.bands):
            self.w.arrived(self.rz.at[k], self.z[k], p.over_z(k))
            total = total + self.rz[k].astype(F32)
        self.mine[...] = total.astype(BF16)
        self.w.start(self.mine, self.peer, self.last, p.over_y, self.links[0])

    def result(self, out, first):
        p, g = self.p, self.g
        self.w.arrived(self.peer, self.last, p.over_y)
        both = g.span - g.own
        middle = self.mine[at(g.own * (1 - p.y), both), :].astype(F32) + self.peer[at(g.own * p.y, both), :].astype(F32)
        out[at(first + g.own, both), :] = middle.astype(out.dtype)
        far = (g.half - g.own) * p.y
        out[at(first + far, g.own), :] = self.mine[at(both * p.y, g.own), :].astype(out.dtype)
        far = (g.half - g.own) * (1 - p.y)
        out[at(first + far, g.own), :] = self.peer[at(both * (1 - p.y), g.own), :].astype(out.dtype)

    def start_share(self, out):
        p, g = self.p, self.g
        self.result(out, g.half * p.c)
        mine = out.at[at(g.half * p.c, g.half), :]
        self.w.start(mine, mine, self.share, p.core)

    def finish(self, out):
        p, g = self.p, self.g
        self.w.arrived(out.at[at(g.half * (1 - p.c), g.half), :], self.share, p.core)


class Exchange:
    def __init__(self, wires, p, value, spaces):
        self.w, self.p, self.value, self.spaces = wires, p, value, spaces
        self.sems = [wires.new() for _ in range(3)]

    def start(self, step, where, src=None):
        self.w.start(self.value if src is None else src, self.spaces[step], self.sems[step], where)
        self.sent = self.w.started.pop()

    def add(self, step, where, spot=None):
        self.w.arrived(self.spaces[step], self.sems[step], where)
        self.sent.wait_send()
        spot = self.value if spot is None else spot
        total = spot[...].astype(F32) + self.spaces[step][...].astype(F32)
        spot[...] = total.astype(spot.dtype)


class Chain:
    def __init__(self, R, wires, landing, place, count, step):
        self.R, self.w, self.landing, self.step, self.place = R, wires, landing, step, place
        self.has_from = place > 0 if step > 0 else place < count - 1
        self.has_to = place < count - 1 if step > 0 else place > 0
        self.sems = [wires.new() for _ in range(BANDS)]

    def copy(self, k, band):
        cols = band_cols(self.R, band)
        where = {"seq": self.place + self.step}
        return cols, self.w.copy(self.R.outgoing.at[:, cols], self.landing.at[:, cols], self.sems[k], where)

    def run(self, k, band):
        R = self.R
        cols, copy = self.copy(k, band)

        @pl.when(self.has_from)
        def _():
            copy.wait_recv()

        @pl.when(self.has_to)
        def _():
            incoming = self.landing[:, cols].astype(F32)
            R.outgoing[:, cols] = (R.piece[:, cols] + R.piece_decay[:, cols] * incoming).astype(BF16)
            copy.start()

    def sent(self, bands):
        @pl.when(self.has_to)
        def _():
            for k, band in enumerate(bands):
                self.copy(k, band)[1].wait_send()


def alias(R, fused):
    half = R.states.shape[0] // 2
    R.sl, R.s_in = R.states.at[0:half, :], R.states.at[half : 2 * half, :]
    R.dl, R.u, R.dyl, R.dconv, R.dpre, R.dz, R.dy = R.sl, R.z, R.gated, R.slope, R.ci, R.dh, R.expx
    R.y = R.dpre.at[0 : R.x.shape[0], 0 : R.wx.shape[1]]
    R.layer_out = R.xn.at[HALO:, :]
    R.input_grad = R.u.at[:, 0 : R.x.shape[1]]
    if fused:
        R.gx = R.states.at[0 : R.wx.shape[0], :]


def own_params(R, p, taps, head_dim):
    cols, width = R.x_kernel.shape[1], R.x.shape[1]
    inner, state = R.wx.shape[1], R.bc_kernel.shape[2]
    row = lambda ref: ref[...].astype(F32).reshape(1, ref.shape[0])
    lane = lax.broadcasted_iota(jnp.int32, (1, cols), 1)
    skip = jnp.zeros((1, cols), F32)
    heads = R.d_skip.shape[0]
    for head in range(heads):
        hit = lax.shift_right_arithmetic(lane, head_dim.bit_length() - 1) == head
        skip = jnp.where(hit, row(R.d_skip)[:, head : head + 1], skip)
    pad = jnp.zeros((1, cols - heads), F32)
    block = [R.x_kernel[...].astype(F32), row(R.x_offset), row(R.gate_gain), skip, jnp.zeros((1, cols), F32)]
    block += [jnp.concatenate([row(ref), pad], axis=1) for ref in (R.dt_bias, R.a_log)]
    R.par[:, lanes(cols * p.b, cols)] = jnp.concatenate([*block, jnp.zeros((6, cols), F32)], axis=0)
    kernel, offset = R.bc_kernel[...].astype(F32), R.bc_offset[...].astype(F32)
    for half in range(2):
        rows = [kernel[:, half, :], offset[half : half + 1, :], jnp.zeros((16 - taps - 1, state), F32)]
        R.par[:, pl.ds(inner + half * state, state)] = jnp.concatenate(rows, axis=0)
    rows, slot = R.w_bc.shape[0], R.w_dt.shape[0]
    block = 64

    @pl.loop(0, rows // block)
    def _(i):
        here = at(rows * p.a + i * block, block)
        w_zx = R.w_zx[pl.ds(i * block, block)].astype(F32)
        for half, whole in enumerate((R.wz, R.wx)):
            whole[here, lanes(cols * p.b, cols)] = w_zx[:, half, :].astype(BF16)
        w_bc = R.w_bc[pl.ds(i * block, block)].astype(F32)
        for half in range(2):
            R.wbc[here, pl.ds(half * state, state)] = w_bc[:, half, :].astype(BF16)

    w_dt = jnp.concatenate([R.w_dt[...].astype(F32), jnp.zeros((SLOTS - slot, rows), F32)], axis=0)
    R.wdt[at(SLOTS * p.b, SLOTS), lanes(rows * p.a, rows)] = w_dt.astype(BF16)
    R.wdt[BANDS * SLOTS :, :] = jnp.zeros((LANES - BANDS * SLOTS, width), BF16)


class Steps:
    def __init__(self, ops):
        self.ops = ops

    def __getattr__(self, name):
        def run(*which):
            step = self.ops.pop(" ".join(map(str, (name, *which))), None)
            if step is not None:
                step()

        return run


def layer(names, fused, head_dim, taps, *refs):
    R = types.SimpleNamespace(**dict(zip(names, refs)))
    alias(R, fused)
    inner = R.wx.shape[1]
    width = R.wx.shape[0]
    count = lax.axis_size("seq")
    place = lax.axis_index("seq")
    per_band = inner // head_dim // BANDS
    length = R.x.shape[0]
    first, last = place == 0, place == count - 1
    early = place < count // 2
    wires = Wires(R)
    ops = {}

    def op(name):
        return lambda run: ops.__setitem__(name, run)

    if fused:
        p = Place()
        greeted = p.greet()
        order = [p.band(-k) for k in range(BANDS)]
        back = [(k, p.band(k)) for k in (*range(1, BANDS), 0)]
        rows, cols = R.w_out.shape
        own_out = R.wo.at[at(rows * p.a, rows), lanes(cols * p.b, cols)]
        loads = [(R.x_in, R.x), (R.g_in, R.g), (R.w_out, own_out)]
    else:
        loads = [(R.x_in, R.x), (R.g_in, R.g)]
        order = list(range(BANDS))
        back = [(k, k) for k in range(BANDS)]
        barrier = pltpu.get_barrier_semaphore()

        @pl.when(jnp.logical_not(last))
        def _():
            pl.semaphore_signal(barrier, 1, device_id={"seq": place + 1}, device_id_type=pl.DeviceIdType.MESH)

        @pl.when(jnp.logical_not(first))
        def _():
            pl.semaphore_signal(barrier, 1, device_id={"seq": place - 1}, device_id_type=pl.DeviceIdType.MESH)

        greeted = lambda: pl.semaphore_wait(barrier, jnp.where(first | last, 1, 2))

    @pl.when(first)
    def _():
        R.x_halo[...] = jnp.zeros_like(R.x_halo)
        R.from_before[...] = jnp.zeros_like(R.from_before)

    @pl.when(last)
    def _():
        R.from_after[...] = jnp.zeros_like(R.from_after)
        R.dpre_halo[...] = jnp.zeros_like(R.dpre_halo)

    loads = [pltpu.make_async_copy(*pair, R.local_sem.at[i]) for i, pair in enumerate(loads)]
    for load in loads:
        load.start()
    if fused:
        own_params(R, p, taps, head_dim)
    R.gain[...] = R.norm_gain[...].astype(F32).reshape(1, width)
    for load in loads:
        load.wait()
    norm_rows(R)
    greeted()

    x_copy = wires.copy(R.x.at[pl.ds(length - HALO, HALO), :], R.x_halo, wires.new(), {"seq": place + 1})
    band_width = inner // BANDS
    groups = [[band for _, band in back[: BANDS // 2]], [band for _, band in back[BANDS // 2 :]]]
    pre_parts = [[(band_width * band, band_width) for band in bands] for bands in groups]
    pre_parts[1].append((inner, R.wbc.shape[1]))
    pre_copies = [
        [
            wires.copy(R.dpre_out.at[:, lanes(*part)], R.dpre_halo.at[:, lanes(*part)], wires.new(), {"seq": place - 1})
            for part in parts
        ]
        for parts in pre_parts
    ]
    forward = Chain(R, wires, R.from_before, place, count, 1)
    backward = Chain(R, wires, R.from_after, place, count, -1)
    layer_copy = pltpu.make_async_copy(R.layer_out, R.layer_to, R.local_sem.at[3])
    input_copy = pltpu.make_async_copy(R.input_grad, R.input_to, R.local_sem.at[4])

    @pl.when(jnp.logical_not(last))
    def _():
        x_copy.start()

    if fused:
        half = rows // 2
        grid = Grid(lambda a, band: rows * a, lambda band: cols * band, half, rows // 6, cols)
        gathers = {
            name: Gather(wires, p, whole, grid) for name, whole in (("x", R.wx), ("z", R.wz), ("o", R.wo))
        }
        dt_here = lambda k: R.wdt.at[at(SLOTS * p.band(-k), SLOTS), lanes(rows * p.a, rows)]
        par_here = lambda k: R.par.at[:, grid.cols(p.band(-k))]
        bc_half = lambda a, c: R.wbc.at[at(rows * a + half * c, half), :]
        dt_col = lambda a: R.wdt.at[pl.ds(0, BANDS * SLOTS), lanes(rows * a, rows)]
        dt_z, par_z = ([wires.new() for _ in range(p.bands)] for _ in range(2))
        dt_x, bc_x, bc_c = wires.new(), wires.new(), wires.new()
        for k in range(1, p.bands):
            wires.start(dt_here(0), dt_here(0), dt_z[k], p.over_z(k))
            wires.start(par_here(0), par_here(0), par_z[k], p.over_z(k))
        wires.start(bc_half(p.a, p.c), bc_half(p.a, p.c), bc_x, p.over_x)
        gathers["x"].start()

        for name, weight in gathers.items():
            if name != "x":
                op(f"GX0 {name} 0")(weight.start)
            for k in range(p.bands):
                if k:
                    op(f"GZ {name} {k}")(functools.partial(weight.start_z, k))
                    op(f"X {name} {k}")(functools.partial(weight.over_x, k))
                op(f"Y {name} {k}")(functools.partial(weight.over_y, k))
                op(f"C {name} {k}")(functools.partial(weight.over_core, k))

        @op("dt1")
        def _():
            for k in range(1, p.bands):
                wires.arrived(dt_here(k), dt_z[k], p.over_z(k))
            wires.start(dt_col(p.a), dt_col(p.a), dt_x, p.over_x)

        @op("bc1")
        def _():
            wires.arrived(bc_half(1 - p.a, p.c), bc_x, p.over_x)
            wires.start(bc_half(1 - p.a, p.c), bc_half(1 - p.a, p.c), bc_c, p.core)

        @op("small")
        def _():
            for k in range(1, p.bands):
                wires.arrived(par_here(k), par_z[k], p.over_z(k))

    def arrived(name, k):
        if fused:
            gathers[name].finish(k)


    op("spread")(lambda: head_spread(R, head_dim))

    @op("halo")
    def _():
        @pl.when(jnp.logical_not(first))
        def _():
            x_copy.wait_recv()

        norm_halo(R)

    @op("bc")
    def _():
        if fused:
            wires.arrived(bc_half(1 - p.a, 1 - p.c), bc_c, p.core)
        project_bc(R)
        convolve_bc(R, taps)

    @op("steps")
    def _():
        if fused:
            wires.arrived(dt_col(1 - p.a), dt_x, p.over_x)
        step_sizes(R, per_band)

    def inner_x(k, band):
        arrived("x", k)
        project(R, R.xn, R.wx, R.ci, band)
        convolve(R, taps, band)

    def inner_z(k, band):
        arrived("z", k)
        project(R, R.xn.at[HALO:, :], R.wz, R.z, band)

    def back_out(k, band):
        arrived("o", k)
        project(R, R.g, R.wo, R.dh, band)

    for k, band in enumerate(order):
        op(f"px {k}")(functools.partial(inner_x, k, band))
        op(f"inside {k}")(functools.partial(inside_forward, R, per_band, band))
        op(f"pz {k}")(functools.partial(inner_z, k, band))
        op(f"dh {k}")(functools.partial(back_out, k, band))

    def states_of(ks):
        local_states(R, [order[k] for k in ks])

        @pl.when(early)
        def _():
            for k in ks:
                forward.run(k, order[k])

    op("ls 0")(lambda: states_of(range(BANDS // 2)))
    op("ls 1")(lambda: states_of(range(BANDS // 2, BANDS)))

    @op("cf")
    def _():
        @pl.when(jnp.logical_not(early))
        def _():
            for k, band in enumerate(order):
                forward.run(k, band)

        carried_forward(R)
        forward.sent(order)

    op("gf")(lambda: gate_forward(R))

    @op("bo")
    def _():
        branch_out(R)
        layer_copy.start()


    scatters = {}

    def gradient(name, left, right, out):
        grad_of(left, right, out)
        if fused:
            scatters[name].start_c()

    op("go")(lambda: gradient("go", R.gT, R.hidden, R.go))
    op("gz")(lambda: gradient("gz", R.xnT, R.dz, R.gz))
    op("gb 0")(lambda: gate_backward(R, 0, 2))
    op("gb 1")(lambda: gate_backward(R, 1, 2))

    @op("adj")
    def _():
        backward_start(R)
        local_adjoints(R)

        @pl.when(jnp.logical_not(early))
        def _():
            for k, (_, band) in enumerate(back):
                backward.run(k, band)

    for k, (_, band) in enumerate(back):
        op(f"ib {k}")(functools.partial(inside_backward, R, per_band, band))

    @op("chain")
    def _():
        @pl.when(early)
        def _():
            for k, (_, band) in enumerate(back):
                backward.run(k, band)

    for which, name in enumerate(("cbA", "cbB")):
        for i in range(length // Q):
            op(f"{name} {i}")(functools.partial(carried_backward, R, i, groups[which]))

    def send_halo(which):
        for part, copy in zip(pre_parts[which], pre_copies[which]):
            R.dpre_out[:, lanes(*part)] = R.dpre[0:HALO, lanes(*part)].astype(BF16)

            @pl.when(jnp.logical_not(first))
            def _():
                copy.start()

    def back_through_conv(which):
        for part, copy in zip(pre_parts[which], pre_copies[which]):

            @pl.when(jnp.logical_not(last))
            def _():
                copy.wait_recv()

            conv_backward(R, taps, *part)

    def inner_gradient(which):
        for k, band in back[: BANDS // 2] if which == 0 else back[BANDS // 2 :]:
            project(R, R.xnT, R.dconv, R.gx, band)
            if fused:
                scatters["gx"].start_c([k])

    @op("sg")
    def _():
        backward.sent([band for _, band in back])
        step_grads(R)
        send_halo(1)

    op("hA")(lambda: send_halo(0))
    op("cvA")(lambda: back_through_conv(0))
    op("cv")(lambda: back_through_conv(1))
    op("gxA")(lambda: inner_gradient(0))
    op("gx")(lambda: inner_gradient(1))

    @op("gbd")
    def _():
        R.gbc[...] = dot(R.xnT[...], R.dconv[:, inner:]).astype(R.gbc.dtype)
        R.gdt[...] = dot_nt(R.d_raw[...].T, R.xnT[...])[0 : R.gdt.shape[0], :].astype(R.gdt.dtype)
        if fused:
            scatters["bc"].start_c()
            dts.start(0, p.core)

    op("i1")(lambda: input_first(R))
    op("i2")(lambda: input_second(R))

    @op("i3")
    def _():
        input_last(R)
        input_copy.start()

    @op("ss")
    def _():
        small_sums(R)
        if fused:
            vecs.start(0, p.core, vec_half(1 - p.c))

    if fused:
        grid = Grid(lambda a, band: rows * a, lambda band: cols * band, half, rows // 8, cols)
        bc_rows = rows // p.bands
        bc_grid = Grid(lambda a, band: rows * a + bc_rows * band, lambda band: 0, bc_rows // 2, 16, R.wbc.shape[1])
        for name, grad, where, space in (
            ("go", R.go, grid, "so"), ("gz", R.gz, grid, "sz"), ("gx", R.gx, grid, "sx"), ("bc", R.gbc, bc_grid, "sbc"),
        ):
            scatters[name] = Scatter(wires, p, grad, where, [getattr(R, f"{space}{i}") for i in range(6)], name != "bc")
        for name, out in (("go", R.oo), ("gz", R.oz), ("gx", R.ox)):
            scatter = scatters[name]
            for k in range(p.bands):
                op(f"sY {name} {k}")(functools.partial(scatter.start_y, [k]))
                op(f"sX {name} {k}")(functools.partial(scatter.start_x, [k]))
                op(f"sZ {name} {k}")(functools.partial(scatter.start_z, [k]))
            op(f"sL {name}")(scatter.start_last)
            op(f"sS {name}")(functools.partial(scatter.start_share, out))
            op(f"sE {name}")(functools.partial(scatter.finish, out))

        dts = Exchange(wires, p, R.gdt, [R.dt_c, R.dt_y, R.dt_x])
        vecs = Exchange(wires, p, R.vec, [R.vec_c, R.vec_y, R.vec_x])
        dtg_z, vec_z, bcg_z, bcg_c = ([wires.new() for _ in range(p.bands)] for _ in range(4))
        vec_lanes = lambda c: lanes(R.vec.shape[1] // 2 * c, R.vec.shape[1] // 2)
        vec_half = lambda c: R.vec.at[:, vec_lanes(c)]
        vec_s = wires.new()
        dt_cols = lambda a: R.gdt.at[:, lanes(rows * a, rows)]
        dt_rows = lambda band: R.gdt.at[at(SLOTS * band, SLOTS), lanes(rows * p.a, rows)]
        bc_out = lambda band, c: R.obc.at[at(bc_rows * band + bc_rows // 2 * c, bc_rows // 2), :]

        op("bY")(lambda: scatters["bc"].start_y())
        op("bX")(lambda: scatters["bc"].start_x())
        op("bZ")(lambda: scatters["bc"].start_z())
        op("bL")(lambda: scatters["bc"].start_last())

        @op("bG")
        def _():
            scatters["bc"].result(R.obc, bc_rows * p.b + bc_rows // 2 * p.c)
            for k in range(1, p.bands):
                wires.start(bc_out(p.b, p.c), bc_out(p.b, p.c), bcg_z[k], p.over_z(k))
            wires.start(bc_out(p.b, p.c), bc_out(p.b, p.c), bcg_c[0], p.core)

        @op("bS")
        def _():
            for k in range(1, p.bands):
                spot = bc_out(p.band(-k), p.c)
                wires.arrived(spot, bcg_z[k], p.over_z(k))
                wires.start(spot, spot, bcg_c[k], p.core)

        @op("bE")
        def _():
            for k in range(p.bands):
                wires.arrived(bc_out(p.band(-k), 1 - p.c), bcg_c[k], p.core)

        @op("dY")
        def _():
            dts.add(0, p.core)
            dts.start(1, p.over_y)

        @op("dX")
        def _():
            dts.add(1, p.over_y)
            dts.start(2, p.over_x, dt_cols(1 - p.a))

        @op("dZ")
        def _():
            dts.add(2, p.over_x, dt_cols(p.a))
            for k in range(1, p.bands):
                wires.start(dt_rows(p.band(k)), R.dt_zs.at[k], dtg_z[k], p.over_z(k))

        @op("dE")
        def _():
            total = dt_rows(p.b)[...].astype(F32)
            for k in range(1, p.bands):
                wires.arrived(R.dt_zs.at[k], dtg_z[k], p.over_z(k))
                total = total + R.dt_zs[k].astype(F32)
            R.odt[...] = total

        @op("vY")
        def _():
            vecs.add(0, p.core, vec_half(p.c))
            vecs.start(1, p.over_y, vec_half(p.c))

        @op("vX")
        def _():
            vecs.add(1, p.over_y, vec_half(p.c))
            vecs.start(2, p.over_x, vec_half(p.c))

        @op("vZ")
        def _():
            vecs.add(2, p.over_x, vec_half(p.c))
            R.vec_zs[p.b] = R.vec[:, vec_lanes(p.c)]
            for k in range(1, p.bands):
                wires.start(vec_half(p.c), R.vec_zs.at[p.b], vec_z[k], p.over_z(k))

        @op("vS")
        def _():
            for k in range(1, p.bands):
                wires.arrived(R.vec_zs.at[p.band(-k)], vec_z[k], p.over_z(k))
            total = R.vec_zs[0]
            for band in range(1, p.bands):
                total = total + R.vec_zs[band]
            mine = R.ovec.at[:, vec_lanes(p.c)]
            mine[...] = total
            wires.start(mine, mine, vec_s, p.core)

        @op("vE")
        def _():
            wires.arrived(R.ovec.at[:, vec_lanes(1 - p.c)], vec_s, p.core)
            R.oband[...] = R.ovec[:, grid.cols(p.b)]
            by_lane = [R.ovec[5:6, inner : inner + LANES], R.ovec[5:6, inner + LANES :], R.ovec[6:7, width : width + LANES]]
            by_lane = jnp.concatenate([*by_lane, jnp.zeros((5, LANES), F32)], axis=0)
            R.oheads[...] = pltpu.roll(by_lane, lax.rem(LANES - SLOTS * p.b, LANES), 1)

    do = Steps(ops)
    wx, wz, wo, go, gz, gx = "x", "z", "o", "go", "gz", "gx"
    do.spread(); do.GZ(wx, 1); do.dt1(); do.small(); do.GZ(wx, 2); do.X(wx, 1); do.halo(); do.GZ(wx, 3)
    do.Y(wx, 0); do.bc1(); do.X(wx, 2); do.bc(); do.Y(wx, 1); do.GZ(wz, 1); do.C(wx, 0); do.X(wx, 3)
    do.steps(); do.Y(wx, 2); do.GZ(wz, 2); do.GX0(wz, 0); do.px(0); do.Y(wx, 3); do.C(wx, 1); do.inside(0)
    do.X(wz, 1); do.GZ(wz, 3); do.C(wx, 2); do.px(1); do.Y(wz, 0); do.X(wz, 2); do.C(wx, 3); do.ls(0)
    do.px(2); do.Y(wz, 1); do.GZ(wo, 1); do.X(wz, 3); do.px(3); do.ls(1); do.GX0(wo, 0); do.Y(wz, 2)
    do.GZ(wo, 2); do.inside(2); do.C(wz, 0); do.Y(wz, 3); do.X(wo, 1); do.GZ(wo, 3); do.C(wz, 1); do.inside(1)
    do.pz(0); do.C(wz, 2); do.inside(3); do.X(wo, 2); do.Y(wo, 0); do.pz(1); do.pz(2); do.C(wz, 3)
    do.Y(wo, 1); do.cf(); do.X(wo, 3); do.pz(3); do.gf(); do.C(wo, 0); do.Y(wo, 2); do.C(wo, 1); do.go()
    do.Y(wo, 3); do.dh(1); do.dh(0); do.C(wo, 2); do.C(wo, 3); do.sY(go, 2); do.dh(2); do.sY(go, 0)
    do.sY(go, 1); do.dh(3); do.gb(0); do.gb(1); do.sX(go, 2); do.gz(); do.adj(); do.sX(go, 1); do.sY(go, 3)
    do.ib(1); do.ib(3); do.sY(gz, 3); do.sX(go, 0); do.ib(2); do.sY(gz, 0); do.ib(0); do.sY(gz, 1)
    do.sX(go, 3); do.sZ(go, 2); do.sY(gz, 2); do.bo(); do.chain(); do.cbA(3); do.cbA(2); do.sX(gz, 0)
    do.cbA(1); do.cbA(0); do.hA(); do.sZ(go, 3); do.cbB(3); do.sX(gz, 2); do.cbB(2); do.cbB(1); do.sZ(go, 1)
    do.cvA(); do.gxA(); do.cbB(0); do.sX(gz, 3); do.sg(); do.sZ(go, 0); do.sY(gx, 1); do.sX(gz, 1)
    do.sZ(gz, 2); do.sZ(gz, 0); do.sY(gx, 2); do.i1(); do.cv(); do.sL(go); do.gbd(); do.gx(); do.sZ(gz, 3)
    do.sX(gx, 1); do.dY(); do.bY(); do.i2(); do.sY(gx, 3); do.sS(go); do.sZ(gz, 1); do.sX(gx, 2); do.i3()
    do.ss(); do.sY(gx, 0); do.bX(); do.sZ(gx, 1); do.vY(); do.sX(gx, 3); do.sZ(gx, 2); do.bZ(); do.sX(gx, 0)
    do.dX(); do.vX(); do.sL(gz); do.sZ(gx, 3); do.bL(); do.vZ(); do.sZ(gx, 0); do.dZ(); do.sL(gx); do.bG()
    do.sS(gz); do.dE(); do.vS(); do.sE(go); do.vE(); do.bS(); do.sS(gx); do.bE(); do.sE(gz); do.sE(gx)
    assert not ops, sorted(ops)

    layer_copy.wait()
    input_copy.wait()
    wires.drain()

    @pl.when(jnp.logical_not(last))
    def _():
        x_copy.wait_send()

    @pl.when(jnp.logical_not(first))
    def _():
        for copy in sum(pre_copies, []):
            copy.wait_send()


def hand_out(taps, names, *refs):
    count = len(names)
    came, refs = refs[:count], refs[count:]
    (
        layer_to, input_to, norm_gain, zx, bc, dt, x_kernel, x_offset, bc_kernel, bc_offset,
        dt_bias, a_log, d_skip, gate_gain, out_to,
    ) = refs[:15]
    here, (zx_via, out_via, bc_via, in_sem, out_sem) = refs[15 : 15 + count], refs[15 + count :]
    R = types.SimpleNamespace(**dict(zip(names, here)))
    loads = {name: pltpu.make_async_copy(a, b, in_sem.at[i]) for i, (name, a, b) in enumerate(zip(names, came, here))}
    stores = [
        pltpu.make_async_copy(*pair, out_sem.at[i])
        for i, pair in enumerate(((zx_via, zx), (out_via, out_to), (R.input_to, input_to), (R.layer_to, layer_to), (bc_via, bc)))
    ]
    first = ("oz", "ox", "oo", "input_to", "layer_to")
    for name in (*first, *(name for name in names if name not in first)):
        loads[name].start()
    loads["oz"].wait()
    zx_via[:, 0, :] = R.oz[...].astype(F32)
    loads["ox"].wait()
    zx_via[:, 1, :] = R.ox[...].astype(F32)
    stores[0].start()
    loads["oo"].wait()
    out_via[...] = R.oo[...].astype(F32)
    stores[1].start()
    for name, store in (("input_to", stores[2]), ("layer_to", stores[3])):
        loads[name].wait()
        store.start()
    for name in names:
        if name not in first:
            loads[name].wait()
    state = bc.shape[2]
    inner, width = R.ovec.shape[1] - 2 * state, R.layer_to.shape[1]
    for half in range(2):
        cols = pl.ds(half * state, state)
        bc_via[:, half, :] = R.obc[:, cols].astype(F32)
        cols = pl.ds(inner + half * state, state)
        bc_kernel[:, half, :] = R.ovec[0:taps, cols]
        bc_offset[half : half + 1, :] = R.ovec[4:5, cols]
    stores[4].start()
    dt[...] = R.odt[0 : dt.shape[0], :]
    norm_gain[...] = R.ovec[6, 0:width]
    x_kernel[...] = R.oband[0:taps, :]
    x_offset[...] = R.oband[4, :]
    gate_gain[...] = R.oband[5, :]
    for row, ref in enumerate((dt_bias, a_log, d_skip)):
        ref[...] = R.oheads[row, 0 : ref.shape[0]]
    for store in stores:
        store.wait()


def run_layer(fused, ins, head_dim, taps):
    length, width = ins["x_in"].shape
    inner, state2 = ins["inner"], ins["state2"]
    conv = inner + state2
    ins = {k: v for k, v in ins.items() if k not in ("inner", "state2")}
    per_band = inner // head_dim // BANDS
    chunks = length // Q
    weights = dict(
        wz=((width, inner), BF16),
        wx=((width, inner), BF16),
        wbc=((width, state2), BF16),
        wdt=((LANES, width), BF16),
        wo=((width, inner), BF16),
        par=((16, conv), F32),
    )
    grads = dict(
        gz=((width, inner), BF16),
        gx=((width, inner), BF16),
        go=((width, inner), BF16),
        gbc=((width, state2), BF16),
        gdt=((BANDS * SLOTS, width), BF16),
        vec=((8, conv), F32),
    )
    outs = dict(layer_to=((length, width), BF16), input_to=((length, width), F32))
    scratch = dict(
        x=((length, width), BF16),
        g=((length, width), BF16),
        gain=((1, width), F32),
        ex=((LANES, inner), BF16),
        pick=((per_band * Q, LANES), BF16),
        xn=((HALO + length, width), BF16),
        xnT=((width, length), BF16),
        gT=((width, length), BF16),
        inv_rms=((length, 1), F32),
        inv_gate=((length, 1), F32),
        x_halo=((HALO, width), BF16),
        ci=((HALO + length, conv), F32),
        cib=((length, conv), BF16),
        z=((length, inner), F32),
        xh=((length, inner), BF16),
        xt=((length, inner), BF16),
        bm=((length, LANES), BF16),
        cm=((length, LANES), BF16),
        prod=((length, Q), F32),
        prodT=((length, Q), F32),
        slope=((length, conv), BF16),
        rate=((1, LANES), F32),
        heads=((8, LANES), F32),
        dt=((length, LANES), F32),
        dt_sig=((length, LANES), F32),
        dt_low=((length, LANES), BF16),
        tail_low=((length, LANES), BF16),
        exp_low=((length, LANES), BF16),
        logs=((length, LANES), F32),
        logsT=((LANES, length), F32),
        ends=((8, LANES), F32),
        decx=((8, inner), F32),
        kept=((8, inner), F32),
        expx=((length, inner), BF16),
        states=((2 * chunks * LANES, inner), BF16),
        piece=((LANES, inner), F32),
        piece_decay=((1, inner), F32),
        outgoing=((LANES, inner), BF16),
        from_before=((LANES, inner), BF16),
        from_after=((LANES, inner), BF16),
        dh=((length, inner), BF16),
        gated=((length, inner), BF16),
        hidden=((length, inner), BF16),
        gain_acc=((8, inner), F32),
        skip_acc=((8, inner), F32),
        norm_acc=((8, width), F32),
        rate_acc=((8, LANES), F32),
        bias_acc=((8, LANES), F32),
        pulls=((length, LANES), F32),
        pullsT=((LANES, length), F32),
        d_prod=((length, Q), F32),
        d_log=((length, LANES), F32),
        d_tail=((length, LANES), F32),
        direct=((length, LANES), F32),
        db=((length, LANES), F32),
        dc=((length, LANES), F32),
        d_raw=((length, LANES), BF16),
        dpre_out=((HALO, conv), BF16),
        dpre_halo=((HALO, conv), BF16),
    )
    if fused:
        rows, cols = ins["w_out"].shape
        bands = inner // cols
        outs.update(
            oz=((rows, cols), BF16),
            ox=((rows, cols), BF16),
            oo=((rows, cols), BF16),
            obc=((rows, state2), BF16),
            odt=((SLOTS, rows), F32),
            ovec=((8, conv), F32),
            oband=((8, cols), F32),
            oheads=((8, LANES), F32),
        )
        scratch.update(weights)
        scratch.update({k: v for k, v in grads.items() if k != "gx"})
        main = Scatter.spaces(bands, Grid(None, None, rows // 2, rows // 8, cols))
        small = Scatter.spaces(bands, Grid(None, None, rows // bands // 2, 16, state2))
        for name, shapes in (("so", main), ("sz", main), ("sx", main), ("sbc", small)):
            scratch.update({f"{name}{i}": (shape, BF16) for i, shape in enumerate(shapes)})
        scratch.update(
            dt_c=((BANDS * SLOTS, width), BF16),
            dt_y=((BANDS * SLOTS, width), BF16),
            dt_x=((BANDS * SLOTS, rows), BF16),
            dt_zs=((bands, SLOTS, rows), BF16),
            vec_c=((8, conv // 2), F32),
            vec_y=((8, conv // 2), F32),
            vec_x=((8, conv // 2), F32),
            vec_zs=((bands, 8, conv // 2), F32),
        )
    else:
        outs.update(grads)
    names = (*ins, *outs, *scratch, "send_sem", "recv_sem", "local_sem")
    results = pl.pallas_call(
        functools.partial(layer, names, fused, head_dim, taps),
        out_shape=[jax.ShapeDtypeStruct(*v) for v in outs.values()],
        in_specs=[pl.BlockSpec(memory_space=pl.ANY if name in ("x_in", "g_in", "w_out") else pltpu.VMEM) for name in ins],
        out_specs=[pl.BlockSpec(memory_space=pl.ANY if name in ("layer_to", "input_to") else pltpu.VMEM) for name in outs],
        scratch_shapes=[pltpu.VMEM(*v) for v in scratch.values()]
        + [pltpu.SemaphoreType.DMA((SEMS,)), pltpu.SemaphoreType.DMA((SEMS,)), pltpu.SemaphoreType.DMA((8,))],
        compiler_params=pltpu.CompilerParams(
            collective_id=0, has_side_effects=True, vmem_limit_bytes=VMEM_BYTES
        ),
    )(*ins.values())
    return dict(zip(outs, results))


VMEM_BYTES = 64 * 2**20 - 2**18


def body(residual, cotangent, norm_gain, w_zx, w_bc, w_dt, x_kernel, x_offset, bc_kernel, bc_offset, dt_bias, a_log, d_skip, gate_gain, w_out):
    _, length, width = residual.shape
    bands = lax.axis_size("wb")
    rows_own, heads_own, inner_own, state = w_zx.shape[0], w_dt.shape[1], w_zx.shape[2], w_bc.shape[2]
    heads, inner = heads_own * bands, inner_own * bands
    head_dim = inner_own // heads_own
    taps = x_kernel.shape[0]
    fused = (lax.axis_size("seq"), lax.axis_size("wa"), bands) == (4, 2, BANDS) and inner_own % LANES == 0
    per = heads // BANDS
    ins = dict(
        x_in=residual.reshape(length, width),
        g_in=cotangent.reshape(length, width),
        norm_gain=norm_gain,
        inner=inner,
        state2=2 * state,
    )

    if fused:
        ins.update(
            w_zx=w_zx, w_out=w_out, w_bc=w_bc, w_dt=w_dt.T, x_kernel=x_kernel, x_offset=x_offset,
            bc_kernel=bc_kernel, bc_offset=bc_offset, dt_bias=dt_bias, a_log=a_log, d_skip=d_skip, gate_gain=gate_gain,
        )
        out = run_layer(True, ins, head_dim, taps)
        any_space, vmem = pl.BlockSpec(memory_space=pl.ANY), pl.BlockSpec(memory_space=pltpu.VMEM)
        shapes = [
            ((length, width), BF16), ((length, width), F32), ((width,), F32), (w_zx.shape, F32), (w_bc.shape, F32),
            (w_dt.shape[::-1], F32), (x_kernel.shape, F32), (x_offset.shape, F32), (bc_kernel.shape, F32),
            (bc_offset.shape, F32), (dt_bias.shape, F32), (a_log.shape, F32), (d_skip.shape, F32), (gate_gain.shape, F32),
            (w_out.shape, F32),
        ]
        results = pl.pallas_call(
            functools.partial(hand_out, taps, tuple(out)),
            out_shape=[jax.ShapeDtypeStruct(*shape) for shape in shapes],
            in_specs=[any_space] * len(out),
            out_specs=[any_space if i in (0, 1, 3, 4, 14) else vmem for i in range(15)],
            scratch_shapes=[pltpu.VMEM(value.shape, value.dtype) for value in out.values()]
            + [pltpu.VMEM(shape, F32) for shape in (w_zx.shape, w_out.shape, w_bc.shape)]
            + [pltpu.SemaphoreType.DMA((len(out),)), pltpu.SemaphoreType.DMA((5,))],
            compiler_params=pltpu.CompilerParams(vmem_limit_bytes=VMEM_BYTES),
        )(*out.values())
        results = list(results)
        results[0] = results[0].reshape(residual.shape)
        results[1] = results[1].reshape(residual.shape)
        results[5] = results[5].T
        return tuple(results)

    own = jnp.concatenate(
        [x_kernel.astype(F32), x_offset.astype(F32)[None], gate_gain.astype(F32)[None], jnp.repeat(d_skip, head_dim)[None]]
    )
    par_bc = jnp.concatenate([bc_kernel.reshape(taps, 2 * state), bc_offset.reshape(1, 2 * state)], axis=0).astype(F32)
    par_bc = jnp.pad(par_bc, ((0, 16 - taps - 1), (0, 0)))
    wzx = lax.all_gather(lax.all_gather(w_zx, "wa", axis=0, tiled=True), "wb", axis=2, tiled=True)
    wdt = lax.all_gather(lax.all_gather(w_dt, "wa", axis=0, tiled=True), "wb", axis=1, tiled=True)
    wdt = jnp.pad(wdt.T.reshape(BANDS, per, width), ((0, 0), (0, SLOTS - per), (0, 0))).reshape(-1, width)
    small = lax.all_gather(jnp.stack([dt_bias, a_log]), "wb", axis=1, tiled=True).reshape(2, BANDS, per)
    small = jnp.pad(small, ((0, 6), (0, 0), (0, inner // BANDS - per))).reshape(8, inner)
    wide = jnp.pad(lax.all_gather(own, "wb", axis=1, tiled=True), ((0, 1), (0, 0)))
    ins.update(
        wz=wzx[:, 0],
        wx=wzx[:, 1],
        wo=lax.all_gather(lax.all_gather(w_out, "wa", axis=0, tiled=True), "wb", axis=1, tiled=True),
        wbc=lax.all_gather(w_bc, "wa", axis=0, tiled=True).reshape(width, 2 * state),
        wdt=jnp.pad(wdt, ((0, LANES - BANDS * SLOTS), (0, 0))),
        par=jnp.concatenate([jnp.concatenate([wide, small], axis=0), par_bc], axis=1),
    )
    out = run_layer(False, ins, head_dim, taps)

    def share(grad, columns=True):
        grad = lax.psum_scatter(grad.astype(F32), "wa", scatter_dimension=0, tiled=True)
        if columns:
            grad = lax.psum_scatter(grad, "wb", scatter_dimension=grad.ndim - 1, tiled=True)
        else:
            grad = lax.psum(grad, "wb")
        return lax.psum(grad, "seq")

    gdt = out["gdt"].reshape(BANDS, SLOTS, width)[:, :per].reshape(heads, width)
    vec = lax.psum(out["vec"], ("seq", "wa", "wb"))
    mine = lax.axis_index("wb")
    band = lax.dynamic_slice_in_dim(vec[:, :inner], mine * inner_own, inner_own, 1)
    by_head = jnp.stack([vec[5, inner : inner + LANES], vec[5, inner + LANES :], vec[6, width : width + LANES]])
    by_head = by_head[:, : BANDS * SLOTS].reshape(3, BANDS, SLOTS)[:, :, :per].reshape(3, heads)
    by_head = lax.dynamic_slice_in_dim(by_head, mine * heads_own, heads_own, 1)
    return (
        out["layer_to"].reshape(residual.shape),
        out["input_to"].reshape(residual.shape),
        vec[6, :width],
        share(jnp.stack([out["gz"], out["gx"]], axis=1)),
        share(out["gbc"], False).reshape(-1, 2, state),
        share(gdt.T),
        band[0:taps],
        band[4],
        vec[0:taps, inner:].reshape(taps, 2, state),
        vec[4, inner:].reshape(2, state),
        by_head[0],
        by_head[1],
        by_head[2],
        band[5],
        share(out["go"]),
    )


def solution(mesh):
    batch = P(("wa", "wb"), "seq", None)
    ins = (
        batch, batch, P(), P("wa", None, "wb"), P("wa", None, None), P("wa", "wb"), P(None, "wb"), P("wb"), P(), P(),
        P("wb"), P("wb"), P("wb"), P("wb"), P("wa", "wb"),
    )
    outs = (
        batch, batch, P(), P("wa", None, "wb"), P("wa", None, None), P("wa", "wb"), P(None, "wb"), P("wb"), P(), P(),
        P("wb"), P("wb"), P("wb"), P("wb"), P("wa", "wb"),
    )
    return jax.shard_map(body, mesh=mesh, in_specs=ins, out_specs=outs, check_vma=False)
```

```python
import functools
import types

import jax
import jax.numpy as jnp
from jax import lax
from jax.experimental import pallas as pl
from jax.experimental.pallas import tpu as pltpu
from jax.sharding import PartitionSpec as P

F32, BF16 = jnp.float32, jnp.bfloat16
EPSILON = 1e-05
Q = 128
LANES = 128
HALO = 16
SLOTS = 16
TILE = 256
BANDS = 4
NT = (((1,), (1,)), ((), ()))


def dot(a, b):
    return jnp.dot(a, b, preferred_element_type=F32)


def dot_nt(a, b):
    return lax.dot_general(a, b, NT, preferred_element_type=F32)


def dot_exact(a, b):
    return jnp.dot(a, b, precision=lax.Precision.HIGHEST, preferred_element_type=F32)


def sigmoid(v):
    return 0.5 + 0.5 * jnp.tanh(0.5 * v)


def fold8(v):
    return v.reshape(v.shape[0] // 8, 8, v.shape[1]).sum(axis=0)


def at(start, size):
    return pl.ds(pl.multiple_of(start, 16), size)


def lanes(start, size):
    return pl.ds(pl.multiple_of(start, LANES), size)


def rows_at(i, size=Q, base=0):
    return at(i * size + base, size)


def cols_at(i, size=LANES):
    return lanes(i * size, size)


def band_cols(R, band):
    width = R.wx.shape[1] // BANDS
    return lanes(width * band, width)


class Columns:
    def __init__(self, R, bands):
        self.parts = [band_cols(R, band) for band in bands]
        self.width = R.wx.shape[1] // BANDS

    def get(self, ref, rows=slice(None)):
        return jnp.concatenate([ref[rows, cols] for cols in self.parts], axis=1)

    def put(self, ref, rows, value):
        for n, cols in enumerate(self.parts):
            ref[rows, cols] = value[:, n * self.width : (n + 1) * self.width]


def head_spread(R, head_dim):
    inner = R.ex.shape[1]
    per_band = inner // BANDS
    row = lax.broadcasted_iota(jnp.int32, (LANES, LANES), 0)

    @pl.loop(0, inner // LANES)
    def _(c):
        lane = lax.broadcasted_iota(jnp.int32, (LANES, LANES), 1) + c * LANES
        hit = jnp.zeros((LANES, LANES), jnp.bool_)
        for band in range(BANDS):
            first = lane - band * per_band
            inside = (first >= 0) & (first < per_band)
            head = lax.shift_right_arithmetic(first, head_dim.bit_length() - 1)
            hit = hit | (inside & (row == band * SLOTS + head))
        R.ex[:, cols_at(c)] = jnp.where(hit, 1.0, 0.0).astype(BF16)

    lane = lax.broadcasted_iota(jnp.int32, (Q, LANES), 1)
    for head in range(R.pick.shape[0] // Q):
        R.pick[pl.ds(head * Q, Q), :] = jnp.where(lane == head, 1.0, 0.0).astype(BF16)


def norm_rows(R):
    gain = R.gain[...]

    @pl.loop(0, R.x.shape[0] // Q)
    def _(i):
        rows = R.x[rows_at(i), :].astype(F32)
        inv = lax.rsqrt(jnp.mean(rows * rows, axis=-1, keepdims=True) + EPSILON)
        value = (rows * inv * gain).astype(BF16)
        R.xn[rows_at(i, base=HALO), :] = value
        R.inv_rms[rows_at(i), :] = inv
        R.xnT[:, cols_at(i)] = value.T
        R.gT[:, cols_at(i)] = R.g[rows_at(i), :].T


def norm_halo(R):
    rows = R.x_halo[...].astype(F32)
    inv = lax.rsqrt(jnp.mean(rows * rows, axis=-1, keepdims=True) + EPSILON)
    R.xn[0:HALO, :] = (rows * inv * R.gain[...]).astype(BF16)


def project(R, left, right, out, band):
    cols = band_cols(R, band)
    out[:, cols] = dot(left[...], right[:, cols]).astype(out.dtype)


def grad_of(left, right, out):
    for j in range(out.shape[1] // (2 * TILE)):
        cols = pl.ds(j * 2 * TILE, 2 * TILE)
        out[:, cols] = dot(left[...], right[:, cols]).astype(out.dtype)


def project_bc(R):
    R.ci[:, R.wx.shape[1] :] = dot(R.xn[...], R.wbc[...])


def conv_tile(R, taps, cols, put):
    for i in range(R.x.shape[0] // Q):
        rows = pl.ds(i * Q, Q)
        pre = R.par[4:5, cols]
        for k in range(taps):
            conv_in = R.ci[pl.ds(HALO - (taps - 1) + k + i * Q, Q), cols]
            pre = pre + R.par[k : k + 1, cols] * conv_in
        R.cib[rows, cols] = conv_in.astype(BF16)
        sig = sigmoid(pre)
        act = pre * sig
        put(rows, act.astype(BF16))
        R.slope[rows, cols] = (sig + act * (1.0 - sig)).astype(BF16)


def convolve(R, taps, band):
    width = R.wx.shape[1] // BANDS
    for c in range(width // LANES):
        cols = lanes(width * band + c * LANES, LANES)

        def put(rows, act):
            R.xh[rows, cols] = act

        conv_tile(R, taps, cols, put)
    for i in range(R.x.shape[0] // Q):
        rows, cols = pl.ds(i * Q, Q), band_cols(R, band)
        dt = dot(R.dt_low[rows, :], R.ex[:, cols])
        R.xt[rows, cols] = (R.xh[rows, cols].astype(F32) * dt).astype(BF16)


def convolve_bc(R, taps):
    inner = R.wx.shape[1]

    def put_b(rows, act):
        R.bm[rows, :] = act

    def put_c(rows, act):
        R.cm[rows, :] = act

    conv_tile(R, taps, pl.ds(inner, LANES), put_b)
    conv_tile(R, taps, pl.ds(inner + LANES, LANES), put_c)

    for i in range(R.x.shape[0] // Q):
        rows = pl.ds(i * Q, Q)
        R.prod[rows, :] = dot_nt(R.cm[rows, :], R.bm[rows, :])
        R.prodT[rows, :] = dot_nt(R.bm[rows, :], R.cm[rows, :])


def lower_ones(strict=False):
    row = lax.broadcasted_iota(jnp.int32, (Q, Q), 0)
    col = lax.broadcasted_iota(jnp.int32, (Q, Q), 1)
    return jnp.where(row > col if strict else row >= col, 1.0, 0.0).astype(F32)


def step_sizes(R, per_band):
    cols = R.wx.shape[1] // BANDS
    lane = lax.broadcasted_iota(jnp.int32, (8, LANES), 1)
    heads = jnp.zeros((8, LANES), F32)
    for band in range(BANDS):
        block = R.par[8:16, pl.ds(band * cols, LANES)]
        heads = heads + pltpu.roll(jnp.where(lane < per_band, block, 0.0), band * SLOTS, 1)
    R.heads[...] = heads
    R.rate[...] = -jnp.exp(R.heads[1:2, :])
    bias, rate = R.heads[0:1, :], R.rate[...]
    ones = lower_ones()
    chunks = R.x.shape[0] // Q
    R.ends[...] = jnp.zeros_like(R.ends)
    for i in range(chunks):
        rows = pl.ds(i * Q, Q)
        v = dot_nt(R.xn[pl.ds(HALO + i * Q, Q), :], R.wdt[...]) + bias
        dt = jnp.maximum(v, 0.0) + jnp.log1p(jnp.exp(-jnp.abs(v)))
        R.dt[rows, :] = dt
        R.dt_sig[rows, :] = jax.nn.sigmoid(v)
        logs = dot_exact(ones, dt * rate)
        R.logs[rows, :] = logs
        R.logsT[:, rows] = logs.T
        last = logs[Q - 1 : Q, :]
        R.ends[i : i + 1, :] = last
        R.dt_low[rows, :] = dt.astype(BF16)
        R.tail_low[rows, :] = jnp.exp(last - logs).astype(BF16)
        R.exp_low[rows, :] = jnp.exp(logs).astype(BF16)
    decay = jnp.exp(R.ends[...])
    high = decay.astype(BF16)
    low = (decay - high.astype(F32)).astype(BF16)
    R.decx[...] = dot(high, R.ex[...]) + dot(low, R.ex[...])


def local_states(R, bands):
    chunks = R.x.shape[0] // Q
    columns = Columns(R, bands)
    get, put = columns.get, columns.put
    spread = get(R.ex)
    total = decay = None
    for i in range(chunks):
        rows = pl.ds(i * Q, Q)
        ended = get(R.xt, rows).astype(F32) * dot(R.tail_low[rows, :], spread)
        fresh = dot(R.bm[rows, :].T, ended.astype(BF16))
        put(R.sl, rows_at(i, LANES), fresh.astype(BF16))
        step = get(R.decx, slice(i, i + 1))
        total = fresh if total is None else total * step + fresh
        decay = step if decay is None else decay * step
    put(R.piece, slice(None), total)
    put(R.piece_decay, slice(None), decay)


def halves(value):
    first = lax.broadcasted_iota(jnp.int32, value.shape, 1) < LANES // 2
    zero = jnp.zeros_like(value)
    return jnp.concatenate([jnp.where(first, value, zero), jnp.where(first, zero, value)], axis=0)


def causal_mask(by_row):
    row = lax.broadcasted_iota(jnp.int32, (Q, Q), 0)
    col = lax.broadcasted_iota(jnp.int32, (Q, Q), 1)
    return row >= col if by_row else row <= col


def band_logs(R, rows, band):
    return pltpu.roll(R.logs[rows, :], lax.rem(LANES - SLOTS * band, LANES), 1)


def inside_forward(R, per_band, band):
    width = R.wx.shape[1] // BANDS
    causal = causal_mask(True)
    for i in range(R.x.shape[0] // Q):
        rows = pl.ds(i * Q, Q)
        logs = band_logs(R, rows, band)
        logsT = R.logsT[at(SLOTS * band, 8), rows]
        for pair in range(per_band // 2):
            cols = lanes(width * band + pair * LANES, LANES)
            mixes = []
            for head in (2 * pair, 2 * pair + 1):
                gap = logs[:, head : head + 1] - logsT[head : head + 1, :]
                decay = jnp.exp(jnp.where(causal, gap, -1e30))
                mixes.append((R.prod[rows, :] * decay).astype(BF16))
            R.y[rows, cols] = dot(jnp.concatenate(mixes, axis=1), halves(R.xt[rows, cols]))


def carried_forward(R):
    chunks = R.x.shape[0] // Q
    state = R.from_before[...].astype(F32)
    for i in range(chunks):
        rows = pl.ds(i * Q, Q)
        block = rows_at(i, LANES)
        low = state.astype(BF16)
        R.s_in[block, :] = low
        spread = dot(R.exp_low[rows, :], R.ex[...])
        R.expx[rows, :] = spread.astype(BF16)
        R.y[rows, :] += dot(R.cm[rows, :], low) * spread
        if i < chunks - 1:
            state = state * R.decx[i : i + 1, :] + R.sl[block, :].astype(F32)


def gate_forward(R):
    inner = R.wx.shape[1]
    block = 64

    @pl.loop(0, R.x.shape[0] // block)
    def _(i):
        rows = rows_at(i, block)
        squares = jnp.zeros((block, LANES), F32)
        for c in range(inner // LANES):
            cols = pl.ds(c * LANES, LANES)
            y = R.y[rows, cols] + R.par[6:7, cols] * R.xh[rows, cols].astype(F32)
            R.y[rows, cols] = y
            z = R.z[rows, cols]
            gated = (y * (z * sigmoid(z))).astype(BF16)
            R.gated[rows, cols] = gated
            gated = gated.astype(F32)
            squares = squares + gated * gated
        inv = lax.rsqrt(jnp.sum(squares, axis=-1, keepdims=True) / inner + EPSILON)
        R.inv_gate[rows, :] = inv
        inv = jnp.broadcast_to(inv, (block, LANES))
        for c in range(inner // LANES):
            cols = pl.ds(c * LANES, LANES)
            R.hidden[rows, cols] = (R.gated[rows, cols].astype(F32) * inv * R.par[5:6, cols]).astype(BF16)


def gate_backward(R, part, parts):
    inner = R.wx.shape[1]
    block = 64
    count = R.x.shape[0] // block // parts
    if part == 0:
        R.gain_acc[...] = jnp.zeros_like(R.gain_acc)
        R.skip_acc[...] = jnp.zeros_like(R.skip_acc)

    @pl.loop(part * count, (part + 1) * count)
    def _(i):
        rows = rows_at(i, block)
        cross = jnp.zeros((block, LANES), F32)
        for c in range(inner // LANES):
            cols = pl.ds(c * LANES, LANES)
            cross = cross + R.gated[rows, cols].astype(F32) * (R.dh[rows, cols].astype(F32) * R.par[5:6, cols])
        inv = R.inv_gate[rows, :]
        cross = jnp.sum(cross, axis=-1, keepdims=True) * (inv * inv * inv / inner)
        inv = jnp.broadcast_to(inv, (block, LANES))
        cross = jnp.broadcast_to(cross, (block, LANES))
        for c in range(inner // LANES):
            cols = pl.ds(c * LANES, LANES)
            gated = R.gated[rows, cols].astype(F32)
            dh = R.dh[rows, cols].astype(F32) * inv
            R.gain_acc[:, cols] += fold8(dh * gated)
            d_gated = dh * R.par[5:6, cols] - gated * cross
            z = R.z[rows, cols]
            sig = sigmoid(z)
            lin = z * sig
            dy = d_gated * lin
            R.dz[rows, cols] = (d_gated * R.y[rows, cols] * (sig + lin * (1.0 - sig))).astype(BF16)
            R.dyl[rows, cols] = (dy * R.expx[rows, cols].astype(F32)).astype(BF16)
            R.dy[rows, cols] = dy.astype(BF16)
            R.skip_acc[:, cols] += fold8(dy * R.xh[rows, cols].astype(F32))


def branch_out(R):
    width = R.x.shape[1]
    for j in range(width // TILE):
        cols = pl.ds(j * TILE, TILE)
        R.layer_out[:, cols] = (
            R.x[:, cols].astype(F32) + dot_nt(R.hidden[...], R.wo[cols, :])
        ).astype(BF16)


def local_adjoints(R):
    chunks = R.x.shape[0] // Q
    total = None
    for i in range(chunks - 1, -1, -1):
        pulled = dot(R.cm[pl.ds(i * Q, Q), :].T, R.dyl[pl.ds(i * Q, Q), :])
        R.dl[rows_at(i, LANES), :] = pulled.astype(BF16)
        total = pulled if total is None else total * R.decx[i : i + 1, :] + pulled
    R.piece[...] = total


def inside_backward(R, per_band, band):
    width = R.wx.shape[1] // BANDS
    causal = causal_mask(False)
    for i in range(R.x.shape[0] // Q):
        rows = pl.ds(i * Q, Q)
        logs = band_logs(R, rows, band)
        logsT = R.logsT[at(SLOTS * band, 8), rows]
        d_prod = R.d_prod[rows, :]
        pulls, sums = [], []
        for pair in range(per_band // 2):
            cols = lanes(width * band + pair * LANES, LANES)
            dy = R.dy[rows, cols]
            d_both = dot_nt(halves(R.xt[rows, cols]), dy)
            mixes = []
            for half in range(2):
                head = 2 * pair + half
                gap = logsT[head : head + 1, :] - logs[:, head : head + 1]
                decay = jnp.exp(jnp.where(causal, gap, -1e30))
                mix = R.prodT[rows, :] * decay
                mixes.append(mix.astype(BF16))
                d_mix = d_both[half * Q : (half + 1) * Q, :]
                d_prod = d_prod + decay * d_mix
                pull = (mix * d_mix).astype(BF16)
                pulls.append(pull)
                sums.append(jnp.sum(pull.astype(F32), axis=0, keepdims=True))
            R.u[rows, cols] = dot(jnp.concatenate(mixes, axis=1), halves(dy))
        R.d_prod[rows, :] = d_prod
        R.pullsT[at(SLOTS * band, 8), rows] = jnp.concatenate([*sums, jnp.zeros((8 - per_band, Q), F32)], axis=0)
        R.pulls[rows, :] += pltpu.roll(dot(jnp.concatenate(pulls, axis=1), R.pick[...]), SLOTS * band, 1)


def backward_start(R):
    for ref in (R.pulls, R.pullsT, R.d_prod, R.d_tail, R.db, R.dc, R.d_log, R.direct):
        ref[...] = jnp.zeros_like(ref)


def carried_backward(R, i, bands):
    columns = Columns(R, bands)
    get, put = columns.get, columns.put
    spread = get(R.ex)
    grad = get(R.from_after).astype(F32) if i == R.x.shape[0] // Q - 1 else get(R.piece)
    rows = pl.ds(i * Q, Q)
    block = rows_at(i, LANES)

    def add(ref, value):
        ref[rows, :] += value

    low = grad.astype(BF16)
    tail = dot(R.tail_low[rows, :], spread)
    xt = get(R.xt, rows).astype(F32)
    pulled = dot(R.bm[rows, :], low) * tail
    u = get(R.u, rows) + pulled
    add(R.d_tail, dot_nt((xt * pulled).astype(BF16), spread))
    add(R.db, dot_nt((xt * tail).astype(BF16), low))
    state = get(R.s_in, block)
    dyl = get(R.dyl, rows)
    add(R.dc, dot_nt(dyl, state))
    add(R.d_log, dot_nt((dyl.astype(F32) * dot(R.cm[rows, :], state)).astype(BF16), spread))
    decay = get(R.decx, slice(i, i + 1))
    put(R.kept, slice(i, i + 1), jnp.sum(grad * state.astype(F32), axis=0, keepdims=True) * decay)
    if i:
        put(R.piece, slice(None), grad * decay + get(R.dl, block).astype(F32))
    add(R.direct, dot_nt((get(R.xh, rows).astype(F32) * u).astype(BF16), spread))
    dx = dot(R.dt_low[rows, :], spread) * u + get(R.par, slice(6, 7)) * get(R.dy, rows).astype(F32)
    put(R.dpre, rows, dx * get(R.slope, rows).astype(F32))


def step_grads(R):
    chunks = R.x.shape[0] // Q
    inner = R.wx.shape[1]
    later = lower_ones().T
    before = lower_ones(strict=True)
    high = R.kept[...].astype(BF16)
    low = (R.kept[...] - high.astype(F32)).astype(BF16)
    kept = dot_nt(high, R.ex[...]) + dot_nt(low, R.ex[...])
    rate_acc = jnp.zeros((8, LANES), F32)
    bias_acc = jnp.zeros((8, LANES), F32)
    for i in range(chunks):
        rows = pl.ds(i * Q, Q)
        sides = R.d_log[rows, :] + R.pullsT[:, rows].T - R.pulls[rows, :]
        d_decay = dot_exact(later, sides) + dot_exact(before, R.d_tail[rows, :]) + kept[i : i + 1, :]
        d_raw = (R.direct[rows, :] + R.rate[...] * d_decay) * R.dt_sig[rows, :]
        rate_acc = rate_acc + fold8(R.dt[rows, :] * d_decay)
        bias_acc = bias_acc + fold8(d_raw)
        R.d_raw[rows, :] = d_raw.astype(BF16)
        d_prod = R.d_prod[rows, :].astype(BF16)
        db = R.db[rows, :] + dot(d_prod, R.cm[rows, :])
        dc = R.dc[rows, :] + dot(d_prod.T, R.bm[rows, :])
        R.dpre[rows, inner : inner + LANES] = db * R.slope[rows, inner : inner + LANES].astype(F32)
        R.dpre[rows, inner + LANES :] = dc * R.slope[rows, inner + LANES :].astype(F32)
    R.rate_acc[...] = rate_acc
    R.bias_acc[...] = bias_acc


def conv_backward(R, taps, first, width):
    length = R.x.shape[0]
    halo = lanes(first, width)
    R.dpre[pl.ds(length, HALO), halo] = R.dpre_halo[:, halo].astype(F32)

    @pl.loop(0, width // LANES)
    def _(c):
        cols = lanes(first + c * LANES, LANES)
        sums = [jnp.zeros((8, LANES), F32) for _ in range(taps + 1)]
        for i in range(length // Q):
            base = i * Q
            conv_in = R.cib[pl.ds(base, Q), cols].astype(F32)
            d_conv = None
            for k in range(taps):
                ahead = R.dpre[pl.ds(base + taps - 1 - k, Q), cols]
                sums[k] = sums[k] + fold8(ahead * conv_in)
                term = R.par[k : k + 1, cols] * ahead
                d_conv = term if d_conv is None else d_conv + term
            sums[taps] = sums[taps] + fold8(ahead)
            R.dconv[pl.ds(base, Q), cols] = d_conv.astype(BF16)
        for k in range(taps + 1):
            R.vec[k : k + 1, cols] = jnp.sum(sums[k], axis=0, keepdims=True)


def input_first(R):
    for j in range(R.x.shape[1] // TILE):
        cols = pl.ds(j * TILE, TILE)
        R.input_grad[:, cols] = dot_nt(R.dz[...], R.wz[cols, :])


def input_second(R):
    inner = R.wx.shape[1]
    for j in range(R.x.shape[1] // TILE):
        cols = pl.ds(j * TILE, TILE)
        R.input_grad[:, cols] += (
            dot_nt(R.dconv[:, 0:inner], R.wx[cols, :])
            + dot_nt(R.dconv[:, inner:], R.wbc[cols, :])
            + dot(R.d_raw[...], R.wdt[:, cols])
        )


def input_last(R):
    width = R.x.shape[1]
    gain = R.gain[...]
    R.norm_acc[...] = jnp.zeros_like(R.norm_acc)

    @pl.loop(0, R.x.shape[0] // 64)
    def _(i):
        rows = rows_at(i, 64)
        d_normed = R.input_grad[rows, :]
        x = R.x[rows, :].astype(F32)
        inv = R.inv_rms[rows, :]
        pulled = d_normed * x
        R.norm_acc[...] += fold8(pulled * inv)
        middle = jnp.sum(pulled * gain, axis=-1, keepdims=True) * (inv * inv * inv / width)
        R.input_grad[rows, :] = R.g[rows, :].astype(F32) + (d_normed * gain) * inv - x * middle


def small_sums(R):
    inner = R.wx.shape[1]
    width = R.gain.shape[1]
    R.vec[5:8, :] = jnp.zeros((3, R.vec.shape[1]), F32)
    R.vec[5:6, 0:inner] = jnp.sum(R.gain_acc[...], axis=0, keepdims=True)
    R.vec[6:7, 0:width] = jnp.sum(R.norm_acc[...], axis=0, keepdims=True)
    R.vec[5:6, inner : inner + LANES] = jnp.sum(R.bias_acc[...], axis=0, keepdims=True)
    R.vec[5:6, inner + LANES :] = jnp.sum(R.rate_acc[...], axis=0, keepdims=True) * R.rate[...]
    skip = R.skip_acc[...]
    high = skip.astype(BF16)
    low = (skip - high.astype(F32)).astype(BF16)
    R.vec[6:7, width : width + LANES] = jnp.sum(
        dot_nt(high, R.ex[...]) + dot_nt(low, R.ex[...]), axis=0, keepdims=True
    )


SEMS = 256
WINDOW = {"x": 3, "y": 4, "z": 2}


class Wires:
    def __init__(self, R):
        self.R, self.used, self.started = R, 0, []
        self.leaving = {link: [] for link in WINDOW}

    def new(self):
        self.used += 1
        return self.used - 1

    def copy(self, src, dst, sem, where):
        return pltpu.make_async_remote_copy(
            src_ref=src,
            dst_ref=dst,
            send_sem=self.R.send_sem.at[sem],
            recv_sem=self.R.recv_sem.at[sem],
            device_id=where,
            device_id_type=pl.DeviceIdType.MESH,
        )

    def start(self, src, dst, sem, where, link=None):
        copy = self.copy(src, dst, sem, where)
        if link is None:
            self.started.append(copy)
        else:
            leaving = self.leaving[link]
            if len(leaving) == WINDOW[link]:
                leaving.pop(0).wait_send()
            leaving.append(copy)
        copy.start()

    def arrived(self, dst, sem, where):
        self.copy(dst, dst, sem, where).wait_recv()

    def drain(self):
        for copy in sum(self.leaving.values(), self.started):
            copy.wait_send()


class Place:
    def __init__(self):
        self.seq, self.a, self.b = lax.axis_index("seq"), lax.axis_index("wa"), lax.axis_index("wb")
        self.bands, self.rows = lax.axis_size("wb"), lax.axis_size("wa")
        self.c = lax.rem(self.seq, 2)
        self.y = lax.div(self.seq, 2)
        self.core = {"seq": self.seq + 1 - 2 * self.c}
        self.over_y = {"seq": lax.rem(self.seq + 2, 4)}
        self.over_x = {"wa": 1 - self.a}

    def band(self, k):
        return lax.rem(self.b + k + self.bands, self.bands)

    def over_z(self, k):
        return {"wb": self.band(k)}

    def greet(self):
        barrier = pltpu.get_barrier_semaphore()
        peers = [{"seq": lax.rem(self.seq + k, 4)} for k in range(1, 4)]
        peers += [self.over_z(k) for k in range(1, self.bands)] + [self.over_x]
        for peer in peers:
            pl.semaphore_signal(barrier, 1, device_id=peer, device_id_type=pl.DeviceIdType.MESH)
        return lambda: pl.semaphore_wait(barrier, len(peers))


class Grid:
    def __init__(self, row, col, half, own, width):
        self.row, self.col, self.half, self.own, self.width = row, col, half, own, width
        self.span = half - own

    def cols(self, band):
        return lanes(self.col(band), self.width)

    def half_rows(self, a, band, c):
        return at(self.row(a, band) + self.half * c, self.half)

    def span_rows(self, a, band, p):
        return at(self.row(a, band) + self.half * p.c + self.own * p.y, self.span)

    def own_rows(self, a, band, p, y):
        return at(self.row(a, band) + self.half * p.c + (self.half - self.own) * y, self.own)


class Gather:
    def __init__(self, wires, p, whole, grid):
        self.w, self.p, self.whole, self.g = wires, p, whole, grid
        self.z = [wires.new() for _ in range(p.bands)]
        self.x = [wires.new() for _ in range(p.bands)]
        self.y = [[wires.new() for _ in range(p.bands)] for _ in range(2)]
        self.c = [[wires.new() for _ in range(p.bands)] for _ in range(2)]

    def here(self, rows, k):
        return self.whole.at[rows, self.g.cols(self.p.band(-k))]

    def start(self):
        mine = self.here(self.g.span_rows(self.p.a, self.p.b, self.p), 0)
        self.w.start(mine, mine, self.x[0], self.p.over_x, "x")

    def start_z(self, k):
        mine = self.here(self.g.span_rows(self.p.a, self.p.b, self.p), 0)
        self.w.start(mine, mine, self.z[k], self.p.over_z(k), "z")

    def over_x(self, k):
        if k == 0:
            return
        p, g = self.p, self.g
        rows = g.span_rows(p.a, p.b, p)
        self.w.arrived(self.here(rows, k), self.z[k], p.over_z(k))
        self.w.start(self.here(rows, k), self.here(rows, k), self.x[k], p.over_x, "x")
        mine = self.here(g.own_rows(p.a, p.b, p, p.y), k)
        self.w.start(mine, mine, self.y[0][k], p.over_y, "y")

    def over_y(self, k):
        p, g = self.p, self.g
        self.w.arrived(self.here(g.span_rows(1 - p.a, p.b, p), k), self.x[k], p.over_x)
        mine = self.here(g.own_rows(1 - p.a, p.b, p, p.y), k)
        self.w.start(mine, mine, self.y[1][k], p.over_y, "y")

    def sides(self, k):
        return [(0, self.p.a), (1, 1 - self.p.a)] if k else [(1, 1 - self.p.a)]

    def over_core(self, k):
        p, g = self.p, self.g
        for side, a in self.sides(k):
            self.w.arrived(self.here(g.own_rows(a, p.b, p, 1 - p.y), k), self.y[side][k], p.over_y)
            mine = self.here(g.half_rows(a, p.b, p.c), k)
            self.w.start(mine, mine, self.c[side][k], p.core)

    def finish(self, k):
        p, g = self.p, self.g
        for side, a in self.sides(k):
            self.w.arrived(self.here(g.half_rows(a, p.b, 1 - p.c), k), self.c[side][k], p.core)

class Scatter:
    def __init__(self, wires, p, grad, grid, spaces, large):
        self.w, self.p, self.grad, self.g = wires, p, grad, grid
        self.links = ("y", "x", "z") if large else (None,) * 3
        self.rc, self.ry, self.rx, self.rz, self.mine, self.peer = spaces
        self.order = [*range(1, p.bands), 0]
        self.c = [[wires.new() for _ in range(p.bands)] for _ in range(2)]
        self.y = [[wires.new() for _ in range(p.bands)] for _ in range(2)]
        self.x = [wires.new() for _ in range(p.bands)]
        self.z = [wires.new() for _ in range(p.bands)]
        self.last, self.share = wires.new(), wires.new()

    @staticmethod
    def spaces(bands, grid):
        half, own, span, width = grid.half, grid.own, grid.span, grid.width
        return [
            (2, bands, half, width),
            (2, bands, own, width),
            (bands, span, width),
            (bands, span, width),
            (span, width),
            (span, width),
        ]

    def here(self, rows, k):
        return self.grad.at[rows, self.g.cols(self.p.band(k))]

    def add(self, rows, k, part):
        spot = self.here(rows, k)
        spot[...] = (spot[...].astype(F32) + part.astype(F32)).astype(BF16)

    def start_c(self, ks=None):
        p, g = self.p, self.g
        for k in self.order if ks is None else ks:
            for a in range(2):
                rows = g.half_rows(a, p.band(k), 1 - p.c)
                self.w.start(self.here(rows, k), self.rc.at[a, k], self.c[a][k], p.core)

    def start_y(self, ks=None):
        p, g = self.p, self.g
        for k in self.order if ks is None else ks:
            for a in range(2):
                self.w.arrived(self.rc.at[a, k], self.c[a][k], p.core)
                self.add(g.half_rows(a, p.band(k), p.c), k, self.rc[a, k])
                rows = g.own_rows(a, p.band(k), p, 1 - p.y)
                self.w.start(self.here(rows, k), self.ry.at[a, k], self.y[a][k], p.over_y, self.links[0])

    def start_x(self, ks=None):
        p, g = self.p, self.g
        for k in self.order if ks is None else ks:
            for a in range(2):
                self.w.arrived(self.ry.at[a, k], self.y[a][k], p.over_y)
                self.add(g.own_rows(a, p.band(k), p, p.y), k, self.ry[a, k])
            rows = g.span_rows(1 - p.a, p.band(k), p)
            self.w.start(self.here(rows, k), self.rx.at[k], self.x[k], p.over_x, self.links[1])

    def start_z(self, ks=None):
        p, g = self.p, self.g
        for k in self.order if ks is None else ks:
            rows = g.span_rows(p.a, p.band(k), p)
            self.w.arrived(self.rx.at[k], self.x[k], p.over_x)
            self.add(rows, k, self.rx[k])
            if k:
                self.w.start(self.here(rows, k), self.rz.at[k], self.z[k], p.over_z(k), self.links[2])

    def start_last(self):
        p, g = self.p, self.g
        total = self.here(g.span_rows(p.a, p.b, p), 0)[...].astype(F32)
        for k in range(1, p.bands):
            self.w.arrived(self.rz.at[k], self.z[k], p.over_z(k))
            total = total + self.rz[k].astype(F32)
        self.mine[...] = total.astype(BF16)
        self.w.start(self.mine, self.peer, self.last, p.over_y, self.links[0])

    def result(self, out, first):
        p, g = self.p, self.g
        self.w.arrived(self.peer, self.last, p.over_y)
        both = g.span - g.own
        middle = self.mine[at(g.own * (1 - p.y), both), :].astype(F32) + self.peer[at(g.own * p.y, both), :].astype(F32)
        out[at(first + g.own, both), :] = middle.astype(out.dtype)
        far = (g.half - g.own) * p.y
        out[at(first + far, g.own), :] = self.mine[at(both * p.y, g.own), :].astype(out.dtype)
        far = (g.half - g.own) * (1 - p.y)
        out[at(first + far, g.own), :] = self.peer[at(both * (1 - p.y), g.own), :].astype(out.dtype)

    def start_share(self, out):
        p, g = self.p, self.g
        self.result(out, g.half * p.c)
        mine = out.at[at(g.half * p.c, g.half), :]
        self.w.start(mine, mine, self.share, p.core)

    def finish(self, out):
        p, g = self.p, self.g
        self.w.arrived(out.at[at(g.half * (1 - p.c), g.half), :], self.share, p.core)


class Exchange:
    def __init__(self, wires, p, value, spaces):
        self.w, self.p, self.value, self.spaces = wires, p, value, spaces
        self.sems = [wires.new() for _ in range(3)]

    def start(self, step, where, src=None):
        self.w.start(self.value if src is None else src, self.spaces[step], self.sems[step], where)
        self.sent = self.w.started.pop()

    def add(self, step, where, spot=None):
        self.w.arrived(self.spaces[step], self.sems[step], where)
        self.sent.wait_send()
        spot = self.value if spot is None else spot
        total = spot[...].astype(F32) + self.spaces[step][...].astype(F32)
        spot[...] = total.astype(spot.dtype)


class Chain:
    def __init__(self, R, wires, landing, place, count, step):
        self.R, self.w, self.landing, self.step, self.place = R, wires, landing, step, place
        self.has_from = place > 0 if step > 0 else place < count - 1
        self.has_to = place < count - 1 if step > 0 else place > 0
        self.sems = [wires.new() for _ in range(BANDS)]

    def copy(self, k, band):
        cols = band_cols(self.R, band)
        where = {"seq": self.place + self.step}
        return cols, self.w.copy(self.R.outgoing.at[:, cols], self.landing.at[:, cols], self.sems[k], where)

    def run(self, k, band):
        R = self.R
        cols, copy = self.copy(k, band)

        @pl.when(self.has_from)
        def _():
            copy.wait_recv()

        @pl.when(self.has_to)
        def _():
            incoming = self.landing[:, cols].astype(F32)
            R.outgoing[:, cols] = (R.piece[:, cols] + R.piece_decay[:, cols] * incoming).astype(BF16)
            copy.start()

    def sent(self, bands):
        @pl.when(self.has_to)
        def _():
            for k, band in enumerate(bands):
                self.copy(k, band)[1].wait_send()


def alias(R, fused):
    half = R.states.shape[0] // 2
    R.sl, R.s_in = R.states.at[0:half, :], R.states.at[half : 2 * half, :]
    R.dl, R.u, R.dyl, R.dconv, R.dpre, R.dz, R.dy = R.sl, R.z, R.gated, R.slope, R.ci, R.dh, R.expx
    R.y = R.dpre.at[0 : R.x.shape[0], 0 : R.wx.shape[1]]
    R.layer_out = R.xn.at[HALO:, :]
    R.input_grad = R.u.at[:, 0 : R.x.shape[1]]
    if fused:
        R.gx = R.states.at[0 : R.wx.shape[0], :]


def own_params(R, p, taps, head_dim):
    cols, width = R.x_kernel.shape[1], R.x.shape[1]
    inner, state = R.wx.shape[1], R.bc_kernel.shape[2]
    row = lambda ref: ref[...].astype(F32).reshape(1, ref.shape[0])
    lane = lax.broadcasted_iota(jnp.int32, (1, cols), 1)
    skip = jnp.zeros((1, cols), F32)
    heads = R.d_skip.shape[0]
    for head in range(heads):
        hit = lax.shift_right_arithmetic(lane, head_dim.bit_length() - 1) == head
        skip = jnp.where(hit, row(R.d_skip)[:, head : head + 1], skip)
    pad = jnp.zeros((1, cols - heads), F32)
    block = [R.x_kernel[...].astype(F32), row(R.x_offset), row(R.gate_gain), skip, jnp.zeros((1, cols), F32)]
    block += [jnp.concatenate([row(ref), pad], axis=1) for ref in (R.dt_bias, R.a_log)]
    R.par[:, lanes(cols * p.b, cols)] = jnp.concatenate([*block, jnp.zeros((6, cols), F32)], axis=0)
    kernel, offset = R.bc_kernel[...].astype(F32), R.bc_offset[...].astype(F32)
    for half in range(2):
        rows = [kernel[:, half, :], offset[half : half + 1, :], jnp.zeros((16 - taps - 1, state), F32)]
        R.par[:, pl.ds(inner + half * state, state)] = jnp.concatenate(rows, axis=0)
    rows, slot = R.w_bc.shape[0], R.w_dt.shape[0]
    block = 64

    @pl.loop(0, rows // block)
    def _(i):
        here = at(rows * p.a + i * block, block)
        w_zx = R.w_zx[pl.ds(i * block, block)].astype(F32)
        for half, whole in enumerate((R.wz, R.wx)):
            whole[here, lanes(cols * p.b, cols)] = w_zx[:, half, :].astype(BF16)
        w_bc = R.w_bc[pl.ds(i * block, block)].astype(F32)
        for half in range(2):
            R.wbc[here, pl.ds(half * state, state)] = w_bc[:, half, :].astype(BF16)

    w_dt = jnp.concatenate([R.w_dt[...].astype(F32), jnp.zeros((SLOTS - slot, rows), F32)], axis=0)
    R.wdt[at(SLOTS * p.b, SLOTS), lanes(rows * p.a, rows)] = w_dt.astype(BF16)
    R.wdt[BANDS * SLOTS :, :] = jnp.zeros((LANES - BANDS * SLOTS, width), BF16)


class Steps:
    def __init__(self, ops):
        self.ops = ops

    def __getattr__(self, name):
        def run(*which):
            step = self.ops.pop(" ".join(map(str, (name, *which))), None)
            if step is not None:
                step()

        return run


def layer(names, fused, head_dim, taps, *refs):
    R = types.SimpleNamespace(**dict(zip(names, refs)))
    alias(R, fused)
    inner = R.wx.shape[1]
    width = R.wx.shape[0]
    count = lax.axis_size("seq")
    place = lax.axis_index("seq")
    per_band = inner // head_dim // BANDS
    length = R.x.shape[0]
    first, last = place == 0, place == count - 1
    early = place < count // 2
    wires = Wires(R)
    ops = {}

    def op(name):
        return lambda run: ops.__setitem__(name, run)

    if fused:
        p = Place()
        greeted = p.greet()
        order = [p.band(-k) for k in range(BANDS)]
        back = [(k, p.band(k)) for k in (*range(1, BANDS), 0)]
        rows, cols = R.w_out.shape
        own_out = R.wo.at[at(rows * p.a, rows), lanes(cols * p.b, cols)]
        loads = [(R.x_in, R.x), (R.g_in, R.g), (R.w_out, own_out)]
    else:
        loads = [(R.x_in, R.x), (R.g_in, R.g)]
        order = list(range(BANDS))
        back = [(k, k) for k in range(BANDS)]
        barrier = pltpu.get_barrier_semaphore()

        @pl.when(jnp.logical_not(last))
        def _():
            pl.semaphore_signal(barrier, 1, device_id={"seq": place + 1}, device_id_type=pl.DeviceIdType.MESH)

        @pl.when(jnp.logical_not(first))
        def _():
            pl.semaphore_signal(barrier, 1, device_id={"seq": place - 1}, device_id_type=pl.DeviceIdType.MESH)

        greeted = lambda: pl.semaphore_wait(barrier, jnp.where(first | last, 1, 2))

    @pl.when(first)
    def _():
        R.x_halo[...] = jnp.zeros_like(R.x_halo)
        R.from_before[...] = jnp.zeros_like(R.from_before)

    @pl.when(last)
    def _():
        R.from_after[...] = jnp.zeros_like(R.from_after)
        R.dpre_halo[...] = jnp.zeros_like(R.dpre_halo)

    loads = [pltpu.make_async_copy(*pair, R.local_sem.at[i]) for i, pair in enumerate(loads)]
    for load in loads:
        load.start()
    if fused:
        own_params(R, p, taps, head_dim)
    R.gain[...] = R.norm_gain[...].astype(F32).reshape(1, width)
    for load in loads:
        load.wait()
    norm_rows(R)
    greeted()

    x_copy = wires.copy(R.x.at[pl.ds(length - HALO, HALO), :], R.x_halo, wires.new(), {"seq": place + 1})
    band_width = inner // BANDS
    groups = [[band for _, band in back[: BANDS // 2]], [band for _, band in back[BANDS // 2 :]]]
    pre_parts = [[(band_width * band, band_width) for band in bands] for bands in groups]
    pre_parts[1].append((inner, R.wbc.shape[1]))
    pre_copies = [
        [
            wires.copy(R.dpre_out.at[:, lanes(*part)], R.dpre_halo.at[:, lanes(*part)], wires.new(), {"seq": place - 1})
            for part in parts
        ]
        for parts in pre_parts
    ]
    forward = Chain(R, wires, R.from_before, place, count, 1)
    backward = Chain(R, wires, R.from_after, place, count, -1)
    layer_copy = pltpu.make_async_copy(R.layer_out, R.layer_to, R.local_sem.at[3])
    input_copy = pltpu.make_async_copy(R.input_grad, R.input_to, R.local_sem.at[4])

    @pl.when(jnp.logical_not(last))
    def _():
        x_copy.start()

    if fused:
        half = rows // 2
        grid = Grid(lambda a, band: rows * a, lambda band: cols * band, half, rows // 6, cols)
        gathers = {
            name: Gather(wires, p, whole, grid) for name, whole in (("x", R.wx), ("z", R.wz), ("o", R.wo))
        }
        dt_here = lambda k: R.wdt.at[at(SLOTS * p.band(-k), SLOTS), lanes(rows * p.a, rows)]
        par_here = lambda k: R.par.at[:, grid.cols(p.band(-k))]
        bc_half = lambda a, c: R.wbc.at[at(rows * a + half * c, half), :]
        dt_col = lambda a: R.wdt.at[pl.ds(0, BANDS * SLOTS), lanes(rows * a, rows)]
        dt_z, par_z = ([wires.new() for _ in range(p.bands)] for _ in range(2))
        dt_x, bc_x, bc_c = wires.new(), wires.new(), wires.new()
        for k in range(1, p.bands):
            wires.start(dt_here(0), dt_here(0), dt_z[k], p.over_z(k))
            wires.start(par_here(0), par_here(0), par_z[k], p.over_z(k))
        wires.start(bc_half(p.a, p.c), bc_half(p.a, p.c), bc_x, p.over_x)
        gathers["x"].start()

        for name, weight in gathers.items():
            if name != "x":
                op(f"GX0 {name} 0")(weight.start)
            for k in range(p.bands):
                if k:
                    op(f"GZ {name} {k}")(functools.partial(weight.start_z, k))
                    op(f"X {name} {k}")(functools.partial(weight.over_x, k))
                op(f"Y {name} {k}")(functools.partial(weight.over_y, k))
                op(f"C {name} {k}")(functools.partial(weight.over_core, k))

        @op("dt1")
        def _():
            for k in range(1, p.bands):
                wires.arrived(dt_here(k), dt_z[k], p.over_z(k))
            wires.start(dt_col(p.a), dt_col(p.a), dt_x, p.over_x)

        @op("bc1")
        def _():
            wires.arrived(bc_half(1 - p.a, p.c), bc_x, p.over_x)
            wires.start(bc_half(1 - p.a, p.c), bc_half(1 - p.a, p.c), bc_c, p.core)

        @op("small")
        def _():
            for k in range(1, p.bands):
                wires.arrived(par_here(k), par_z[k], p.over_z(k))

    def arrived(name, k):
        if fused:
            gathers[name].finish(k)


    op("spread")(lambda: head_spread(R, head_dim))

    @op("halo")
    def _():
        @pl.when(jnp.logical_not(first))
        def _():
            x_copy.wait_recv()

        norm_halo(R)

    @op("bc")
    def _():
        if fused:
            wires.arrived(bc_half(1 - p.a, 1 - p.c), bc_c, p.core)
        project_bc(R)
        convolve_bc(R, taps)

    @op("steps")
    def _():
        if fused:
            wires.arrived(dt_col(1 - p.a), dt_x, p.over_x)
        step_sizes(R, per_band)

    def inner_x(k, band):
        arrived("x", k)
        project(R, R.xn, R.wx, R.ci, band)
        convolve(R, taps, band)

    def inner_z(k, band):
        arrived("z", k)
        project(R, R.xn.at[HALO:, :], R.wz, R.z, band)

    def back_out(k, band):
        arrived("o", k)
        project(R, R.g, R.wo, R.dh, band)

    for k, band in enumerate(order):
        op(f"px {k}")(functools.partial(inner_x, k, band))
        op(f"inside {k}")(functools.partial(inside_forward, R, per_band, band))
        op(f"pz {k}")(functools.partial(inner_z, k, band))
        op(f"dh {k}")(functools.partial(back_out, k, band))

    def states_of(ks):
        local_states(R, [order[k] for k in ks])

        @pl.when(early)
        def _():
            for k in ks:
                forward.run(k, order[k])

    op("ls 0")(lambda: states_of(range(BANDS // 2)))
    op("ls 1")(lambda: states_of(range(BANDS // 2, BANDS)))

    @op("cf")
    def _():
        @pl.when(jnp.logical_not(early))
        def _():
            for k, band in enumerate(order):
                forward.run(k, band)

        carried_forward(R)
        forward.sent(order)

    op("gf")(lambda: gate_forward(R))

    @op("bo")
    def _():
        branch_out(R)
        layer_copy.start()


    scatters = {}

    def gradient(name, left, right, out):
        grad_of(left, right, out)
        if fused:
            scatters[name].start_c()

    op("go")(lambda: gradient("go", R.gT, R.hidden, R.go))
    op("gz")(lambda: gradient("gz", R.xnT, R.dz, R.gz))
    op("gb 0")(lambda: gate_backward(R, 0, 2))
    op("gb 1")(lambda: gate_backward(R, 1, 2))

    @op("adj")
    def _():
        backward_start(R)
        local_adjoints(R)

        @pl.when(jnp.logical_not(early))
        def _():
            for k, (_, band) in enumerate(back):
                backward.run(k, band)

    for k, (_, band) in enumerate(back):
        op(f"ib {k}")(functools.partial(inside_backward, R, per_band, band))

    @op("chain")
    def _():
        @pl.when(early)
        def _():
            for k, (_, band) in enumerate(back):
                backward.run(k, band)

    for which, name in enumerate(("cbA", "cbB")):
        for i in range(length // Q):
            op(f"{name} {i}")(functools.partial(carried_backward, R, i, groups[which]))

    def send_halo(which):
        for part, copy in zip(pre_parts[which], pre_copies[which]):
            R.dpre_out[:, lanes(*part)] = R.dpre[0:HALO, lanes(*part)].astype(BF16)

            @pl.when(jnp.logical_not(first))
            def _():
                copy.start()

    def back_through_conv(which):
        for part, copy in zip(pre_parts[which], pre_copies[which]):

            @pl.when(jnp.logical_not(last))
            def _():
                copy.wait_recv()

            conv_backward(R, taps, *part)

    def inner_gradient(which):
        for k, band in back[: BANDS // 2] if which == 0 else back[BANDS // 2 :]:
            project(R, R.xnT, R.dconv, R.gx, band)
            if fused:
                scatters["gx"].start_c([k])

    @op("sg")
    def _():
        backward.sent([band for _, band in back])
        step_grads(R)
        send_halo(1)

    op("hA")(lambda: send_halo(0))
    op("cvA")(lambda: back_through_conv(0))
    op("cv")(lambda: back_through_conv(1))
    op("gxA")(lambda: inner_gradient(0))
    op("gx")(lambda: inner_gradient(1))

    @op("gbd")
    def _():
        R.gbc[...] = dot(R.xnT[...], R.dconv[:, inner:]).astype(R.gbc.dtype)
        R.gdt[...] = dot_nt(R.d_raw[...].T, R.xnT[...])[0 : R.gdt.shape[0], :].astype(R.gdt.dtype)
        if fused:
            scatters["bc"].start_c()
            dts.start(0, p.core)

    op("i1")(lambda: input_first(R))
    op("i2")(lambda: input_second(R))

    @op("i3")
    def _():
        input_last(R)
        input_copy.start()

    @op("ss")
    def _():
        small_sums(R)
        if fused:
            vecs.start(0, p.core, vec_half(1 - p.c))

    if fused:
        grid = Grid(lambda a, band: rows * a, lambda band: cols * band, half, rows // 8, cols)
        bc_rows = rows // p.bands
        bc_grid = Grid(lambda a, band: rows * a + bc_rows * band, lambda band: 0, bc_rows // 2, 16, R.wbc.shape[1])
        for name, grad, where, space in (
            ("go", R.go, grid, "so"), ("gz", R.gz, grid, "sz"), ("gx", R.gx, grid, "sx"), ("bc", R.gbc, bc_grid, "sbc"),
        ):
            scatters[name] = Scatter(wires, p, grad, where, [getattr(R, f"{space}{i}") for i in range(6)], name != "bc")
        for name, out in (("go", R.oo), ("gz", R.oz), ("gx", R.ox)):
            scatter = scatters[name]
            for k in range(p.bands):
                op(f"sY {name} {k}")(functools.partial(scatter.start_y, [k]))
                op(f"sX {name} {k}")(functools.partial(scatter.start_x, [k]))
                op(f"sZ {name} {k}")(functools.partial(scatter.start_z, [k]))
            op(f"sL {name}")(scatter.start_last)
            op(f"sS {name}")(functools.partial(scatter.start_share, out))
            op(f"sE {name}")(functools.partial(scatter.finish, out))

        dts = Exchange(wires, p, R.gdt, [R.dt_c, R.dt_y, R.dt_x])
        vecs = Exchange(wires, p, R.vec, [R.vec_c, R.vec_y, R.vec_x])
        dtg_z, vec_z, bcg_z, bcg_c = ([wires.new() for _ in range(p.bands)] for _ in range(4))
        vec_lanes = lambda c: lanes(R.vec.shape[1] // 2 * c, R.vec.shape[1] // 2)
        vec_half = lambda c: R.vec.at[:, vec_lanes(c)]
        vec_s = wires.new()
        dt_cols = lambda a: R.gdt.at[:, lanes(rows * a, rows)]
        dt_rows = lambda band: R.gdt.at[at(SLOTS * band, SLOTS), lanes(rows * p.a, rows)]
        bc_out = lambda band, c: R.obc.at[at(bc_rows * band + bc_rows // 2 * c, bc_rows // 2), :]

        op("bY")(lambda: scatters["bc"].start_y())
        op("bX")(lambda: scatters["bc"].start_x())
        op("bZ")(lambda: scatters["bc"].start_z())
        op("bL")(lambda: scatters["bc"].start_last())

        @op("bG")
        def _():
            scatters["bc"].result(R.obc, bc_rows * p.b + bc_rows // 2 * p.c)
            for k in range(1, p.bands):
                wires.start(bc_out(p.b, p.c), bc_out(p.b, p.c), bcg_z[k], p.over_z(k))
            wires.start(bc_out(p.b, p.c), bc_out(p.b, p.c), bcg_c[0], p.core)

        @op("bS")
        def _():
            for k in range(1, p.bands):
                spot = bc_out(p.band(-k), p.c)
                wires.arrived(spot, bcg_z[k], p.over_z(k))
                wires.start(spot, spot, bcg_c[k], p.core)

        @op("bE")
        def _():
            for k in range(p.bands):
                wires.arrived(bc_out(p.band(-k), 1 - p.c), bcg_c[k], p.core)

        @op("dY")
        def _():
            dts.add(0, p.core)
            dts.start(1, p.over_y)

        @op("dX")
        def _():
            dts.add(1, p.over_y)
            dts.start(2, p.over_x, dt_cols(1 - p.a))

        @op("dZ")
        def _():
            dts.add(2, p.over_x, dt_cols(p.a))
            for k in range(1, p.bands):
                wires.start(dt_rows(p.band(k)), R.dt_zs.at[k], dtg_z[k], p.over_z(k))

        @op("dE")
        def _():
            total = dt_rows(p.b)[...].astype(F32)
            for k in range(1, p.bands):
                wires.arrived(R.dt_zs.at[k], dtg_z[k], p.over_z(k))
                total = total + R.dt_zs[k].astype(F32)
            R.odt[...] = total

        @op("vY")
        def _():
            vecs.add(0, p.core, vec_half(p.c))
            vecs.start(1, p.over_y, vec_half(p.c))

        @op("vX")
        def _():
            vecs.add(1, p.over_y, vec_half(p.c))
            vecs.start(2, p.over_x, vec_half(p.c))

        @op("vZ")
        def _():
            vecs.add(2, p.over_x, vec_half(p.c))
            R.vec_zs[p.b] = R.vec[:, vec_lanes(p.c)]
            for k in range(1, p.bands):
                wires.start(vec_half(p.c), R.vec_zs.at[p.b], vec_z[k], p.over_z(k))

        @op("vS")
        def _():
            for k in range(1, p.bands):
                wires.arrived(R.vec_zs.at[p.band(-k)], vec_z[k], p.over_z(k))
            total = R.vec_zs[0]
            for band in range(1, p.bands):
                total = total + R.vec_zs[band]
            mine = R.ovec.at[:, vec_lanes(p.c)]
            mine[...] = total
            wires.start(mine, mine, vec_s, p.core)

        @op("vE")
        def _():
            wires.arrived(R.ovec.at[:, vec_lanes(1 - p.c)], vec_s, p.core)
            R.oband[...] = R.ovec[:, grid.cols(p.b)]
            by_lane = [R.ovec[5:6, inner : inner + LANES], R.ovec[5:6, inner + LANES :], R.ovec[6:7, width : width + LANES]]
            by_lane = jnp.concatenate([*by_lane, jnp.zeros((5, LANES), F32)], axis=0)
            R.oheads[...] = pltpu.roll(by_lane, lax.rem(LANES - SLOTS * p.b, LANES), 1)

    do = Steps(ops)
    wx, wz, wo, go, gz, gx = "x", "z", "o", "go", "gz", "gx"
    do.spread(); do.GZ(wx, 1); do.dt1(); do.small(); do.GZ(wx, 2); do.X(wx, 1); do.halo(); do.GZ(wx, 3)
    do.bc1(); do.Y(wx, 0); do.X(wx, 2); do.bc(); do.Y(wx, 1); do.GZ(wz, 1); do.C(wx, 0); do.X(wx, 3)
    do.steps(); do.Y(wx, 2); do.GX0(wz, 0); do.GZ(wz, 2); do.px(0); do.C(wx, 1); do.Y(wx, 3); do.X(wz, 1)
    do.GZ(wz, 3); do.inside(0); do.C(wx, 2); do.px(1); do.Y(wz, 0); do.X(wz, 2); do.ls(0); do.C(wx, 3)
    do.Y(wz, 1); do.GZ(wo, 1); do.px(2); do.X(wz, 3); do.px(3); do.Y(wz, 2); do.GZ(wo, 2); do.C(wz, 0)
    do.GX0(wo, 0); do.ls(1); do.inside(2); do.X(wo, 1); do.pz(0); do.C(wz, 1); do.Y(wz, 3); do.GZ(wo, 3)
    do.inside(1); do.C(wz, 2); do.inside(3); do.Y(wo, 0); do.pz(1); do.X(wo, 2); do.pz(2); do.C(wz, 3)
    do.Y(wo, 1); do.cf(); do.X(wo, 3); do.pz(3); do.C(wo, 0); do.gf(); do.Y(wo, 2); do.C(wo, 1); do.go()
    do.Y(wo, 3); do.dh(1); do.C(wo, 2); do.dh(0); do.C(wo, 3); do.sY(go, 2); do.sY(go, 1); do.sY(go, 0)
    do.dh(2); do.dh(3); do.gb(0); do.gb(1); do.gz(); do.sX(go, 2); do.adj(); do.sX(go, 0); do.sY(go, 3)
    do.sX(go, 1); do.ib(3); do.ib(1); do.sY(gz, 0); do.ib(0); do.sY(gz, 3); do.sY(gz, 2); do.bo()
    do.sX(go, 3); do.ib(2); do.sZ(go, 2); do.sX(gz, 0); do.chain(); do.cbA(3); do.cbA(2); do.cbA(1); do.cbA(0)
    do.hA(); do.sZ(go, 1); do.sY(gz, 1); do.sX(gz, 2); do.cbB(3); do.cbB(2); do.cbB(1); do.sX(gz, 3)
    do.sZ(go, 3); do.cvA(); do.gxA(); do.cbB(0); do.sg(); do.sX(gz, 1); do.sZ(go, 0); do.sZ(gz, 2)
    do.sY(gx, 1); do.i1(); do.sY(gx, 2); do.sZ(gz, 3); do.sL(go); do.cv(); do.gbd(); do.gx(); do.sX(gx, 1)
    do.sZ(gz, 1); do.bY(); do.i2(); do.sY(gx, 3); do.sX(gx, 2); do.i3(); do.ss(); do.sZ(gx, 1); do.bX()
    do.sY(gx, 0); do.sZ(gz, 0); do.vY(); do.sX(gx, 3); do.sZ(gx, 2); do.sL(gz); do.vX(); do.bZ(); do.sS(go)
    do.sX(gx, 0); do.dY(); do.sZ(gx, 3); do.bL(); do.sS(gz); do.vZ(); do.sE(go); do.sZ(gx, 0); do.dX()
    do.sL(gx); do.bG(); do.vS(); do.dZ(); do.bS(); do.sS(gx); do.vE(); do.dE(); do.sE(gz); do.bE(); do.sE(gx)
    assert not ops, sorted(ops)

    layer_copy.wait()
    input_copy.wait()
    wires.drain()

    @pl.when(jnp.logical_not(last))
    def _():
        x_copy.wait_send()

    @pl.when(jnp.logical_not(first))
    def _():
        for copy in sum(pre_copies, []):
            copy.wait_send()


def hand_out(taps, names, *refs):
    count = len(names)
    came, refs = refs[:count], refs[count:]
    (
        layer_to, input_to, norm_gain, zx, bc, dt, x_kernel, x_offset, bc_kernel, bc_offset,
        dt_bias, a_log, d_skip, gate_gain, out_to,
    ) = refs[:15]
    here, (zx_via, out_via, bc_via, in_sem, out_sem) = refs[15 : 15 + count], refs[15 + count :]
    R = types.SimpleNamespace(**dict(zip(names, here)))
    loads = {name: pltpu.make_async_copy(a, b, in_sem.at[i]) for i, (name, a, b) in enumerate(zip(names, came, here))}
    stores = [
        pltpu.make_async_copy(*pair, out_sem.at[i])
        for i, pair in enumerate(((zx_via, zx), (out_via, out_to), (R.input_to, input_to), (R.layer_to, layer_to), (bc_via, bc)))
    ]
    first = ("oz", "ox", "oo", "input_to", "layer_to")
    for name in (*first, *(name for name in names if name not in first)):
        loads[name].start()
    loads["oz"].wait()
    zx_via[:, 0, :] = R.oz[...].astype(F32)
    loads["ox"].wait()
    zx_via[:, 1, :] = R.ox[...].astype(F32)
    stores[0].start()
    loads["oo"].wait()
    out_via[...] = R.oo[...].astype(F32)
    stores[1].start()
    for name, store in (("input_to", stores[2]), ("layer_to", stores[3])):
        loads[name].wait()
        store.start()
    for name in names:
        if name not in first:
            loads[name].wait()
    state = bc.shape[2]
    inner, width = R.ovec.shape[1] - 2 * state, R.layer_to.shape[1]
    for half in range(2):
        cols = pl.ds(half * state, state)
        bc_via[:, half, :] = R.obc[:, cols].astype(F32)
        cols = pl.ds(inner + half * state, state)
        bc_kernel[:, half, :] = R.ovec[0:taps, cols]
        bc_offset[half : half + 1, :] = R.ovec[4:5, cols]
    stores[4].start()
    dt[...] = R.odt[0 : dt.shape[0], :]
    norm_gain[...] = R.ovec[6, 0:width]
    x_kernel[...] = R.oband[0:taps, :]
    x_offset[...] = R.oband[4, :]
    gate_gain[...] = R.oband[5, :]
    for row, ref in enumerate((dt_bias, a_log, d_skip)):
        ref[...] = R.oheads[row, 0 : ref.shape[0]]
    for store in stores:
        store.wait()


def run_layer(fused, ins, head_dim, taps):
    length, width = ins["x_in"].shape
    inner, state2 = ins["inner"], ins["state2"]
    conv = inner + state2
    ins = {k: v for k, v in ins.items() if k not in ("inner", "state2")}
    per_band = inner // head_dim // BANDS
    chunks = length // Q
    weights = dict(
        wz=((width, inner), BF16),
        wx=((width, inner), BF16),
        wbc=((width, state2), BF16),
        wdt=((LANES, width), BF16),
        wo=((width, inner), BF16),
        par=((16, conv), F32),
    )
    grads = dict(
        gz=((width, inner), BF16),
        gx=((width, inner), BF16),
        go=((width, inner), BF16),
        gbc=((width, state2), BF16),
        gdt=((BANDS * SLOTS, width), BF16),
        vec=((8, conv), F32),
    )
    outs = dict(layer_to=((length, width), BF16), input_to=((length, width), F32))
    scratch = dict(
        x=((length, width), BF16),
        g=((length, width), BF16),
        gain=((1, width), F32),
        ex=((LANES, inner), BF16),
        pick=((per_band * Q, LANES), BF16),
        xn=((HALO + length, width), BF16),
        xnT=((width, length), BF16),
        gT=((width, length), BF16),
        inv_rms=((length, 1), F32),
        inv_gate=((length, 1), F32),
        x_halo=((HALO, width), BF16),
        ci=((HALO + length, conv), F32),
        cib=((length, conv), BF16),
        z=((length, inner), F32),
        xh=((length, inner), BF16),
        xt=((length, inner), BF16),
        bm=((length, LANES), BF16),
        cm=((length, LANES), BF16),
        prod=((length, Q), F32),
        prodT=((length, Q), F32),
        slope=((length, conv), BF16),
        rate=((1, LANES), F32),
        heads=((8, LANES), F32),
        dt=((length, LANES), F32),
        dt_sig=((length, LANES), F32),
        dt_low=((length, LANES), BF16),
        tail_low=((length, LANES), BF16),
        exp_low=((length, LANES), BF16),
        logs=((length, LANES), F32),
        logsT=((LANES, length), F32),
        ends=((8, LANES), F32),
        decx=((8, inner), F32),
        kept=((8, inner), F32),
        expx=((length, inner), BF16),
        states=((2 * chunks * LANES, inner), BF16),
        piece=((LANES, inner), F32),
        piece_decay=((1, inner), F32),
        outgoing=((LANES, inner), BF16),
        from_before=((LANES, inner), BF16),
        from_after=((LANES, inner), BF16),
        dh=((length, inner), BF16),
        gated=((length, inner), BF16),
        hidden=((length, inner), BF16),
        gain_acc=((8, inner), F32),
        skip_acc=((8, inner), F32),
        norm_acc=((8, width), F32),
        rate_acc=((8, LANES), F32),
        bias_acc=((8, LANES), F32),
        pulls=((length, LANES), F32),
        pullsT=((LANES, length), F32),
        d_prod=((length, Q), F32),
        d_log=((length, LANES), F32),
        d_tail=((length, LANES), F32),
        direct=((length, LANES), F32),
        db=((length, LANES), F32),
        dc=((length, LANES), F32),
        d_raw=((length, LANES), BF16),
        dpre_out=((HALO, conv), BF16),
        dpre_halo=((HALO, conv), BF16),
    )
    if fused:
        rows, cols = ins["w_out"].shape
        bands = inner // cols
        outs.update(
            oz=((rows, cols), BF16),
            ox=((rows, cols), BF16),
            oo=((rows, cols), BF16),
            obc=((rows, state2), BF16),
            odt=((SLOTS, rows), F32),
            ovec=((8, conv), F32),
            oband=((8, cols), F32),
            oheads=((8, LANES), F32),
        )
        scratch.update(weights)
        scratch.update({k: v for k, v in grads.items() if k != "gx"})
        main = Scatter.spaces(bands, Grid(None, None, rows // 2, rows // 8, cols))
        small = Scatter.spaces(bands, Grid(None, None, rows // bands // 2, 16, state2))
        for name, shapes in (("so", main), ("sz", main), ("sx", main), ("sbc", small)):
            scratch.update({f"{name}{i}": (shape, BF16) for i, shape in enumerate(shapes)})
        scratch.update(
            dt_c=((BANDS * SLOTS, width), BF16),
            dt_y=((BANDS * SLOTS, width), BF16),
            dt_x=((BANDS * SLOTS, rows), BF16),
            dt_zs=((bands, SLOTS, rows), BF16),
            vec_c=((8, conv // 2), F32),
            vec_y=((8, conv // 2), F32),
            vec_x=((8, conv // 2), F32),
            vec_zs=((bands, 8, conv // 2), F32),
        )
    else:
        outs.update(grads)
    names = (*ins, *outs, *scratch, "send_sem", "recv_sem", "local_sem")
    results = pl.pallas_call(
        functools.partial(layer, names, fused, head_dim, taps),
        out_shape=[jax.ShapeDtypeStruct(*v) for v in outs.values()],
        in_specs=[pl.BlockSpec(memory_space=pl.ANY if name in ("x_in", "g_in", "w_out") else pltpu.VMEM) for name in ins],
        out_specs=[pl.BlockSpec(memory_space=pl.ANY if name in ("layer_to", "input_to") else pltpu.VMEM) for name in outs],
        scratch_shapes=[pltpu.VMEM(*v) for v in scratch.values()]
        + [pltpu.SemaphoreType.DMA((SEMS,)), pltpu.SemaphoreType.DMA((SEMS,)), pltpu.SemaphoreType.DMA((8,))],
        compiler_params=pltpu.CompilerParams(
            collective_id=0, has_side_effects=True, vmem_limit_bytes=VMEM_BYTES
        ),
    )(*ins.values())
    return dict(zip(outs, results))


VMEM_BYTES = 64 * 2**20 - 2**18


def body(residual, cotangent, norm_gain, w_zx, w_bc, w_dt, x_kernel, x_offset, bc_kernel, bc_offset, dt_bias, a_log, d_skip, gate_gain, w_out):
    _, length, width = residual.shape
    bands = lax.axis_size("wb")
    rows_own, heads_own, inner_own, state = w_zx.shape[0], w_dt.shape[1], w_zx.shape[2], w_bc.shape[2]
    heads, inner = heads_own * bands, inner_own * bands
    head_dim = inner_own // heads_own
    taps = x_kernel.shape[0]
    fused = (lax.axis_size("seq"), lax.axis_size("wa"), bands) == (4, 2, BANDS) and inner_own % LANES == 0
    per = heads // BANDS
    ins = dict(
        x_in=residual.reshape(length, width),
        g_in=cotangent.reshape(length, width),
        norm_gain=norm_gain,
        inner=inner,
        state2=2 * state,
    )

    if fused:
        ins.update(
            w_zx=w_zx, w_out=w_out, w_bc=w_bc, w_dt=w_dt.T, x_kernel=x_kernel, x_offset=x_offset,
            bc_kernel=bc_kernel, bc_offset=bc_offset, dt_bias=dt_bias, a_log=a_log, d_skip=d_skip, gate_gain=gate_gain,
        )
        out = run_layer(True, ins, head_dim, taps)
        any_space, vmem = pl.BlockSpec(memory_space=pl.ANY), pl.BlockSpec(memory_space=pltpu.VMEM)
        shapes = [
            ((length, width), BF16), ((length, width), F32), ((width,), F32), (w_zx.shape, F32), (w_bc.shape, F32),
            (w_dt.shape[::-1], F32), (x_kernel.shape, F32), (x_offset.shape, F32), (bc_kernel.shape, F32),
            (bc_offset.shape, F32), (dt_bias.shape, F32), (a_log.shape, F32), (d_skip.shape, F32), (gate_gain.shape, F32),
            (w_out.shape, F32),
        ]
        results = pl.pallas_call(
            functools.partial(hand_out, taps, tuple(out)),
            out_shape=[jax.ShapeDtypeStruct(*shape) for shape in shapes],
            in_specs=[any_space] * len(out),
            out_specs=[any_space if i in (0, 1, 3, 4, 14) else vmem for i in range(15)],
            scratch_shapes=[pltpu.VMEM(value.shape, value.dtype) for value in out.values()]
            + [pltpu.VMEM(shape, F32) for shape in (w_zx.shape, w_out.shape, w_bc.shape)]
            + [pltpu.SemaphoreType.DMA((len(out),)), pltpu.SemaphoreType.DMA((5,))],
            compiler_params=pltpu.CompilerParams(vmem_limit_bytes=VMEM_BYTES),
        )(*out.values())
        results = list(results)
        results[0] = results[0].reshape(residual.shape)
        results[1] = results[1].reshape(residual.shape)
        results[5] = results[5].T
        return tuple(results)

    own = jnp.concatenate(
        [x_kernel.astype(F32), x_offset.astype(F32)[None], gate_gain.astype(F32)[None], jnp.repeat(d_skip, head_dim)[None]]
    )
    par_bc = jnp.concatenate([bc_kernel.reshape(taps, 2 * state), bc_offset.reshape(1, 2 * state)], axis=0).astype(F32)
    par_bc = jnp.pad(par_bc, ((0, 16 - taps - 1), (0, 0)))
    wzx = lax.all_gather(lax.all_gather(w_zx, "wa", axis=0, tiled=True), "wb", axis=2, tiled=True)
    wdt = lax.all_gather(lax.all_gather(w_dt, "wa", axis=0, tiled=True), "wb", axis=1, tiled=True)
    wdt = jnp.pad(wdt.T.reshape(BANDS, per, width), ((0, 0), (0, SLOTS - per), (0, 0))).reshape(-1, width)
    small = lax.all_gather(jnp.stack([dt_bias, a_log]), "wb", axis=1, tiled=True).reshape(2, BANDS, per)
    small = jnp.pad(small, ((0, 6), (0, 0), (0, inner // BANDS - per))).reshape(8, inner)
    wide = jnp.pad(lax.all_gather(own, "wb", axis=1, tiled=True), ((0, 1), (0, 0)))
    ins.update(
        wz=wzx[:, 0],
        wx=wzx[:, 1],
        wo=lax.all_gather(lax.all_gather(w_out, "wa", axis=0, tiled=True), "wb", axis=1, tiled=True),
        wbc=lax.all_gather(w_bc, "wa", axis=0, tiled=True).reshape(width, 2 * state),
        wdt=jnp.pad(wdt, ((0, LANES - BANDS * SLOTS), (0, 0))),
        par=jnp.concatenate([jnp.concatenate([wide, small], axis=0), par_bc], axis=1),
    )
    out = run_layer(False, ins, head_dim, taps)

    def share(grad, columns=True):
        grad = lax.psum_scatter(grad.astype(F32), "wa", scatter_dimension=0, tiled=True)
        if columns:
            grad = lax.psum_scatter(grad, "wb", scatter_dimension=grad.ndim - 1, tiled=True)
        else:
            grad = lax.psum(grad, "wb")
        return lax.psum(grad, "seq")

    gdt = out["gdt"].reshape(BANDS, SLOTS, width)[:, :per].reshape(heads, width)
    vec = lax.psum(out["vec"], ("seq", "wa", "wb"))
    mine = lax.axis_index("wb")
    band = lax.dynamic_slice_in_dim(vec[:, :inner], mine * inner_own, inner_own, 1)
    by_head = jnp.stack([vec[5, inner : inner + LANES], vec[5, inner + LANES :], vec[6, width : width + LANES]])
    by_head = by_head[:, : BANDS * SLOTS].reshape(3, BANDS, SLOTS)[:, :, :per].reshape(3, heads)
    by_head = lax.dynamic_slice_in_dim(by_head, mine * heads_own, heads_own, 1)
    return (
        out["layer_to"].reshape(residual.shape),
        out["input_to"].reshape(residual.shape),
        vec[6, :width],
        share(jnp.stack([out["gz"], out["gx"]], axis=1)),
        share(out["gbc"], False).reshape(-1, 2, state),
        share(gdt.T),
        band[0:taps],
        band[4],
        vec[0:taps, inner:].reshape(taps, 2, state),
        vec[4, inner:].reshape(2, state),
        by_head[0],
        by_head[1],
        by_head[2],
        band[5],
        share(out["go"]),
    )


def solution(mesh):
    batch = P(("wa", "wb"), "seq", None)
    ins = (
        batch, batch, P(), P("wa", None, "wb"), P("wa", None, None), P("wa", "wb"), P(None, "wb"), P("wb"), P(), P(),
        P("wb"), P("wb"), P("wb"), P("wb"), P("wa", "wb"),
    )
    outs = (
        batch, batch, P(), P("wa", None, "wb"), P("wa", None, None), P("wa", "wb"), P(None, "wb"), P("wb"), P(), P(),
        P("wb"), P("wb"), P("wb"), P("wb"), P("wa", "wb"),
    )
    return jax.shard_map(body, mesh=mesh, in_specs=ins, out_specs=outs, check_vma=False)
```

```python
import functools
import types

import jax
import jax.numpy as jnp
from jax import lax
from jax.experimental import pallas as pl
from jax.experimental.pallas import tpu as pltpu
from jax.sharding import PartitionSpec as P

F32, BF16 = jnp.float32, jnp.bfloat16
EPSILON = 1e-05
Q = 128
LANES = 128
HALO = 16
SLOTS = 16
TILE = 256
BANDS = 4
NT = (((1,), (1,)), ((), ()))


def dot(a, b):
    return jnp.dot(a, b, preferred_element_type=F32)


def dot_nt(a, b):
    return lax.dot_general(a, b, NT, preferred_element_type=F32)


def dot_exact(a, b):
    return jnp.dot(a, b, precision=lax.Precision.HIGHEST, preferred_element_type=F32)


def sigmoid(v):
    return 0.5 + 0.5 * jnp.tanh(0.5 * v)


def fold8(v):
    return v.reshape(v.shape[0] // 8, 8, v.shape[1]).sum(axis=0)


def at(start, size):
    return pl.ds(pl.multiple_of(start, 16), size)


def lanes(start, size):
    return pl.ds(pl.multiple_of(start, LANES), size)


def rows_at(i, size=Q, base=0):
    return at(i * size + base, size)


def cols_at(i, size=LANES):
    return lanes(i * size, size)


def band_cols(R, band):
    width = R.wx.shape[1] // BANDS
    return lanes(width * band, width)


class Columns:
    def __init__(self, R, bands):
        self.parts = [band_cols(R, band) for band in bands]
        self.width = R.wx.shape[1] // BANDS

    def get(self, ref, rows=slice(None)):
        return jnp.concatenate([ref[rows, cols] for cols in self.parts], axis=1)

    def put(self, ref, rows, value):
        for n, cols in enumerate(self.parts):
            ref[rows, cols] = value[:, n * self.width : (n + 1) * self.width]


def head_spread(R, head_dim):
    inner = R.ex.shape[1]
    per_band = inner // BANDS
    row = lax.broadcasted_iota(jnp.int32, (LANES, LANES), 0)

    @pl.loop(0, inner // LANES)
    def _(c):
        lane = lax.broadcasted_iota(jnp.int32, (LANES, LANES), 1) + c * LANES
        hit = jnp.zeros((LANES, LANES), jnp.bool_)
        for band in range(BANDS):
            first = lane - band * per_band
            inside = (first >= 0) & (first < per_band)
            head = lax.shift_right_arithmetic(first, head_dim.bit_length() - 1)
            hit = hit | (inside & (row == band * SLOTS + head))
        R.ex[:, cols_at(c)] = jnp.where(hit, 1.0, 0.0).astype(BF16)

    lane = lax.broadcasted_iota(jnp.int32, (Q, LANES), 1)
    for head in range(R.pick.shape[0] // Q):
        R.pick[pl.ds(head * Q, Q), :] = jnp.where(lane == head, 1.0, 0.0).astype(BF16)


def norm_rows(R):
    gain = R.gain[...]

    @pl.loop(0, R.x.shape[0] // Q)
    def _(i):
        rows = R.x[rows_at(i), :].astype(F32)
        inv = lax.rsqrt(jnp.mean(rows * rows, axis=-1, keepdims=True) + EPSILON)
        value = (rows * inv * gain).astype(BF16)
        R.xn[rows_at(i, base=HALO), :] = value
        R.inv_rms[rows_at(i), :] = inv
        R.xnT[:, cols_at(i)] = value.T
        R.gT[:, cols_at(i)] = R.g[rows_at(i), :].T


def norm_halo(R):
    rows = R.x_halo[...].astype(F32)
    inv = lax.rsqrt(jnp.mean(rows * rows, axis=-1, keepdims=True) + EPSILON)
    R.xn[0:HALO, :] = (rows * inv * R.gain[...]).astype(BF16)


def project(R, left, right, out, band):
    cols = band_cols(R, band)
    out[:, cols] = dot(left[...], right[:, cols]).astype(out.dtype)


def grad_of(left, right, out):
    for j in range(out.shape[1] // (2 * TILE)):
        cols = pl.ds(j * 2 * TILE, 2 * TILE)
        out[:, cols] = dot(left[...], right[:, cols]).astype(out.dtype)


def project_bc(R):
    R.ci[:, R.wx.shape[1] :] = dot(R.xn[...], R.wbc[...])


def conv_tile(R, taps, cols, put):
    for i in range(R.x.shape[0] // Q):
        rows = pl.ds(i * Q, Q)
        pre = R.par[4:5, cols]
        for k in range(taps):
            conv_in = R.ci[pl.ds(HALO - (taps - 1) + k + i * Q, Q), cols]
            pre = pre + R.par[k : k + 1, cols] * conv_in
        R.cib[rows, cols] = conv_in.astype(BF16)
        sig = sigmoid(pre)
        act = pre * sig
        put(rows, act.astype(BF16))
        R.slope[rows, cols] = (sig + act * (1.0 - sig)).astype(BF16)


def convolve(R, taps, band):
    width = R.wx.shape[1] // BANDS
    for c in range(width // LANES):
        cols = lanes(width * band + c * LANES, LANES)

        def put(rows, act):
            R.xh[rows, cols] = act

        conv_tile(R, taps, cols, put)
    for i in range(R.x.shape[0] // Q):
        rows, cols = pl.ds(i * Q, Q), band_cols(R, band)
        dt = dot(R.dt_low[rows, :], R.ex[:, cols])
        R.xt[rows, cols] = (R.xh[rows, cols].astype(F32) * dt).astype(BF16)


def convolve_bc(R, taps):
    inner = R.wx.shape[1]

    def put_b(rows, act):
        R.bm[rows, :] = act

    def put_c(rows, act):
        R.cm[rows, :] = act

    conv_tile(R, taps, pl.ds(inner, LANES), put_b)
    conv_tile(R, taps, pl.ds(inner + LANES, LANES), put_c)

    for i in range(R.x.shape[0] // Q):
        rows = pl.ds(i * Q, Q)
        R.prod[rows, :] = dot_nt(R.cm[rows, :], R.bm[rows, :])
        R.prodT[rows, :] = dot_nt(R.bm[rows, :], R.cm[rows, :])


def lower_ones(strict=False):
    row = lax.broadcasted_iota(jnp.int32, (Q, Q), 0)
    col = lax.broadcasted_iota(jnp.int32, (Q, Q), 1)
    return jnp.where(row > col if strict else row >= col, 1.0, 0.0).astype(F32)


def step_sizes(R, per_band):
    cols = R.wx.shape[1] // BANDS
    lane = lax.broadcasted_iota(jnp.int32, (8, LANES), 1)
    heads = jnp.zeros((8, LANES), F32)
    for band in range(BANDS):
        block = R.par[8:16, pl.ds(band * cols, LANES)]
        heads = heads + pltpu.roll(jnp.where(lane < per_band, block, 0.0), band * SLOTS, 1)
    R.heads[...] = heads
    R.rate[...] = -jnp.exp(R.heads[1:2, :])
    bias, rate = R.heads[0:1, :], R.rate[...]
    ones = lower_ones()
    chunks = R.x.shape[0] // Q
    R.ends[...] = jnp.zeros_like(R.ends)
    for i in range(chunks):
        rows = pl.ds(i * Q, Q)
        v = dot_nt(R.xn[pl.ds(HALO + i * Q, Q), :], R.wdt[...]) + bias
        dt = jnp.maximum(v, 0.0) + jnp.log1p(jnp.exp(-jnp.abs(v)))
        R.dt[rows, :] = dt
        R.dt_sig[rows, :] = jax.nn.sigmoid(v)
        logs = dot_exact(ones, dt * rate)
        R.logs[rows, :] = logs
        R.logsT[:, rows] = logs.T
        last = logs[Q - 1 : Q, :]
        R.ends[i : i + 1, :] = last
        R.dt_low[rows, :] = dt.astype(BF16)
        R.tail_low[rows, :] = jnp.exp(last - logs).astype(BF16)
        R.exp_low[rows, :] = jnp.exp(logs).astype(BF16)
    decay = jnp.exp(R.ends[...])
    high = decay.astype(BF16)
    low = (decay - high.astype(F32)).astype(BF16)
    R.decx[...] = dot(high, R.ex[...]) + dot(low, R.ex[...])


def local_states(R, bands):
    chunks = R.x.shape[0] // Q
    columns = Columns(R, bands)
    get, put = columns.get, columns.put
    spread = get(R.ex)
    total = decay = None
    for i in range(chunks):
        rows = pl.ds(i * Q, Q)
        ended = get(R.xt, rows).astype(F32) * dot(R.tail_low[rows, :], spread)
        fresh = dot(R.bm[rows, :].T, ended.astype(BF16))
        put(R.sl, rows_at(i, LANES), fresh.astype(BF16))
        step = get(R.decx, slice(i, i + 1))
        total = fresh if total is None else total * step + fresh
        decay = step if decay is None else decay * step
    put(R.piece, slice(None), total)
    put(R.piece_decay, slice(None), decay)


def halves(value):
    first = lax.broadcasted_iota(jnp.int32, value.shape, 1) < LANES // 2
    zero = jnp.zeros_like(value)
    return jnp.concatenate([jnp.where(first, value, zero), jnp.where(first, zero, value)], axis=0)


def causal_mask(by_row):
    row = lax.broadcasted_iota(jnp.int32, (Q, Q), 0)
    col = lax.broadcasted_iota(jnp.int32, (Q, Q), 1)
    return row >= col if by_row else row <= col


def band_logs(R, rows, band):
    return pltpu.roll(R.logs[rows, :], lax.rem(LANES - SLOTS * band, LANES), 1)


def inside_forward(R, per_band, band):
    width = R.wx.shape[1] // BANDS
    causal = causal_mask(True)
    for i in range(R.x.shape[0] // Q):
        rows = pl.ds(i * Q, Q)
        logs = band_logs(R, rows, band)
        logsT = R.logsT[at(SLOTS * band, 8), rows]
        for pair in range(per_band // 2):
            cols = lanes(width * band + pair * LANES, LANES)
            mixes = []
            for head in (2 * pair, 2 * pair + 1):
                gap = logs[:, head : head + 1] - logsT[head : head + 1, :]
                decay = jnp.exp(jnp.where(causal, gap, -1e30))
                mixes.append((R.prod[rows, :] * decay).astype(BF16))
            R.y[rows, cols] = dot(jnp.concatenate(mixes, axis=1), halves(R.xt[rows, cols]))


def carried_forward(R):
    chunks = R.x.shape[0] // Q
    state = R.from_before[...].astype(F32)
    for i in range(chunks):
        rows = pl.ds(i * Q, Q)
        block = rows_at(i, LANES)
        low = state.astype(BF16)
        R.s_in[block, :] = low
        spread = dot(R.exp_low[rows, :], R.ex[...])
        R.expx[rows, :] = spread.astype(BF16)
        R.y[rows, :] += dot(R.cm[rows, :], low) * spread
        if i < chunks - 1:
            state = state * R.decx[i : i + 1, :] + R.sl[block, :].astype(F32)


def gate_forward(R):
    inner = R.wx.shape[1]
    block = 64

    @pl.loop(0, R.x.shape[0] // block)
    def _(i):
        rows = rows_at(i, block)
        squares = jnp.zeros((block, LANES), F32)
        for c in range(inner // LANES):
            cols = pl.ds(c * LANES, LANES)
            y = R.y[rows, cols] + R.par[6:7, cols] * R.xh[rows, cols].astype(F32)
            R.y[rows, cols] = y
            z = R.z[rows, cols]
            gated = (y * (z * sigmoid(z))).astype(BF16)
            R.gated[rows, cols] = gated
            gated = gated.astype(F32)
            squares = squares + gated * gated
        inv = lax.rsqrt(jnp.sum(squares, axis=-1, keepdims=True) / inner + EPSILON)
        R.inv_gate[rows, :] = inv
        inv = jnp.broadcast_to(inv, (block, LANES))
        for c in range(inner // LANES):
            cols = pl.ds(c * LANES, LANES)
            R.hidden[rows, cols] = (R.gated[rows, cols].astype(F32) * inv * R.par[5:6, cols]).astype(BF16)


def gate_backward(R, part, parts):
    inner = R.wx.shape[1]
    block = 64
    count = R.x.shape[0] // block // parts
    if part == 0:
        R.gain_acc[...] = jnp.zeros_like(R.gain_acc)
        R.skip_acc[...] = jnp.zeros_like(R.skip_acc)

    @pl.loop(part * count, (part + 1) * count)
    def _(i):
        rows = rows_at(i, block)
        cross = jnp.zeros((block, LANES), F32)
        for c in range(inner // LANES):
            cols = pl.ds(c * LANES, LANES)
            cross = cross + R.gated[rows, cols].astype(F32) * (R.dh[rows, cols].astype(F32) * R.par[5:6, cols])
        inv = R.inv_gate[rows, :]
        cross = jnp.sum(cross, axis=-1, keepdims=True) * (inv * inv * inv / inner)
        inv = jnp.broadcast_to(inv, (block, LANES))
        cross = jnp.broadcast_to(cross, (block, LANES))
        for c in range(inner // LANES):
            cols = pl.ds(c * LANES, LANES)
            gated = R.gated[rows, cols].astype(F32)
            dh = R.dh[rows, cols].astype(F32) * inv
            R.gain_acc[:, cols] += fold8(dh * gated)
            d_gated = dh * R.par[5:6, cols] - gated * cross
            z = R.z[rows, cols]
            sig = sigmoid(z)
            lin = z * sig
            dy = d_gated * lin
            R.dz[rows, cols] = (d_gated * R.y[rows, cols] * (sig + lin * (1.0 - sig))).astype(BF16)
            R.dyl[rows, cols] = (dy * R.expx[rows, cols].astype(F32)).astype(BF16)
            R.dy[rows, cols] = dy.astype(BF16)
            R.skip_acc[:, cols] += fold8(dy * R.xh[rows, cols].astype(F32))


def branch_out(R):
    width = R.x.shape[1]
    for j in range(width // TILE):
        cols = pl.ds(j * TILE, TILE)
        R.layer_out[:, cols] = (
            R.x[:, cols].astype(F32) + dot_nt(R.hidden[...], R.wo[cols, :])
        ).astype(BF16)


def local_adjoints(R):
    chunks = R.x.shape[0] // Q
    total = None
    for i in range(chunks - 1, -1, -1):
        pulled = dot(R.cm[pl.ds(i * Q, Q), :].T, R.dyl[pl.ds(i * Q, Q), :])
        R.dl[rows_at(i, LANES), :] = pulled.astype(BF16)
        total = pulled if total is None else total * R.decx[i : i + 1, :] + pulled
    R.piece[...] = total


def inside_backward(R, per_band, band):
    width = R.wx.shape[1] // BANDS
    causal = causal_mask(False)
    for i in range(R.x.shape[0] // Q):
        rows = pl.ds(i * Q, Q)
        logs = band_logs(R, rows, band)
        logsT = R.logsT[at(SLOTS * band, 8), rows]
        d_prod = R.d_prod[rows, :]
        pulls, sums = [], []
        for pair in range(per_band // 2):
            cols = lanes(width * band + pair * LANES, LANES)
            dy = R.dy[rows, cols]
            d_both = dot_nt(halves(R.xt[rows, cols]), dy)
            mixes = []
            for half in range(2):
                head = 2 * pair + half
                gap = logsT[head : head + 1, :] - logs[:, head : head + 1]
                decay = jnp.exp(jnp.where(causal, gap, -1e30))
                mix = R.prodT[rows, :] * decay
                mixes.append(mix.astype(BF16))
                d_mix = d_both[half * Q : (half + 1) * Q, :]
                d_prod = d_prod + decay * d_mix
                pull = (mix * d_mix).astype(BF16)
                pulls.append(pull)
                sums.append(jnp.sum(pull.astype(F32), axis=0, keepdims=True))
            R.u[rows, cols] = dot(jnp.concatenate(mixes, axis=1), halves(dy))
        R.d_prod[rows, :] = d_prod
        R.pullsT[at(SLOTS * band, 8), rows] = jnp.concatenate([*sums, jnp.zeros((8 - per_band, Q), F32)], axis=0)
        R.pulls[rows, :] += pltpu.roll(dot(jnp.concatenate(pulls, axis=1), R.pick[...]), SLOTS * band, 1)


def backward_start(R):
    for ref in (R.pulls, R.pullsT, R.d_prod, R.d_tail, R.db, R.dc, R.d_log, R.direct):
        ref[...] = jnp.zeros_like(ref)


def carried_backward(R, i, bands):
    columns = Columns(R, bands)
    get, put = columns.get, columns.put
    spread = get(R.ex)
    grad = get(R.from_after).astype(F32) if i == R.x.shape[0] // Q - 1 else get(R.piece)
    rows = pl.ds(i * Q, Q)
    block = rows_at(i, LANES)

    def add(ref, value):
        ref[rows, :] += value

    low = grad.astype(BF16)
    tail = dot(R.tail_low[rows, :], spread)
    xt = get(R.xt, rows).astype(F32)
    pulled = dot(R.bm[rows, :], low) * tail
    u = get(R.u, rows) + pulled
    add(R.d_tail, dot_nt((xt * pulled).astype(BF16), spread))
    add(R.db, dot_nt((xt * tail).astype(BF16), low))
    state = get(R.s_in, block)
    dyl = get(R.dyl, rows)
    add(R.dc, dot_nt(dyl, state))
    add(R.d_log, dot_nt((dyl.astype(F32) * dot(R.cm[rows, :], state)).astype(BF16), spread))
    decay = get(R.decx, slice(i, i + 1))
    put(R.kept, slice(i, i + 1), jnp.sum(grad * state.astype(F32), axis=0, keepdims=True) * decay)
    if i:
        put(R.piece, slice(None), grad * decay + get(R.dl, block).astype(F32))
    add(R.direct, dot_nt((get(R.xh, rows).astype(F32) * u).astype(BF16), spread))
    dx = dot(R.dt_low[rows, :], spread) * u + get(R.par, slice(6, 7)) * get(R.dy, rows).astype(F32)
    put(R.dpre, rows, dx * get(R.slope, rows).astype(F32))


def step_grads(R):
    chunks = R.x.shape[0] // Q
    inner = R.wx.shape[1]
    later = lower_ones().T
    before = lower_ones(strict=True)
    high = R.kept[...].astype(BF16)
    low = (R.kept[...] - high.astype(F32)).astype(BF16)
    kept = dot_nt(high, R.ex[...]) + dot_nt(low, R.ex[...])
    rate_acc = jnp.zeros((8, LANES), F32)
    bias_acc = jnp.zeros((8, LANES), F32)
    for i in range(chunks):
        rows = pl.ds(i * Q, Q)
        sides = R.d_log[rows, :] + R.pullsT[:, rows].T - R.pulls[rows, :]
        d_decay = dot_exact(later, sides) + dot_exact(before, R.d_tail[rows, :]) + kept[i : i + 1, :]
        d_raw = (R.direct[rows, :] + R.rate[...] * d_decay) * R.dt_sig[rows, :]
        rate_acc = rate_acc + fold8(R.dt[rows, :] * d_decay)
        bias_acc = bias_acc + fold8(d_raw)
        R.d_raw[rows, :] = d_raw.astype(BF16)
        d_prod = R.d_prod[rows, :].astype(BF16)
        db = R.db[rows, :] + dot(d_prod, R.cm[rows, :])
        dc = R.dc[rows, :] + dot(d_prod.T, R.bm[rows, :])
        R.dpre[rows, inner : inner + LANES] = db * R.slope[rows, inner : inner + LANES].astype(F32)
        R.dpre[rows, inner + LANES :] = dc * R.slope[rows, inner + LANES :].astype(F32)
    R.rate_acc[...] = rate_acc
    R.bias_acc[...] = bias_acc


def conv_backward(R, taps, first, width):
    length = R.x.shape[0]
    halo = lanes(first, width)
    R.dpre[pl.ds(length, HALO), halo] = R.dpre_halo[:, halo].astype(F32)

    @pl.loop(0, width // LANES)
    def _(c):
        cols = lanes(first + c * LANES, LANES)
        sums = [jnp.zeros((8, LANES), F32) for _ in range(taps + 1)]
        for i in range(length // Q):
            base = i * Q
            conv_in = R.cib[pl.ds(base, Q), cols].astype(F32)
            d_conv = None
            for k in range(taps):
                ahead = R.dpre[pl.ds(base + taps - 1 - k, Q), cols]
                sums[k] = sums[k] + fold8(ahead * conv_in)
                term = R.par[k : k + 1, cols] * ahead
                d_conv = term if d_conv is None else d_conv + term
            sums[taps] = sums[taps] + fold8(ahead)
            R.dconv[pl.ds(base, Q), cols] = d_conv.astype(BF16)
        for k in range(taps + 1):
            R.vec[k : k + 1, cols] = jnp.sum(sums[k], axis=0, keepdims=True)


def input_first(R):
    for j in range(R.x.shape[1] // TILE):
        cols = pl.ds(j * TILE, TILE)
        R.input_grad[:, cols] = dot_nt(R.dz[...], R.wz[cols, :])


def input_second(R):
    inner = R.wx.shape[1]
    for j in range(R.x.shape[1] // TILE):
        cols = pl.ds(j * TILE, TILE)
        R.input_grad[:, cols] += (
            dot_nt(R.dconv[:, 0:inner], R.wx[cols, :])
            + dot_nt(R.dconv[:, inner:], R.wbc[cols, :])
            + dot(R.d_raw[...], R.wdt[:, cols])
        )


def input_last(R):
    width = R.x.shape[1]
    gain = R.gain[...]
    R.norm_acc[...] = jnp.zeros_like(R.norm_acc)

    @pl.loop(0, R.x.shape[0] // 64)
    def _(i):
        rows = rows_at(i, 64)
        d_normed = R.input_grad[rows, :]
        x = R.x[rows, :].astype(F32)
        inv = R.inv_rms[rows, :]
        pulled = d_normed * x
        R.norm_acc[...] += fold8(pulled * inv)
        middle = jnp.sum(pulled * gain, axis=-1, keepdims=True) * (inv * inv * inv / width)
        R.input_grad[rows, :] = R.g[rows, :].astype(F32) + (d_normed * gain) * inv - x * middle


def small_sums(R):
    inner = R.wx.shape[1]
    width = R.gain.shape[1]
    R.vec[5:8, :] = jnp.zeros((3, R.vec.shape[1]), F32)
    R.vec[5:6, 0:inner] = jnp.sum(R.gain_acc[...], axis=0, keepdims=True)
    R.vec[6:7, 0:width] = jnp.sum(R.norm_acc[...], axis=0, keepdims=True)
    R.vec[5:6, inner : inner + LANES] = jnp.sum(R.bias_acc[...], axis=0, keepdims=True)
    R.vec[5:6, inner + LANES :] = jnp.sum(R.rate_acc[...], axis=0, keepdims=True) * R.rate[...]
    skip = R.skip_acc[...]
    high = skip.astype(BF16)
    low = (skip - high.astype(F32)).astype(BF16)
    R.vec[6:7, width : width + LANES] = jnp.sum(
        dot_nt(high, R.ex[...]) + dot_nt(low, R.ex[...]), axis=0, keepdims=True
    )


SEMS = 256
WINDOW = {"x": 3, "y": 4, "z": 2}


class Wires:
    def __init__(self, R):
        self.R, self.used, self.started = R, 0, []
        self.leaving = {link: [] for link in WINDOW}

    def new(self):
        self.used += 1
        return self.used - 1

    def copy(self, src, dst, sem, where):
        return pltpu.make_async_remote_copy(
            src_ref=src,
            dst_ref=dst,
            send_sem=self.R.send_sem.at[sem],
            recv_sem=self.R.recv_sem.at[sem],
            device_id=where,
            device_id_type=pl.DeviceIdType.MESH,
        )

    def start(self, src, dst, sem, where, link=None):
        copy = self.copy(src, dst, sem, where)
        if link is None:
            self.started.append(copy)
        else:
            leaving = self.leaving[link]
            if len(leaving) == WINDOW[link]:
                leaving.pop(0).wait_send()
            leaving.append(copy)
        copy.start()

    def arrived(self, dst, sem, where):
        self.copy(dst, dst, sem, where).wait_recv()

    def drain(self):
        for copy in sum(self.leaving.values(), self.started):
            copy.wait_send()


class Place:
    def __init__(self):
        self.seq, self.a, self.b = lax.axis_index("seq"), lax.axis_index("wa"), lax.axis_index("wb")
        self.bands, self.rows = lax.axis_size("wb"), lax.axis_size("wa")
        self.c = lax.rem(self.seq, 2)
        self.y = lax.div(self.seq, 2)
        self.core = {"seq": self.seq + 1 - 2 * self.c}
        self.over_y = {"seq": lax.rem(self.seq + 2, 4)}
        self.over_x = {"wa": 1 - self.a}

    def band(self, k):
        return lax.rem(self.b + k + self.bands, self.bands)

    def over_z(self, k):
        return {"wb": self.band(k)}

    def greet(self):
        barrier = pltpu.get_barrier_semaphore()
        peers = [{"seq": lax.rem(self.seq + k, 4)} for k in range(1, 4)]
        peers += [self.over_z(k) for k in range(1, self.bands)] + [self.over_x]
        for peer in peers:
            pl.semaphore_signal(barrier, 1, device_id=peer, device_id_type=pl.DeviceIdType.MESH)
        return lambda: pl.semaphore_wait(barrier, len(peers))


class Grid:
    def __init__(self, row, col, half, own, width):
        self.row, self.col, self.half, self.own, self.width = row, col, half, own, width
        self.span = half - own

    def cols(self, band):
        return lanes(self.col(band), self.width)

    def half_rows(self, a, band, c):
        return at(self.row(a, band) + self.half * c, self.half)

    def span_rows(self, a, band, p):
        return at(self.row(a, band) + self.half * p.c + self.own * p.y, self.span)

    def own_rows(self, a, band, p, y):
        return at(self.row(a, band) + self.half * p.c + (self.half - self.own) * y, self.own)


class Gather:
    def __init__(self, wires, p, whole, grid):
        self.w, self.p, self.whole, self.g = wires, p, whole, grid
        self.z = [wires.new() for _ in range(p.bands)]
        self.x = [wires.new() for _ in range(p.bands)]
        self.y = [[wires.new() for _ in range(p.bands)] for _ in range(2)]
        self.c = [[wires.new() for _ in range(p.bands)] for _ in range(2)]

    def here(self, rows, k):
        return self.whole.at[rows, self.g.cols(self.p.band(-k))]

    def start(self):
        mine = self.here(self.g.span_rows(self.p.a, self.p.b, self.p), 0)
        self.w.start(mine, mine, self.x[0], self.p.over_x, "x")

    def start_z(self, k):
        mine = self.here(self.g.span_rows(self.p.a, self.p.b, self.p), 0)
        self.w.start(mine, mine, self.z[k], self.p.over_z(k), "z")

    def over_x(self, k):
        if k == 0:
            return
        p, g = self.p, self.g
        rows = g.span_rows(p.a, p.b, p)
        self.w.arrived(self.here(rows, k), self.z[k], p.over_z(k))
        self.w.start(self.here(rows, k), self.here(rows, k), self.x[k], p.over_x, "x")
        mine = self.here(g.own_rows(p.a, p.b, p, p.y), k)
        self.w.start(mine, mine, self.y[0][k], p.over_y, "y")

    def over_y(self, k):
        p, g = self.p, self.g
        self.w.arrived(self.here(g.span_rows(1 - p.a, p.b, p), k), self.x[k], p.over_x)
        mine = self.here(g.own_rows(1 - p.a, p.b, p, p.y), k)
        self.w.start(mine, mine, self.y[1][k], p.over_y, "y")

    def sides(self, k):
        return [(0, self.p.a), (1, 1 - self.p.a)] if k else [(1, 1 - self.p.a)]

    def over_core(self, k):
        p, g = self.p, self.g
        for side, a in self.sides(k):
            self.w.arrived(self.here(g.own_rows(a, p.b, p, 1 - p.y), k), self.y[side][k], p.over_y)
            mine = self.here(g.half_rows(a, p.b, p.c), k)
            self.w.start(mine, mine, self.c[side][k], p.core)

    def finish(self, k):
        p, g = self.p, self.g
        for side, a in self.sides(k):
            self.w.arrived(self.here(g.half_rows(a, p.b, 1 - p.c), k), self.c[side][k], p.core)

class Scatter:
    def __init__(self, wires, p, grad, grid, spaces, large):
        self.w, self.p, self.grad, self.g = wires, p, grad, grid
        self.links = ("y", "x", "z") if large else (None,) * 3
        self.rc, self.ry, self.rx, self.rz, self.mine, self.peer = spaces
        self.order = [*range(1, p.bands), 0]
        self.c = [[wires.new() for _ in range(p.bands)] for _ in range(2)]
        self.y = [[wires.new() for _ in range(p.bands)] for _ in range(2)]
        self.x = [wires.new() for _ in range(p.bands)]
        self.z = [wires.new() for _ in range(p.bands)]
        self.last, self.share = wires.new(), wires.new()

    @staticmethod
    def spaces(bands, grid):
        half, own, span, width = grid.half, grid.own, grid.span, grid.width
        return [
            (2, bands, half, width),
            (2, bands, own, width),
            (bands, span, width),
            (bands, span, width),
            (span, width),
            (span, width),
        ]

    def here(self, rows, k):
        return self.grad.at[rows, self.g.cols(self.p.band(k))]

    def add(self, rows, k, part):
        spot = self.here(rows, k)
        spot[...] = (spot[...].astype(F32) + part.astype(F32)).astype(BF16)

    def start_c(self, ks=None):
        p, g = self.p, self.g
        for k in self.order if ks is None else ks:
            for a in range(2):
                rows = g.half_rows(a, p.band(k), 1 - p.c)
                self.w.start(self.here(rows, k), self.rc.at[a, k], self.c[a][k], p.core)

    def start_y(self, ks=None):
        p, g = self.p, self.g
        for k in self.order if ks is None else ks:
            for a in range(2):
                self.w.arrived(self.rc.at[a, k], self.c[a][k], p.core)
                self.add(g.half_rows(a, p.band(k), p.c), k, self.rc[a, k])
                rows = g.own_rows(a, p.band(k), p, 1 - p.y)
                self.w.start(self.here(rows, k), self.ry.at[a, k], self.y[a][k], p.over_y, self.links[0])

    def start_x(self, ks=None):
        p, g = self.p, self.g
        for k in self.order if ks is None else ks:
            for a in range(2):
                self.w.arrived(self.ry.at[a, k], self.y[a][k], p.over_y)
                self.add(g.own_rows(a, p.band(k), p, p.y), k, self.ry[a, k])
            rows = g.span_rows(1 - p.a, p.band(k), p)
            self.w.start(self.here(rows, k), self.rx.at[k], self.x[k], p.over_x, self.links[1])

    def start_z(self, ks=None):
        p, g = self.p, self.g
        for k in self.order if ks is None else ks:
            rows = g.span_rows(p.a, p.band(k), p)
            self.w.arrived(self.rx.at[k], self.x[k], p.over_x)
            self.add(rows, k, self.rx[k])
            if k:
                self.w.start(self.here(rows, k), self.rz.at[k], self.z[k], p.over_z(k), self.links[2])

    def start_last(self):
        p, g = self.p, self.g
        total = self.here(g.span_rows(p.a, p.b, p), 0)[...].astype(F32)
        for k in range(1, p.bands):
            self.w.arrived(self.rz.at[k], self.z[k], p.over_z(k))
            total = total + self.rz[k].astype(F32)
        self.mine[...] = total.astype(BF16)
        self.w.start(self.mine, self.peer, self.last, p.over_y, self.links[0])

    def result(self, out, first):
        p, g = self.p, self.g
        self.w.arrived(self.peer, self.last, p.over_y)
        both = g.span - g.own
        middle = self.mine[at(g.own * (1 - p.y), both), :].astype(F32) + self.peer[at(g.own * p.y, both), :].astype(F32)
        out[at(first + g.own, both), :] = middle.astype(out.dtype)
        far = (g.half - g.own) * p.y
        out[at(first + far, g.own), :] = self.mine[at(both * p.y, g.own), :].astype(out.dtype)
        far = (g.half - g.own) * (1 - p.y)
        out[at(first + far, g.own), :] = self.peer[at(both * (1 - p.y), g.own), :].astype(out.dtype)

    def start_share(self, out):
        p, g = self.p, self.g
        self.result(out, g.half * p.c)
        mine = out.at[at(g.half * p.c, g.half), :]
        self.w.start(mine, mine, self.share, p.core)

    def finish(self, out):
        p, g = self.p, self.g
        self.w.arrived(out.at[at(g.half * (1 - p.c), g.half), :], self.share, p.core)


class Exchange:
    def __init__(self, wires, p, value, spaces):
        self.w, self.p, self.value, self.spaces = wires, p, value, spaces
        self.sems = [wires.new() for _ in range(3)]

    def start(self, step, where, src=None):
        self.w.start(self.value if src is None else src, self.spaces[step], self.sems[step], where)
        self.sent = self.w.started.pop()

    def add(self, step, where, spot=None):
        self.w.arrived(self.spaces[step], self.sems[step], where)
        self.sent.wait_send()
        spot = self.value if spot is None else spot
        total = spot[...].astype(F32) + self.spaces[step][...].astype(F32)
        spot[...] = total.astype(spot.dtype)


class Chain:
    def __init__(self, R, wires, landing, place, count, step):
        self.R, self.w, self.landing, self.step, self.place = R, wires, landing, step, place
        self.has_from = place > 0 if step > 0 else place < count - 1
        self.has_to = place < count - 1 if step > 0 else place > 0
        self.sems = [wires.new() for _ in range(BANDS)]

    def copy(self, k, band):
        cols = band_cols(self.R, band)
        where = {"seq": self.place + self.step}
        return cols, self.w.copy(self.R.outgoing.at[:, cols], self.landing.at[:, cols], self.sems[k], where)

    def run(self, k, band):
        R = self.R
        cols, copy = self.copy(k, band)

        @pl.when(self.has_from)
        def _():
            copy.wait_recv()

        @pl.when(self.has_to)
        def _():
            incoming = self.landing[:, cols].astype(F32)
            R.outgoing[:, cols] = (R.piece[:, cols] + R.piece_decay[:, cols] * incoming).astype(BF16)
            copy.start()

    def sent(self, bands):
        @pl.when(self.has_to)
        def _():
            for k, band in enumerate(bands):
                self.copy(k, band)[1].wait_send()


def alias(R, fused):
    half = R.states.shape[0] // 2
    R.sl, R.s_in = R.states.at[0:half, :], R.states.at[half : 2 * half, :]
    R.dl, R.u, R.dyl, R.dconv, R.dpre, R.dz, R.dy = R.sl, R.z, R.gated, R.slope, R.ci, R.dh, R.expx
    R.y = R.dpre.at[0 : R.x.shape[0], 0 : R.wx.shape[1]]
    R.layer_out = R.xn.at[HALO:, :]
    R.input_grad = R.u.at[:, 0 : R.x.shape[1]]
    if fused:
        R.gx = R.states.at[0 : R.wx.shape[0], :]


def own_params(R, p, taps, head_dim):
    cols, width = R.x_kernel.shape[1], R.x.shape[1]
    inner, state = R.wx.shape[1], R.bc_kernel.shape[2]
    row = lambda ref: ref[...].astype(F32).reshape(1, ref.shape[0])
    lane = lax.broadcasted_iota(jnp.int32, (1, cols), 1)
    skip = jnp.zeros((1, cols), F32)
    heads = R.d_skip.shape[0]
    for head in range(heads):
        hit = lax.shift_right_arithmetic(lane, head_dim.bit_length() - 1) == head
        skip = jnp.where(hit, row(R.d_skip)[:, head : head + 1], skip)
    pad = jnp.zeros((1, cols - heads), F32)
    block = [R.x_kernel[...].astype(F32), row(R.x_offset), row(R.gate_gain), skip, jnp.zeros((1, cols), F32)]
    block += [jnp.concatenate([row(ref), pad], axis=1) for ref in (R.dt_bias, R.a_log)]
    R.par[:, lanes(cols * p.b, cols)] = jnp.concatenate([*block, jnp.zeros((6, cols), F32)], axis=0)
    kernel, offset = R.bc_kernel[...].astype(F32), R.bc_offset[...].astype(F32)
    for half in range(2):
        rows = [kernel[:, half, :], offset[half : half + 1, :], jnp.zeros((16 - taps - 1, state), F32)]
        R.par[:, pl.ds(inner + half * state, state)] = jnp.concatenate(rows, axis=0)
    rows, slot = R.w_bc.shape[0], R.w_dt.shape[0]
    block = 64

    @pl.loop(0, rows // block)
    def _(i):
        here = at(rows * p.a + i * block, block)
        w_zx = R.w_zx[pl.ds(i * block, block)].astype(F32)
        for half, whole in enumerate((R.wz, R.wx)):
            whole[here, lanes(cols * p.b, cols)] = w_zx[:, half, :].astype(BF16)
        w_bc = R.w_bc[pl.ds(i * block, block)].astype(F32)
        for half in range(2):
            R.wbc[here, pl.ds(half * state, state)] = w_bc[:, half, :].astype(BF16)

    w_dt = jnp.concatenate([R.w_dt[...].astype(F32), jnp.zeros((SLOTS - slot, rows), F32)], axis=0)
    R.wdt[at(SLOTS * p.b, SLOTS), lanes(rows * p.a, rows)] = w_dt.astype(BF16)
    R.wdt[BANDS * SLOTS :, :] = jnp.zeros((LANES - BANDS * SLOTS, width), BF16)


class Steps:
    def __init__(self, ops):
        self.ops = ops

    def __getattr__(self, name):
        def run(*which):
            step = self.ops.pop(" ".join(map(str, (name, *which))), None)
            if step is not None:
                step()

        return run


def layer(names, fused, head_dim, taps, *refs):
    R = types.SimpleNamespace(**dict(zip(names, refs)))
    alias(R, fused)
    inner = R.wx.shape[1]
    width = R.wx.shape[0]
    count = lax.axis_size("seq")
    place = lax.axis_index("seq")
    per_band = inner // head_dim // BANDS
    length = R.x.shape[0]
    first, last = place == 0, place == count - 1
    early = place < count // 2
    wires = Wires(R)
    ops = {}

    def op(name):
        return lambda run: ops.__setitem__(name, run)

    if fused:
        p = Place()
        greeted = p.greet()
        order = [p.band(-k) for k in range(BANDS)]
        back = [(k, p.band(k)) for k in (*range(1, BANDS), 0)]
        rows, cols = R.w_out.shape
        own_out = R.wo.at[at(rows * p.a, rows), lanes(cols * p.b, cols)]
        loads = [(R.x_in, R.x), (R.g_in, R.g), (R.w_out, own_out)]
    else:
        loads = [(R.x_in, R.x), (R.g_in, R.g)]
        order = list(range(BANDS))
        back = [(k, k) for k in range(BANDS)]
        barrier = pltpu.get_barrier_semaphore()

        @pl.when(jnp.logical_not(last))
        def _():
            pl.semaphore_signal(barrier, 1, device_id={"seq": place + 1}, device_id_type=pl.DeviceIdType.MESH)

        @pl.when(jnp.logical_not(first))
        def _():
            pl.semaphore_signal(barrier, 1, device_id={"seq": place - 1}, device_id_type=pl.DeviceIdType.MESH)

        greeted = lambda: pl.semaphore_wait(barrier, jnp.where(first | last, 1, 2))

    @pl.when(first)
    def _():
        R.x_halo[...] = jnp.zeros_like(R.x_halo)
        R.from_before[...] = jnp.zeros_like(R.from_before)

    @pl.when(last)
    def _():
        R.from_after[...] = jnp.zeros_like(R.from_after)
        R.dpre_halo[...] = jnp.zeros_like(R.dpre_halo)

    loads = [pltpu.make_async_copy(*pair, R.local_sem.at[i]) for i, pair in enumerate(loads)]
    for load in loads:
        load.start()
    if fused:
        own_params(R, p, taps, head_dim)
    R.gain[...] = R.norm_gain[...].astype(F32).reshape(1, width)
    for load in loads:
        load.wait()
    norm_rows(R)
    greeted()

    x_copy = wires.copy(R.x.at[pl.ds(length - HALO, HALO), :], R.x_halo, wires.new(), {"seq": place + 1})
    band_width = inner // BANDS
    groups = [[band for _, band in back[: BANDS // 2]], [band for _, band in back[BANDS // 2 :]]]
    pre_parts = [[(band_width * band, band_width) for band in bands] for bands in groups]
    pre_parts[1].append((inner, R.wbc.shape[1]))
    pre_copies = [
        [
            wires.copy(R.dpre_out.at[:, lanes(*part)], R.dpre_halo.at[:, lanes(*part)], wires.new(), {"seq": place - 1})
            for part in parts
        ]
        for parts in pre_parts
    ]
    forward = Chain(R, wires, R.from_before, place, count, 1)
    backward = Chain(R, wires, R.from_after, place, count, -1)
    layer_copy = pltpu.make_async_copy(R.layer_out, R.layer_to, R.local_sem.at[3])
    input_copy = pltpu.make_async_copy(R.input_grad, R.input_to, R.local_sem.at[4])

    @pl.when(jnp.logical_not(last))
    def _():
        x_copy.start()

    if fused:
        half = rows // 2
        grid = Grid(lambda a, band: rows * a, lambda band: cols * band, half, rows // 6, cols)
        gathers = {
            name: Gather(wires, p, whole, grid) for name, whole in (("x", R.wx), ("z", R.wz), ("o", R.wo))
        }
        dt_here = lambda k: R.wdt.at[at(SLOTS * p.band(-k), SLOTS), lanes(rows * p.a, rows)]
        par_here = lambda k: R.par.at[:, grid.cols(p.band(-k))]
        bc_half = lambda a, c: R.wbc.at[at(rows * a + half * c, half), :]
        dt_col = lambda a: R.wdt.at[pl.ds(0, BANDS * SLOTS), lanes(rows * a, rows)]
        dt_z, par_z = ([wires.new() for _ in range(p.bands)] for _ in range(2))
        dt_x, bc_x, bc_c = wires.new(), wires.new(), wires.new()
        for k in range(1, p.bands):
            wires.start(dt_here(0), dt_here(0), dt_z[k], p.over_z(k))
            wires.start(par_here(0), par_here(0), par_z[k], p.over_z(k))
        wires.start(bc_half(p.a, p.c), bc_half(p.a, p.c), bc_x, p.over_x)
        gathers["x"].start()

        for name, weight in gathers.items():
            if name != "x":
                op(f"GX0 {name} 0")(weight.start)
            for k in range(p.bands):
                if k:
                    op(f"GZ {name} {k}")(functools.partial(weight.start_z, k))
                    op(f"X {name} {k}")(functools.partial(weight.over_x, k))
                op(f"Y {name} {k}")(functools.partial(weight.over_y, k))
                op(f"C {name} {k}")(functools.partial(weight.over_core, k))

        @op("dt1")
        def _():
            for k in range(1, p.bands):
                wires.arrived(dt_here(k), dt_z[k], p.over_z(k))
            wires.start(dt_col(p.a), dt_col(p.a), dt_x, p.over_x)

        @op("bc1")
        def _():
            wires.arrived(bc_half(1 - p.a, p.c), bc_x, p.over_x)
            wires.start(bc_half(1 - p.a, p.c), bc_half(1 - p.a, p.c), bc_c, p.core)

        @op("small")
        def _():
            for k in range(1, p.bands):
                wires.arrived(par_here(k), par_z[k], p.over_z(k))

    def arrived(name, k):
        if fused:
            gathers[name].finish(k)


    op("spread")(lambda: head_spread(R, head_dim))

    @op("halo")
    def _():
        @pl.when(jnp.logical_not(first))
        def _():
            x_copy.wait_recv()

        norm_halo(R)

    @op("bc")
    def _():
        if fused:
            wires.arrived(bc_half(1 - p.a, 1 - p.c), bc_c, p.core)
        project_bc(R)
        convolve_bc(R, taps)

    @op("steps")
    def _():
        if fused:
            wires.arrived(dt_col(1 - p.a), dt_x, p.over_x)
        step_sizes(R, per_band)

    def inner_x(k, band):
        arrived("x", k)
        project(R, R.xn, R.wx, R.ci, band)
        convolve(R, taps, band)

    def inner_z(k, band):
        arrived("z", k)
        project(R, R.xn.at[HALO:, :], R.wz, R.z, band)

    def back_out(k, band):
        arrived("o", k)
        project(R, R.g, R.wo, R.dh, band)

    for k, band in enumerate(order):
        op(f"px {k}")(functools.partial(inner_x, k, band))
        op(f"inside {k}")(functools.partial(inside_forward, R, per_band, band))
        op(f"pz {k}")(functools.partial(inner_z, k, band))
        op(f"dh {k}")(functools.partial(back_out, k, band))

    def states_of(ks):
        local_states(R, [order[k] for k in ks])

        @pl.when(early)
        def _():
            for k in ks:
                forward.run(k, order[k])

    op("ls 0")(lambda: states_of(range(BANDS // 2)))
    op("ls 1")(lambda: states_of(range(BANDS // 2, BANDS)))

    @op("cf")
    def _():
        @pl.when(jnp.logical_not(early))
        def _():
            for k, band in enumerate(order):
                forward.run(k, band)

        carried_forward(R)
        forward.sent(order)

    op("gf")(lambda: gate_forward(R))

    @op("bo")
    def _():
        branch_out(R)
        layer_copy.start()


    scatters = {}

    def gradient(name, left, right, out):
        grad_of(left, right, out)
        if fused:
            scatters[name].start_c()

    op("go")(lambda: gradient("go", R.gT, R.hidden, R.go))
    op("gz")(lambda: gradient("gz", R.xnT, R.dz, R.gz))
    op("gb 0")(lambda: gate_backward(R, 0, 2))
    op("gb 1")(lambda: gate_backward(R, 1, 2))

    @op("adj")
    def _():
        backward_start(R)
        local_adjoints(R)

        @pl.when(jnp.logical_not(early))
        def _():
            for k, (_, band) in enumerate(back):
                backward.run(k, band)

    for k, (_, band) in enumerate(back):
        op(f"ib {k}")(functools.partial(inside_backward, R, per_band, band))

    @op("chain")
    def _():
        @pl.when(early)
        def _():
            for k, (_, band) in enumerate(back):
                backward.run(k, band)

    for which, name in enumerate(("cbA", "cbB")):
        for i in range(length // Q):
            op(f"{name} {i}")(functools.partial(carried_backward, R, i, groups[which]))

    def send_halo(which):
        for part, copy in zip(pre_parts[which], pre_copies[which]):
            R.dpre_out[:, lanes(*part)] = R.dpre[0:HALO, lanes(*part)].astype(BF16)

            @pl.when(jnp.logical_not(first))
            def _():
                copy.start()

    def back_through_conv(which):
        for part, copy in zip(pre_parts[which], pre_copies[which]):

            @pl.when(jnp.logical_not(last))
            def _():
                copy.wait_recv()

            conv_backward(R, taps, *part)

    def inner_gradient(which):
        for k, band in back[: BANDS // 2] if which == 0 else back[BANDS // 2 :]:
            project(R, R.xnT, R.dconv, R.gx, band)
            if fused:
                scatters["gx"].start_c([k])

    @op("sg")
    def _():
        backward.sent([band for _, band in back])
        step_grads(R)
        send_halo(1)

    op("hA")(lambda: send_halo(0))
    op("cvA")(lambda: back_through_conv(0))
    op("cv")(lambda: back_through_conv(1))
    op("gxA")(lambda: inner_gradient(0))
    op("gx")(lambda: inner_gradient(1))

    @op("gbd")
    def _():
        R.gbc[...] = dot(R.xnT[...], R.dconv[:, inner:]).astype(R.gbc.dtype)
        R.gdt[...] = dot_nt(R.d_raw[...].T, R.xnT[...])[0 : R.gdt.shape[0], :].astype(R.gdt.dtype)
        if fused:
            scatters["bc"].start_c()
            dts.start(0, p.core)

    op("i1")(lambda: input_first(R))
    op("i2")(lambda: input_second(R))

    @op("i3")
    def _():
        input_last(R)
        input_copy.start()

    @op("ss")
    def _():
        small_sums(R)
        if fused:
            vecs.start(0, p.core, vec_half(1 - p.c))

    if fused:
        grid = Grid(lambda a, band: rows * a, lambda band: cols * band, half, rows // 8, cols)
        bc_rows = rows // p.bands
        bc_grid = Grid(lambda a, band: rows * a + bc_rows * band, lambda band: 0, bc_rows // 2, 16, R.wbc.shape[1])
        for name, grad, where, space in (
            ("go", R.go, grid, "so"), ("gz", R.gz, grid, "sz"), ("gx", R.gx, grid, "sx"), ("bc", R.gbc, bc_grid, "sbc"),
        ):
            scatters[name] = Scatter(wires, p, grad, where, [getattr(R, f"{space}{i}") for i in range(6)], name != "bc")
        for name, out in (("go", R.oo), ("gz", R.oz), ("gx", R.ox)):
            scatter = scatters[name]
            for k in range(p.bands):
                op(f"sY {name} {k}")(functools.partial(scatter.start_y, [k]))
                op(f"sX {name} {k}")(functools.partial(scatter.start_x, [k]))
                op(f"sZ {name} {k}")(functools.partial(scatter.start_z, [k]))
            op(f"sL {name}")(scatter.start_last)
            op(f"sS {name}")(functools.partial(scatter.start_share, out))
            op(f"sE {name}")(functools.partial(scatter.finish, out))

        dts = Exchange(wires, p, R.gdt, [R.dt_c, R.dt_y, R.dt_x])
        vecs = Exchange(wires, p, R.vec, [R.vec_c, R.vec_y, R.vec_x])
        dtg_z, vec_z, bcg_z, bcg_c = ([wires.new() for _ in range(p.bands)] for _ in range(4))
        vec_lanes = lambda c: lanes(R.vec.shape[1] // 2 * c, R.vec.shape[1] // 2)
        vec_half = lambda c: R.vec.at[:, vec_lanes(c)]
        vec_s = wires.new()
        dt_cols = lambda a: R.gdt.at[:, lanes(rows * a, rows)]
        dt_rows = lambda band: R.gdt.at[at(SLOTS * band, SLOTS), lanes(rows * p.a, rows)]
        bc_out = lambda band, c: R.obc.at[at(bc_rows * band + bc_rows // 2 * c, bc_rows // 2), :]

        op("bY")(lambda: scatters["bc"].start_y())
        op("bX")(lambda: scatters["bc"].start_x())
        op("bZ")(lambda: scatters["bc"].start_z())
        op("bL")(lambda: scatters["bc"].start_last())

        @op("bG")
        def _():
            scatters["bc"].result(R.obc, bc_rows * p.b + bc_rows // 2 * p.c)
            for k in range(1, p.bands):
                wires.start(bc_out(p.b, p.c), bc_out(p.b, p.c), bcg_z[k], p.over_z(k))
            wires.start(bc_out(p.b, p.c), bc_out(p.b, p.c), bcg_c[0], p.core)

        @op("bS")
        def _():
            for k in range(1, p.bands):
                spot = bc_out(p.band(-k), p.c)
                wires.arrived(spot, bcg_z[k], p.over_z(k))
                wires.start(spot, spot, bcg_c[k], p.core)

        @op("bE")
        def _():
            for k in range(p.bands):
                wires.arrived(bc_out(p.band(-k), 1 - p.c), bcg_c[k], p.core)

        @op("dY")
        def _():
            dts.add(0, p.core)
            dts.start(1, p.over_y)

        @op("dX")
        def _():
            dts.add(1, p.over_y)
            dts.start(2, p.over_x, dt_cols(1 - p.a))

        @op("dZ")
        def _():
            dts.add(2, p.over_x, dt_cols(p.a))
            for k in range(1, p.bands):
                wires.start(dt_rows(p.band(k)), R.dt_zs.at[k], dtg_z[k], p.over_z(k))

        @op("dE")
        def _():
            total = dt_rows(p.b)[...].astype(F32)
            for k in range(1, p.bands):
                wires.arrived(R.dt_zs.at[k], dtg_z[k], p.over_z(k))
                total = total + R.dt_zs[k].astype(F32)
            R.odt[...] = total

        @op("vY")
        def _():
            vecs.add(0, p.core, vec_half(p.c))
            vecs.start(1, p.over_y, vec_half(p.c))

        @op("vX")
        def _():
            vecs.add(1, p.over_y, vec_half(p.c))
            vecs.start(2, p.over_x, vec_half(p.c))

        @op("vZ")
        def _():
            vecs.add(2, p.over_x, vec_half(p.c))
            R.vec_zs[p.b] = R.vec[:, vec_lanes(p.c)]
            for k in range(1, p.bands):
                wires.start(vec_half(p.c), R.vec_zs.at[p.b], vec_z[k], p.over_z(k))

        @op("vS")
        def _():
            for k in range(1, p.bands):
                wires.arrived(R.vec_zs.at[p.band(-k)], vec_z[k], p.over_z(k))
            total = R.vec_zs[0]
            for band in range(1, p.bands):
                total = total + R.vec_zs[band]
            mine = R.ovec.at[:, vec_lanes(p.c)]
            mine[...] = total
            wires.start(mine, mine, vec_s, p.core)

        @op("vE")
        def _():
            wires.arrived(R.ovec.at[:, vec_lanes(1 - p.c)], vec_s, p.core)
            R.oband[...] = R.ovec[:, grid.cols(p.b)]
            by_lane = [R.ovec[5:6, inner : inner + LANES], R.ovec[5:6, inner + LANES :], R.ovec[6:7, width : width + LANES]]
            by_lane = jnp.concatenate([*by_lane, jnp.zeros((5, LANES), F32)], axis=0)
            R.oheads[...] = pltpu.roll(by_lane, lax.rem(LANES - SLOTS * p.b, LANES), 1)

    do = Steps(ops)
    wx, wz, wo, go, gz, gx = "x", "z", "o", "go", "gz", "gx"
    do.spread(); do.GZ(wx, 1); do.dt1(); do.small(); do.GZ(wx, 2); do.X(wx, 1); do.halo(); do.GZ(wx, 3)
    do.bc1(); do.Y(wx, 0); do.X(wx, 2); do.bc(); do.Y(wx, 1); do.GZ(wz, 1); do.C(wx, 0); do.X(wx, 3)
    do.steps(); do.Y(wx, 2); do.GX0(wz, 0); do.GZ(wz, 2); do.px(0); do.C(wx, 1); do.Y(wx, 3); do.X(wz, 1)
    do.GZ(wz, 3); do.inside(0); do.C(wx, 2); do.px(1); do.Y(wz, 0); do.X(wz, 2); do.ls(0); do.C(wx, 3)
    do.Y(wz, 1); do.GZ(wo, 1); do.px(2); do.X(wz, 3); do.px(3); do.Y(wz, 2); do.GZ(wo, 2); do.C(wz, 0)
    do.GX0(wo, 0); do.ls(1); do.inside(2); do.X(wo, 1); do.C(wz, 1); do.pz(0); do.Y(wz, 3); do.GZ(wo, 3)
    do.inside(1); do.C(wz, 2); do.inside(3); do.Y(wo, 0); do.pz(1); do.X(wo, 2); do.pz(2); do.C(wz, 3)
    do.Y(wo, 1); do.cf(); do.X(wo, 3); do.pz(3); do.gf(); do.C(wo, 0); do.C(wo, 1); do.Y(wo, 2); do.go()
    do.Y(wo, 3); do.dh(0); do.C(wo, 2); do.dh(1); do.C(wo, 3); do.sY(go, 1); do.dh(2); do.sY(go, 0)
    do.sY(go, 2); do.sY(go, 3); do.dh(3); do.gb(0); do.gb(1); do.adj(); do.sX(go, 1); do.gz(); do.ib(3)
    do.sX(go, 2); do.ib(1); do.sX(go, 3); do.ib(0); do.bo(); do.sZ(go, 1); do.sY(gz, 2); do.ib(2)
    do.sX(go, 0); do.sY(gz, 3); do.chain(); do.cbA(3); do.cbA(2); do.cbA(1); do.cbA(0); do.hA(); do.sZ(go, 2)
    do.sZ(go, 3); do.sX(gz, 2); do.sY(gz, 0); do.sY(gz, 1); do.cbB(3); do.cbB(2); do.sX(gz, 3); do.cbB(1)
    do.cvA(); do.gxA(); do.cbB(0); do.sg(); do.sX(gz, 1); do.sZ(go, 0); do.sZ(gz, 2); do.sY(gx, 1); do.i1()
    do.sY(gx, 2); do.sX(gz, 0); do.sZ(gz, 3); do.sL(go); do.cv(); do.gbd(); do.gx(); do.sX(gx, 1)
    do.sZ(gz, 1); do.bY(); do.i2(); do.sY(gx, 3); do.sX(gx, 2); do.i3(); do.ss(); do.sZ(gx, 1); do.bX()
    do.sY(gx, 0); do.sZ(gz, 0); do.vY(); do.sX(gx, 3); do.sL(gz); do.sZ(gx, 2); do.dY(); do.sS(go); do.vX()
    do.bZ(); do.sX(gx, 0); do.sZ(gx, 3); do.bL(); do.dX(); do.vZ(); do.sZ(gx, 0); do.sS(gz); do.sL(gx)
    do.sE(go); do.bG(); do.vS(); do.dZ(); do.bS(); do.sS(gx); do.vE(); do.bE(); do.dE(); do.sE(gz); do.sE(gx)
    assert not ops, sorted(ops)

    layer_copy.wait()
    input_copy.wait()
    wires.drain()

    @pl.when(jnp.logical_not(last))
    def _():
        x_copy.wait_send()

    @pl.when(jnp.logical_not(first))
    def _():
        for copy in sum(pre_copies, []):
            copy.wait_send()


def hand_out(taps, names, *refs):
    count = len(names)
    came, refs = refs[:count], refs[count:]
    (
        layer_to, input_to, norm_gain, zx, bc, dt, x_kernel, x_offset, bc_kernel, bc_offset,
        dt_bias, a_log, d_skip, gate_gain, out_to,
    ) = refs[:15]
    here, (zx_via, out_via, bc_via, in_sem, out_sem) = refs[15 : 15 + count], refs[15 + count :]
    R = types.SimpleNamespace(**dict(zip(names, here)))
    loads = {name: pltpu.make_async_copy(a, b, in_sem.at[i]) for i, (name, a, b) in enumerate(zip(names, came, here))}
    stores = [
        pltpu.make_async_copy(*pair, out_sem.at[i])
        for i, pair in enumerate(((zx_via, zx), (out_via, out_to), (R.input_to, input_to), (R.layer_to, layer_to), (bc_via, bc)))
    ]
    first = ("oz", "ox", "oo", "input_to", "layer_to")
    for name in (*first, *(name for name in names if name not in first)):
        loads[name].start()
    loads["oz"].wait()
    zx_via[:, 0, :] = R.oz[...].astype(F32)
    loads["ox"].wait()
    zx_via[:, 1, :] = R.ox[...].astype(F32)
    stores[0].start()
    loads["oo"].wait()
    out_via[...] = R.oo[...].astype(F32)
    stores[1].start()
    for name, store in (("input_to", stores[2]), ("layer_to", stores[3])):
        loads[name].wait()
        store.start()
    for name in names:
        if name not in first:
            loads[name].wait()
    state = bc.shape[2]
    inner, width = R.ovec.shape[1] - 2 * state, R.layer_to.shape[1]
    for half in range(2):
        cols = pl.ds(half * state, state)
        bc_via[:, half, :] = R.obc[:, cols].astype(F32)
        cols = pl.ds(inner + half * state, state)
        bc_kernel[:, half, :] = R.ovec[0:taps, cols]
        bc_offset[half : half + 1, :] = R.ovec[4:5, cols]
    stores[4].start()
    dt[...] = R.odt[0 : dt.shape[0], :]
    norm_gain[...] = R.ovec[6, 0:width]
    x_kernel[...] = R.oband[0:taps, :]
    x_offset[...] = R.oband[4, :]
    gate_gain[...] = R.oband[5, :]
    for row, ref in enumerate((dt_bias, a_log, d_skip)):
        ref[...] = R.oheads[row, 0 : ref.shape[0]]
    for store in stores:
        store.wait()


def run_layer(fused, ins, head_dim, taps):
    length, width = ins["x_in"].shape
    inner, state2 = ins["inner"], ins["state2"]
    conv = inner + state2
    ins = {k: v for k, v in ins.items() if k not in ("inner", "state2")}
    per_band = inner // head_dim // BANDS
    chunks = length // Q
    weights = dict(
        wz=((width, inner), BF16),
        wx=((width, inner), BF16),
        wbc=((width, state2), BF16),
        wdt=((LANES, width), BF16),
        wo=((width, inner), BF16),
        par=((16, conv), F32),
    )
    grads = dict(
        gz=((width, inner), BF16),
        gx=((width, inner), BF16),
        go=((width, inner), BF16),
        gbc=((width, state2), BF16),
        gdt=((BANDS * SLOTS, width), BF16),
        vec=((8, conv), F32),
    )
    outs = dict(layer_to=((length, width), BF16), input_to=((length, width), F32))
    scratch = dict(
        x=((length, width), BF16),
        g=((length, width), BF16),
        gain=((1, width), F32),
        ex=((LANES, inner), BF16),
        pick=((per_band * Q, LANES), BF16),
        xn=((HALO + length, width), BF16),
        xnT=((width, length), BF16),
        gT=((width, length), BF16),
        inv_rms=((length, 1), F32),
        inv_gate=((length, 1), F32),
        x_halo=((HALO, width), BF16),
        ci=((HALO + length, conv), F32),
        cib=((length, conv), BF16),
        z=((length, inner), F32),
        xh=((length, inner), BF16),
        xt=((length, inner), BF16),
        bm=((length, LANES), BF16),
        cm=((length, LANES), BF16),
        prod=((length, Q), F32),
        prodT=((length, Q), F32),
        slope=((length, conv), BF16),
        rate=((1, LANES), F32),
        heads=((8, LANES), F32),
        dt=((length, LANES), F32),
        dt_sig=((length, LANES), F32),
        dt_low=((length, LANES), BF16),
        tail_low=((length, LANES), BF16),
        exp_low=((length, LANES), BF16),
        logs=((length, LANES), F32),
        logsT=((LANES, length), F32),
        ends=((8, LANES), F32),
        decx=((8, inner), F32),
        kept=((8, inner), F32),
        expx=((length, inner), BF16),
        states=((2 * chunks * LANES, inner), BF16),
        piece=((LANES, inner), F32),
        piece_decay=((1, inner), F32),
        outgoing=((LANES, inner), BF16),
        from_before=((LANES, inner), BF16),
        from_after=((LANES, inner), BF16),
        dh=((length, inner), BF16),
        gated=((length, inner), BF16),
        hidden=((length, inner), BF16),
        gain_acc=((8, inner), F32),
        skip_acc=((8, inner), F32),
        norm_acc=((8, width), F32),
        rate_acc=((8, LANES), F32),
        bias_acc=((8, LANES), F32),
        pulls=((length, LANES), F32),
        pullsT=((LANES, length), F32),
        d_prod=((length, Q), F32),
        d_log=((length, LANES), F32),
        d_tail=((length, LANES), F32),
        direct=((length, LANES), F32),
        db=((length, LANES), F32),
        dc=((length, LANES), F32),
        d_raw=((length, LANES), BF16),
        dpre_out=((HALO, conv), BF16),
        dpre_halo=((HALO, conv), BF16),
    )
    if fused:
        rows, cols = ins["w_out"].shape
        bands = inner // cols
        outs.update(
            oz=((rows, cols), BF16),
            ox=((rows, cols), BF16),
            oo=((rows, cols), BF16),
            obc=((rows, state2), BF16),
            odt=((SLOTS, rows), F32),
            ovec=((8, conv), F32),
            oband=((8, cols), F32),
            oheads=((8, LANES), F32),
        )
        scratch.update(weights)
        scratch.update({k: v for k, v in grads.items() if k != "gx"})
        main = Scatter.spaces(bands, Grid(None, None, rows // 2, rows // 8, cols))
        small = Scatter.spaces(bands, Grid(None, None, rows // bands // 2, 16, state2))
        for name, shapes in (("so", main), ("sz", main), ("sx", main), ("sbc", small)):
            scratch.update({f"{name}{i}": (shape, BF16) for i, shape in enumerate(shapes)})
        scratch.update(
            dt_c=((BANDS * SLOTS, width), BF16),
            dt_y=((BANDS * SLOTS, width), BF16),
            dt_x=((BANDS * SLOTS, rows), BF16),
            dt_zs=((bands, SLOTS, rows), BF16),
            vec_c=((8, conv // 2), F32),
            vec_y=((8, conv // 2), F32),
            vec_x=((8, conv // 2), F32),
            vec_zs=((bands, 8, conv // 2), F32),
        )
    else:
        outs.update(grads)
    names = (*ins, *outs, *scratch, "send_sem", "recv_sem", "local_sem")
    results = pl.pallas_call(
        functools.partial(layer, names, fused, head_dim, taps),
        out_shape=[jax.ShapeDtypeStruct(*v) for v in outs.values()],
        in_specs=[pl.BlockSpec(memory_space=pl.ANY if name in ("x_in", "g_in", "w_out") else pltpu.VMEM) for name in ins],
        out_specs=[pl.BlockSpec(memory_space=pl.ANY if name in ("layer_to", "input_to") else pltpu.VMEM) for name in outs],
        scratch_shapes=[pltpu.VMEM(*v) for v in scratch.values()]
        + [pltpu.SemaphoreType.DMA((SEMS,)), pltpu.SemaphoreType.DMA((SEMS,)), pltpu.SemaphoreType.DMA((8,))],
        compiler_params=pltpu.CompilerParams(
            collective_id=0, has_side_effects=True, vmem_limit_bytes=VMEM_BYTES
        ),
    )(*ins.values())
    return dict(zip(outs, results))


VMEM_BYTES = 64 * 2**20 - 2**18


def body(residual, cotangent, norm_gain, w_zx, w_bc, w_dt, x_kernel, x_offset, bc_kernel, bc_offset, dt_bias, a_log, d_skip, gate_gain, w_out):
    _, length, width = residual.shape
    bands = lax.axis_size("wb")
    rows_own, heads_own, inner_own, state = w_zx.shape[0], w_dt.shape[1], w_zx.shape[2], w_bc.shape[2]
    heads, inner = heads_own * bands, inner_own * bands
    head_dim = inner_own // heads_own
    taps = x_kernel.shape[0]
    fused = (lax.axis_size("seq"), lax.axis_size("wa"), bands) == (4, 2, BANDS) and inner_own % LANES == 0
    per = heads // BANDS
    ins = dict(
        x_in=residual.reshape(length, width),
        g_in=cotangent.reshape(length, width),
        norm_gain=norm_gain,
        inner=inner,
        state2=2 * state,
    )

    if fused:
        ins.update(
            w_zx=w_zx, w_out=w_out, w_bc=w_bc, w_dt=w_dt.T, x_kernel=x_kernel, x_offset=x_offset,
            bc_kernel=bc_kernel, bc_offset=bc_offset, dt_bias=dt_bias, a_log=a_log, d_skip=d_skip, gate_gain=gate_gain,
        )
        out = run_layer(True, ins, head_dim, taps)
        any_space, vmem = pl.BlockSpec(memory_space=pl.ANY), pl.BlockSpec(memory_space=pltpu.VMEM)
        shapes = [
            ((length, width), BF16), ((length, width), F32), ((width,), F32), (w_zx.shape, F32), (w_bc.shape, F32),
            (w_dt.shape[::-1], F32), (x_kernel.shape, F32), (x_offset.shape, F32), (bc_kernel.shape, F32),
            (bc_offset.shape, F32), (dt_bias.shape, F32), (a_log.shape, F32), (d_skip.shape, F32), (gate_gain.shape, F32),
            (w_out.shape, F32),
        ]
        results = pl.pallas_call(
            functools.partial(hand_out, taps, tuple(out)),
            out_shape=[jax.ShapeDtypeStruct(*shape) for shape in shapes],
            in_specs=[any_space] * len(out),
            out_specs=[any_space if i in (0, 1, 3, 4, 14) else vmem for i in range(15)],
            scratch_shapes=[pltpu.VMEM(value.shape, value.dtype) for value in out.values()]
            + [pltpu.VMEM(shape, F32) for shape in (w_zx.shape, w_out.shape, w_bc.shape)]
            + [pltpu.SemaphoreType.DMA((len(out),)), pltpu.SemaphoreType.DMA((5,))],
            compiler_params=pltpu.CompilerParams(vmem_limit_bytes=VMEM_BYTES),
        )(*out.values())
        results = list(results)
        results[0] = results[0].reshape(residual.shape)
        results[1] = results[1].reshape(residual.shape)
        results[5] = results[5].T
        return tuple(results)

    own = jnp.concatenate(
        [x_kernel.astype(F32), x_offset.astype(F32)[None], gate_gain.astype(F32)[None], jnp.repeat(d_skip, head_dim)[None]]
    )
    par_bc = jnp.concatenate([bc_kernel.reshape(taps, 2 * state), bc_offset.reshape(1, 2 * state)], axis=0).astype(F32)
    par_bc = jnp.pad(par_bc, ((0, 16 - taps - 1), (0, 0)))
    wzx = lax.all_gather(lax.all_gather(w_zx, "wa", axis=0, tiled=True), "wb", axis=2, tiled=True)
    wdt = lax.all_gather(lax.all_gather(w_dt, "wa", axis=0, tiled=True), "wb", axis=1, tiled=True)
    wdt = jnp.pad(wdt.T.reshape(BANDS, per, width), ((0, 0), (0, SLOTS - per), (0, 0))).reshape(-1, width)
    small = lax.all_gather(jnp.stack([dt_bias, a_log]), "wb", axis=1, tiled=True).reshape(2, BANDS, per)
    small = jnp.pad(small, ((0, 6), (0, 0), (0, inner // BANDS - per))).reshape(8, inner)
    wide = jnp.pad(lax.all_gather(own, "wb", axis=1, tiled=True), ((0, 1), (0, 0)))
    ins.update(
        wz=wzx[:, 0],
        wx=wzx[:, 1],
        wo=lax.all_gather(lax.all_gather(w_out, "wa", axis=0, tiled=True), "wb", axis=1, tiled=True),
        wbc=lax.all_gather(w_bc, "wa", axis=0, tiled=True).reshape(width, 2 * state),
        wdt=jnp.pad(wdt, ((0, LANES - BANDS * SLOTS), (0, 0))),
        par=jnp.concatenate([jnp.concatenate([wide, small], axis=0), par_bc], axis=1),
    )
    out = run_layer(False, ins, head_dim, taps)

    def share(grad, columns=True):
        grad = lax.psum_scatter(grad.astype(F32), "wa", scatter_dimension=0, tiled=True)
        if columns:
            grad = lax.psum_scatter(grad, "wb", scatter_dimension=grad.ndim - 1, tiled=True)
        else:
            grad = lax.psum(grad, "wb")
        return lax.psum(grad, "seq")

    gdt = out["gdt"].reshape(BANDS, SLOTS, width)[:, :per].reshape(heads, width)
    vec = lax.psum(out["vec"], ("seq", "wa", "wb"))
    mine = lax.axis_index("wb")
    band = lax.dynamic_slice_in_dim(vec[:, :inner], mine * inner_own, inner_own, 1)
    by_head = jnp.stack([vec[5, inner : inner + LANES], vec[5, inner + LANES :], vec[6, width : width + LANES]])
    by_head = by_head[:, : BANDS * SLOTS].reshape(3, BANDS, SLOTS)[:, :, :per].reshape(3, heads)
    by_head = lax.dynamic_slice_in_dim(by_head, mine * heads_own, heads_own, 1)
    return (
        out["layer_to"].reshape(residual.shape),
        out["input_to"].reshape(residual.shape),
        vec[6, :width],
        share(jnp.stack([out["gz"], out["gx"]], axis=1)),
        share(out["gbc"], False).reshape(-1, 2, state),
        share(gdt.T),
        band[0:taps],
        band[4],
        vec[0:taps, inner:].reshape(taps, 2, state),
        vec[4, inner:].reshape(2, state),
        by_head[0],
        by_head[1],
        by_head[2],
        band[5],
        share(out["go"]),
    )


def solution(mesh):
    batch = P(("wa", "wb"), "seq", None)
    ins = (
        batch, batch, P(), P("wa", None, "wb"), P("wa", None, None), P("wa", "wb"), P(None, "wb"), P("wb"), P(), P(),
        P("wb"), P("wb"), P("wb"), P("wb"), P("wa", "wb"),
    )
    outs = (
        batch, batch, P(), P("wa", None, "wb"), P("wa", None, None), P("wa", "wb"), P(None, "wb"), P("wb"), P(), P(),
        P("wb"), P("wb"), P("wb"), P("wb"), P("wa", "wb"),
    )
    return jax.shard_map(body, mesh=mesh, in_specs=ins, out_specs=outs, check_vma=False)
```
